128 devices in a mesh: band: 4 (over z_hi, core), fft: 32 (over z_lo, x, y).
Axes of the slice: x: 4, y: 4, z: 4 (z_hi: 2, z_lo: 2; z = z_hi * 2 + z_lo), core: 2. Of those that a mesh axis runs over, the one named last changes fastest.
Arguments:
- basis: bfloat16 [512, 512, 128], P('band', 'fft'), may hold values from -6 to 6
- potential: float32 [192, 192, 192], P('fft'), may hold values from -24 to 24
- colmap: int32 [512], replicated, may hold values from 0 to 36863, as said below
- hsub_old: float32 [512, 504], P('band'), may hold values from -6 to 6
- inv_factor: float32 [512, 512], replicated, may hold values from -1 to 1.5, as said below
- angles: float32 [30, 8, 32], replicated, may hold values from -3.140625 to 3.140625
Outputs:
- hblock: bfloat16 [8, 512, 128], P('band', 'fft')
- rotated: float32 [512, 512], P(('band', 'fft'))
- bands_new: bfloat16 [8, 512, 128], P('band', 'fft')
The draws below stay inside these ranges and needn't reach their ends.
Inputs may be any that keep to these rules, and one draw needn't show every extreme that they name: `colmap`: distinct plane positions ix * 192 + iy, one for each pencil column. `inv_factor`: zero above the diagonal, positive on it.
All inputs are finite; a program needn't handle non-finite values.
Results may differ from the reference program's by a relative error of at most 0.015.
Values may be sent and summed in bfloat16 or wider, within the bound.
A program may use at most 448 MiB of HBM per device.

```python
import math
import jax
import jax.numpy as jnp
from jax import lax

NG = 192
NZC = 64
ORDER = 512
NEWB = 2
NCOL = 512
NEW = 8
GROUP = 128
OLD = 504
TILE = 32
ROUNDS = 30
N_BAND = 4


def draw_colmap(key, part):
    key = jax.random.fold_in(key, 7)
    plane_ids = jnp.arange(NG * NG, dtype=jnp.int32)
    row_ids = plane_ids // NG
    col_ids = plane_ids % NG
    freq_x = jnp.where(row_ids < NG // 2, row_ids, row_ids - NG)
    freq_y = jnp.where(col_ids < NG // 2, col_ids, col_ids - NG)
    radius = freq_x * freq_x + freq_y * freq_y
    rank_ids = jax.random.permutation(key, NG * NG).astype(jnp.int32)
    score_ids = radius * (NG * NG) + rank_ids
    nearest = jnp.argsort(score_ids, stable=True)[:NCOL]
    shuffle = jax.random.permutation(jax.random.fold_in(key, 1), NCOL)
    return plane_ids[nearest][shuffle].astype(jnp.int32)


def draw_inv_factor(key, part):
    key = jax.random.fold_in(key, 11)
    off_key, diag_key = jax.random.split(key)
    row_ids = jnp.arange(ORDER)[:, None]
    col_ids = jnp.arange(ORDER)[None, :]
    off_diag = jax.random.normal(off_key, (ORDER, ORDER), jnp.float32) * (0.7 / math.sqrt(ORDER))
    diag_vals = jax.random.uniform(diag_key, (ORDER,), jnp.float32, 0.7, 1.3)
    lower_part = jnp.where(row_ids > col_ids, off_diag, 0.0)
    return (lower_part + jnp.diag(diag_vals)).astype(jnp.float32)


def block_levels(own_key, shape, cuts, low, largest):
    def one(dim, parts):
        heights = jax.random.uniform(jax.random.fold_in(jax.random.fold_in(own_key, 6), dim), (parts,), jnp.float32, low / len(cuts), largest / len(cuts))
        return jnp.repeat(jnp.exp(heights), shape[dim] // parts).reshape((-1,) + (1,) * (len(shape) - dim - 1))

    factor_of = one(*cuts[0])
    for cut in cuts[1:]:
        factor_of = factor_of * one(*cut)
    return factor_of


def gaussian(stream_key, dims, spread, bound, cuts=(), kind=jnp.bfloat16):
    array = spread * jax.random.normal(stream_key, dims, jnp.float32)
    if cuts:
        array = array * block_levels(stream_key, dims, cuts, -0.22, 0.18)
    return jnp.clip(array, -bound, bound).astype(kind)


def setup_inputs(seed: int = 0) -> dict:
    seeds = jax.random.split(jax.random.key(seed), 7)
    return {
        "basis": gaussian(seeds[0], (ORDER, NCOL, 2 * NZC), 1.0, 6.0, ((0, 4), (1, 32))),
        "potential": gaussian(seeds[1], (NG, NG, NG), 4.0, 24.0, ((0, 32),), jnp.float32),
        "colmap": draw_colmap(jax.random.fold_in(seeds[6], 71), 0),
        "hsub_old": gaussian(seeds[3], (ORDER, OLD), 1.0, 6.0, ((0, 4),), jnp.float32),
        "inv_factor": draw_inv_factor(jax.random.fold_in(seeds[6], 71), 0),
        "angles": jnp.clip(jax.random.uniform(seeds[5], (ROUNDS, 8, TILE), jnp.float32, -3.140625, 3.140625), -3.140625, 3.140625),
    }


HIGHEST_PRECISION = lax.Precision.HIGHEST

def signed_index(position, extent):
    return jnp.where(position < extent // 2, position, position - extent)

def slot_frequency(extent):
    slot_ids = jnp.arange(extent, dtype=jnp.int32)
    return jnp.where(slot_ids < extent // 2, slot_ids, slot_ids - extent)

def kinetic_table(columns, grid_size, slot_count):
    freq_x = signed_index(columns // grid_size, grid_size)
    freq_y = signed_index(columns % grid_size, grid_size)
    freq_z = slot_frequency(slot_count)
    radius = (freq_x * freq_x + freq_y * freq_y)[:, None] + (freq_z * freq_z)[None, :]
    return radius.astype(jnp.float32) / (2.0 * (grid_size // 4) ** 2)

def rotation_round(rot_table, angle_set, round_index, tile_size):
    pair_turn = round_index % 15
    in_shift = round_index % tile_size
    seat_list = jnp.arange(16, dtype=jnp.int32)
    seat_list = jnp.where(seat_list == 0, 0, 1 + (seat_list - 1 + pair_turn) % 15)
    first_tiles = seat_list[:8]
    second_tiles = seat_list[8:][::-1]
    cos_table = jnp.cos(angle_set)
    sine_table = jnp.sin(angle_set)
    left_cols = jnp.take(rot_table, first_tiles, axis=1)
    right_cols = jnp.roll(jnp.take(rot_table, second_tiles, axis=1), -in_shift, axis=2)
    new_left = cos_table * left_cols - sine_table * right_cols
    new_right = jnp.roll(sine_table * left_cols + cos_table * right_cols, in_shift, axis=2)
    return rot_table.at[:, first_tiles].set(new_left).at[:, second_tiles].set(new_right)

def rotate_rows(start_rows, angles, tile_size):
    row_count = start_rows.shape[0]
    rot_table = start_rows.reshape(row_count, 16, tile_size)

    def step_round(round_index, current):
        angle_set = lax.dynamic_index_in_dim(angles, round_index, 0, keepdims=False)
        return rotation_round(current, angle_set, round_index, tile_size)
    rot_table = lax.fori_loop(0, angles.shape[0], step_round, rot_table)
    return rot_table.reshape(row_count, 16 * tile_size)

def reference(basis, potential, colmap, hsub_old, inv_factor, angles):
    tile_size = ORDER // 16
    grouped = basis.reshape(N_BAND, GROUP, NCOL, 2 * NZC)
    new_block = grouped[:, GROUP - NEWB:].reshape(NEW, NCOL, 2 * NZC)
    kinetic = kinetic_table(colmap, NG, NZC)
    kinetic = jnp.concatenate([kinetic, kinetic], axis=1)
    pos_x = colmap // NG
    pos_y = colmap % NG
    slot_z = slot_frequency(NZC) % NG

    def apply_one(vector):
        coeffs = vector.astype(jnp.float32)
        values = lax.complex(coeffs[:, :NZC], coeffs[:, NZC:])
        cube_data = jnp.zeros((NG, NG, NG), values.dtype).at[slot_z[None, :], pos_x[:, None], pos_y[:, None]].set(values)
        field_data = jnp.fft.ifftn(cube_data) * NG ** 3
        product = jnp.fft.fftn(potential * field_data) / NG ** 3
        picked = product[slot_z[None, :], pos_x[:, None], pos_y[:, None]]
        local_term = jnp.concatenate([jnp.real(picked), jnp.imag(picked)], axis=1)
        return (kinetic * coeffs + local_term).astype(jnp.bfloat16)
    hblock = lax.map(apply_one, new_block)
    flat_basis = basis.reshape(ORDER, NCOL * 2 * NZC)
    inner_scale = 1.0 / math.sqrt(2 * NCOL * NZC)
    new_columns = inner_scale * jnp.dot(flat_basis, hblock.reshape(NEW, NCOL * 2 * NZC).T, preferred_element_type=jnp.float32)
    sub_matrix = jnp.concatenate([hsub_old.reshape(ORDER, N_BAND, GROUP - NEWB), new_columns.reshape(ORDER, N_BAND, NEWB)], axis=2).reshape(ORDER, ORDER)
    rotation = rotate_rows(jnp.eye(ORDER, dtype=jnp.float32), angles, tile_size)
    coupled = jnp.dot(inv_factor.T, rotation, precision=HIGHEST_PRECISION, preferred_element_type=jnp.float32)
    image = jnp.dot(sub_matrix, coupled, precision=HIGHEST_PRECISION, preferred_element_type=jnp.float32)
    rotated = jnp.dot(coupled.T, image, precision=HIGHEST_PRECISION, preferred_element_type=jnp.float32)
    weights = coupled[:, :NEW].astype(jnp.bfloat16)
    bands_new = jnp.dot(weights.T, flat_basis, preferred_element_type=jnp.float32).astype(jnp.bfloat16)
    return (hblock, rotated, bands_new.reshape(NEW, NCOL, 2 * NZC))
```

```python
import functools
import math

import jax
import jax.numpy as jnp
import numpy as np
from jax import lax
from jax.experimental import pallas as pl
from jax.experimental.pallas import tpu as pltpu
from jax.sharding import PartitionSpec as P

NG = 192
NZC = 64
ORDER = 512
GROUP = 128
NCOL = 512
NBAND = 4
NFFT = 32
SLAB = 6
ROUNDS = 30
TILE = 32
F32 = jnp.float32
BF16 = jnp.bfloat16
HIGH = lax.Precision.HIGHEST
MESH = pl.DeviceIdType.MESH
NT = (((1,), (1,)), ((), ()))


def dot(a, b, precision=None):
    return jnp.dot(a, b, precision=precision, preferred_element_type=F32)


def dot_nt(a, b, precision=None):
    return lax.dot_general(a, b, NT, precision=precision, preferred_element_type=F32)


def z_table():
    slot = np.arange(NZC)
    freq = np.where(slot < NZC // 2, slot, slot - NZC) % NG
    table = np.zeros((NFFT, 8, 4, NZC), np.float64)
    z = np.arange(NG).reshape(NFFT, SLAB)
    angle = 2.0 * np.pi * ((z[:, :, None] * freq) % NG) / NG
    table[:, :SLAB, 0] = np.cos(angle)
    table[:, :SLAB, 1] = -np.sin(angle)
    table[:, :SLAB, 2] = np.sin(angle)
    table[:, :SLAB, 3] = np.cos(angle)
    return table.reshape(NFFT * 8, 4 * NZC)


def plane_angles():
    ids = np.arange(NG)
    return 2.0 * np.pi * ((ids[:, None] * ids[None, :]) % NG) / NG


def x_table():
    angle = plane_angles()
    both = np.concatenate([np.cos(angle), np.sin(angle)], 0)
    high = np.asarray(both, np.float32).astype(BF16)
    low = (both - high.astype(np.float64)).astype(BF16)
    table = np.zeros((2 * NG, 512), BF16)
    table[:, :NG] = high
    table[:, 256 : 256 + NG] = low
    return table


def y_table_left():
    angle = plane_angles()
    table = np.zeros((2, 256, 2, 256), np.float64)
    table[0, :NG, 0, :NG] = np.cos(angle)
    table[0, :NG, 1, :NG] = -np.sin(angle)
    table[1, :NG, 0, :NG] = np.sin(angle)
    table[1, :NG, 1, :NG] = np.cos(angle)
    return table.reshape(512, 512)


def seats(turn):
    return [0] + [1 + ((m - 1 + turn) % 15) for m in range(1, 16)]


def rounds(state, cos_t, sin_t, forward):
    order = range(ROUNDS) if forward else range(ROUNDS - 1, -1, -1)
    for r in order:
        seat = seats(r % 15)
        shift = r % TILE
        for m in range(8):
            first = pl.ds(TILE * seat[m], TILE)
            second = pl.ds(TILE * seat[15 - m], TILE)
            q = r * 8 + m
            c = jnp.broadcast_to(cos_t[:, q : q + 1], (TILE, 128))
            s = jnp.broadcast_to(sin_t[:, q : q + 1], (TILE, 128))
            a = state[first, :]
            b = state[second, :]
            if shift:
                b = pltpu.roll(b, TILE - shift, 0)
            if forward:
                new_a = c * a - s * b
                new_b = s * a + c * b
            else:
                new_a = c * a + s * b
                new_b = c * b - s * a
            if shift:
                new_b = pltpu.roll(new_b, shift, 0)
            state[first, :] = new_a
            state[second, :] = new_b


def rotation_kernel(
    ids, angles, inv, hsub, basis, y_out, rows_out, bands_out, state, cos_t, sin_t, y_buf, z_buf, w_buf
):
    band = ids[0]
    me = ids[1]
    ang = jnp.concatenate([angles[...], jnp.zeros((16, TILE), F32)], 0)
    ang = jnp.concatenate([ang, jnp.zeros((256, 128 - TILE), F32)], 1)
    cos_t[...] = jnp.cos(ang).T[:TILE]
    sin_t[...] = jnp.sin(ang).T[:TILE]
    row = lax.broadcasted_iota(jnp.int32, (ORDER, 128), 0)
    lane = lax.broadcasted_iota(jnp.int32, (ORDER, 128), 1)
    target = ((lane >> 3) * NFFT + me) * 4 + (lane & 7)
    target = jnp.where((lane < 32) & ((lane & 7) < 4), target, -1)
    target = jnp.where((lane >= 32) & (lane < 40), lane - 32, target)
    state[...] = (row == target).astype(F32)
    rounds(state, cos_t, sin_t, False)
    low = inv[...].astype(BF16)
    y_all = dot(state[...].T.astype(BF16), low)
    y_buf[...] = y_all
    y_own = y_buf[:, pl.ds(pl.multiple_of(band * GROUP, GROUP), GROUP)]
    y_out[...] = y_own[:40]
    z_old = dot(y_own[:32].astype(BF16), hsub[...].astype(BF16))
    z_buf[...] = jnp.zeros_like(z_buf)
    for b in range(NBAND):
        z_buf[0:32, b * GROUP : b * GROUP + 126] = z_old[:, b * 126 : (b + 1) * 126]
    pick_row = lax.broadcasted_iota(jnp.int32, (8, ORDER), 0)
    pick_lane = lax.broadcasted_iota(jnp.int32, (8, ORDER), 1)
    z_buf[32:40, :] = (pick_lane == (pick_row >> 1) * GROUP + 126 + (pick_row & 1)).astype(F32)
    state[...] = dot(low, z_buf[...].T.astype(BF16))
    rounds(state, cos_t, sin_t, True)
    rows_out[...] = state[...].T[:40]
    weights = y_own[32:40].astype(BF16)
    spread_row = lax.broadcasted_iota(jnp.int32, (GROUP, 2048), 0)
    spread_lane = lax.broadcasted_iota(jnp.int32, (GROUP, 2048), 1)
    spread = (spread_row == (spread_lane >> 4)).astype(F32).astype(BF16)
    wide = dot(weights, spread)
    own_row = lax.broadcasted_iota(jnp.int32, (16, 2048), 0)
    own_lane = lax.broadcasted_iota(jnp.int32, (16, 2048), 1)
    keep = own_row == (own_lane & 15)
    for k in range(8):
        w_buf[16 * k : 16 * k + 16, :] = jnp.where(keep, wide[k : k + 1], 0.0).astype(BF16)
    bands_out[...] = dot(w_buf[...], basis[...]).astype(BF16)


def rotation_part(ids, angles, inv, hsub, basis):
    vmem = pl.BlockSpec(memory_space=pltpu.VMEM)
    return pl.pallas_call(
        rotation_kernel,
        out_shape=(
            jax.ShapeDtypeStruct((40, GROUP), F32),
            jax.ShapeDtypeStruct((40, ORDER), F32),
            jax.ShapeDtypeStruct((128, 128), BF16),
        ),
        in_specs=[pl.BlockSpec(memory_space=pltpu.SMEM)] + [vmem] * 4,
        out_specs=(vmem,) * 3,
        scratch_shapes=[
            pltpu.VMEM((ORDER, 128), F32),
            pltpu.VMEM((TILE, 256), F32),
            pltpu.VMEM((TILE, 256), F32),
            pltpu.VMEM((128, ORDER), F32),
            pltpu.VMEM((128, ORDER), F32),
            pltpu.VMEM((128, 2048), BF16),
        ],
        compiler_params=pltpu.CompilerParams(vmem_limit_bytes=48 * 2**20),
        name="rotation_part",
    )(ids, angles, inv, hsub, basis)


def main_kernel(
    basis, potential, columns, tz, tx, ty, ty_t, y_own, rows, bands_part,
    hblock_out, rotated_out, bands_out,
    send1, recv1, send2, recv2, send3, recv3, sendh, gath, recvb, sendf, recvf,
    a_cos, a_sin, right1, right2, radius, coef, d_buf, p_buf, g_buf,
    s1, r1, s2, r2, s3, r3, sh, rh, sb, rb, sf, rf,
):
    band = lax.axis_index("band")
    me = lax.axis_index("fft")

    barrier = pltpu.get_barrier_semaphore()

    def greet(i, carry):
        pl.semaphore_signal(
            barrier, inc=1, device_id=(band, lax.rem(me + i, NFFT)), device_id_type=MESH
        )
        return carry

    lax.fori_loop(1, NFFT, greet, 0)
    for i in range(1, NBAND):
        pl.semaphore_signal(
            barrier, inc=1, device_id=(lax.rem(band + i, NBAND), me), device_id_type=MESH
        )
    pl.semaphore_wait(barrier, NFFT - 1 + NBAND - 1)

    def fft_copy(i, send, recv, ssem, rsem, whole):
        to = lax.rem(me + i, NFFT)
        return pltpu.make_async_remote_copy(
            src_ref=send if whole else send.at[to],
            dst_ref=recv.at[me],
            send_sem=ssem.at[i],
            recv_sem=rsem.at[me],
            device_id=(band, to),
            device_id_type=MESH,
        )

    def fft_arrival(i, send, recv, ssem, rsem, whole):
        source = lax.rem(me + NFFT - i, NFFT)
        return pltpu.make_async_remote_copy(
            src_ref=send if whole else send.at[source],
            dst_ref=recv.at[source],
            send_sem=ssem.at[i],
            recv_sem=rsem.at[source],
            device_id=(band, source),
            device_id_type=MESH,
        )

    def fft_start(*args):
        def step(i, carry):
            fft_copy(i, *args).start()
            return carry

        lax.fori_loop(1, NFFT, step, 0)

    def fft_wait_recv(*args):
        def step(i, carry):
            fft_arrival(i, *args).wait_recv()
            return carry

        lax.fori_loop(1, NFFT, step, 0)

    def fft_wait_send(*args):
        def step(i, carry):
            fft_copy(i, *args).wait_send()
            return carry

        lax.fori_loop(1, NFFT, step, 0)

    def band_copy(i, src, dst, ssem, rsem):
        to = lax.rem(band + i, NBAND)
        return pltpu.make_async_remote_copy(
            src_ref=src(to),
            dst_ref=dst.at[band],
            send_sem=ssem.at[i],
            recv_sem=rsem.at[band],
            device_id=(to, me),
            device_id_type=MESH,
        )

    def band_arrival(i, src, dst, ssem, rsem):
        source = lax.rem(band + NBAND - i, NBAND)
        return pltpu.make_async_remote_copy(
            src_ref=src(source),
            dst_ref=dst.at[source],
            send_sem=ssem.at[i],
            recv_sem=rsem.at[source],
            device_id=(source, me),
            device_id_type=MESH,
        )

    new = basis[2016:2048, :]
    none = jnp.zeros((16, 128), BF16)
    right = jnp.concatenate(
        [
            jnp.concatenate([new[0:16], none], 1),
            jnp.concatenate([none, new[0:16]], 1),
            jnp.concatenate([new[16:32], none], 1),
            jnp.concatenate([none, new[16:32]], 1),
            jnp.zeros((64, 256), BF16),
        ],
        0,
    )
    send1[...] = dot_nt(tz[...], right).reshape(NFFT, 8, 128)
    first = (send1, recv1, s1, r1, False)
    fft_start(*first)
    recv1[pl.ds(me, 1)] = send1[pl.ds(me, 1)]

    bands_args = (lambda to: bands_part.at[to], recvb, sb, rb)
    for i in range(1, NBAND):
        band_copy(i, *bands_args).start()
    recvb[pl.ds(band, 1)] = bands_part[pl.ds(band, 1)]

    position = columns[...].astype(F32)
    pos_x = jnp.floor((position + 0.5) * (1.0 / NG))
    pos_y = position - NG * pos_x
    k_row = lax.broadcasted_iota(jnp.int32, (256, NCOL), 0).astype(F32)
    hot_x = (k_row == pos_x).astype(F32).astype(BF16)
    hot_y = (k_row == pos_y).astype(F32).astype(BF16)
    a_both = dot(tx[...], jnp.concatenate([hot_x, hot_x], 0))
    a_cos[...] = a_both[:NG]
    a_sin[...] = a_both[NG:]
    right2[:, :NCOL] = dot(ty[:, :256], hot_y).astype(BF16)
    right2[:, NCOL:] = dot(ty[:, 256:], hot_y).astype(BF16)
    wide_y = jnp.broadcast_to(pos_y, (128, NCOL)).T
    lane_k = lax.broadcasted_iota(jnp.int32, (NCOL, 128), 1).astype(F32)
    hot_yt = jnp.concatenate(
        [(wide_y == lane_k).astype(F32), (wide_y == lane_k + 128.0).astype(F32)], 1
    ).astype(BF16)
    right1[:NCOL, :] = dot(hot_yt, ty_t[:256, :]).astype(BF16)
    right1[NCOL:, :] = dot(hot_yt, ty_t[256:, :]).astype(BF16)
    freq_x = jnp.where(pos_x < NG // 2, pos_x, pos_x - NG)
    freq_y = jnp.where(pos_y < NG // 2, pos_y, pos_y - NG)
    radius[...] = jnp.broadcast_to(freq_x * freq_x + freq_y * freq_y, (128, NCOL)).T
    g_buf[...] = jnp.zeros_like(g_buf)
    p_buf[...] = jnp.zeros_like(p_buf)

    fft_wait_recv(*first)

    lanes = lax.broadcasted_iota(jnp.int32, (8, 128), 1)
    for q in range(4):
        for j in range(4):
            total = jnp.zeros((8, 128), F32)
            for t in range(8):
                piece = recv1[8 * j + t]
                move = (16 * t - 16 * q) % 128
                if move:
                    piece = pltpu.roll(piece, move, 1)
                total = jnp.where((lanes >> 4) == t, piece, total)
            coef[q, :, 128 * j : 128 * j + 128] = total

    def vector(v, carry):
        for z in range(SLAB):
            c_re = coef[2 * v, z : z + 1, :]
            c_im = coef[2 * v + 1, z : z + 1, :]
            d_buf[NG * z : NG * z + NG, :NCOL] = (a_cos[...] * c_re - a_sin[...] * c_im).astype(BF16)
            d_buf[NG * z : NG * z + NG, NCOL:] = (a_sin[...] * c_re + a_cos[...] * c_im).astype(BF16)
        field = dot(d_buf[...], right1[...])
        for z in range(SLAB):
            v_z = potential[z]
            p_buf[NG * z : NG * z + NG, 0:NG] = (field[NG * z : NG * z + NG, 0:NG] * v_z).astype(BF16)
            p_buf[NG * z : NG * z + NG, 256 : 256 + NG] = (
                field[NG * z : NG * z + NG, 256 : 256 + NG] * v_z
            ).astype(BF16)
        back = dot(p_buf[...], right2[...])
        for z in range(SLAB):
            u_re = back[NG * z : NG * z + NG, :NCOL]
            u_im = back[NG * z : NG * z + NG, NCOL:]
            g_buf[2 * v, z : z + 1, :] = jnp.sum(
                a_cos[...] * u_re + a_sin[...] * u_im, axis=0, keepdims=True
            )
            g_buf[2 * v + 1, z : z + 1, :] = jnp.sum(
                a_cos[...] * u_im - a_sin[...] * u_re, axis=0, keepdims=True
            )
        return carry

    lax.fori_loop(0, 2, vector, 0)

    volume = 1.0 / float(NG) ** 3
    for p in range(NFFT):
        total = jnp.zeros((8, 128), F32)
        for q in range(4):
            piece = g_buf[q, :, 128 * (p // 8) : 128 * (p // 8) + 128]
            move = (16 * q - 16 * (p % 8)) % 128
            if move:
                piece = pltpu.roll(piece, move, 1)
            total = jnp.where((lanes >> 4) == q, piece, total)
        send2[p] = total * volume
    second = (send2, recv2, s2, r2, False)
    fft_start(*second)
    recv2[pl.ds(me, 1)] = send2[pl.ds(me, 1)]

    for i in range(1, NBAND):
        band_arrival(i, *bands_args).wait_recv()
    bands_total = recvb[0].astype(F32)
    for b in range(1, NBAND):
        bands_total = bands_total + recvb[b].astype(F32)
    bands_out[...] = bands_total.astype(BF16)

    fft_wait_recv(*second)
    slabs = recv2[...].reshape(NFFT * 8, 128).T.astype(BF16)
    local = dot(slabs, tz[...])
    slot = lax.broadcasted_iota(jnp.int32, (16, 128), 1) & (NZC - 1)
    freq_z = jnp.where(slot < NZC // 2, slot, slot - NZC).astype(F32)
    own_radius = radius[pl.ds(pl.multiple_of(me * 16, 16), 16), :]
    kinetic = (own_radius + freq_z * freq_z) / (2.0 * (NG // 4) ** 2)
    for v in range(2):
        term = local[32 * v : 32 * v + 16, :128] + local[32 * v + 16 : 32 * v + 32, 128:]
        coeffs = basis[2016 + 16 * v : 2032 + 16 * v, :].astype(F32)
        sendh[16 * v : 16 * v + 16, :] = (kinetic * coeffs + term).astype(BF16)
    gather_args = (lambda to: sendh, gath, sh, rh)
    for i in range(1, NBAND):
        band_copy(i, *gather_args).start()
    gath[pl.ds(band, 1)] = sendh[...].reshape(1, 32, 128)
    hblock_out[...] = sendh[...]
    for i in range(1, NBAND):
        band_arrival(i, *gather_args).wait_recv()

    pairs = dot_nt(basis[...], gath[...].reshape(128, 128))
    pair_row = lax.broadcasted_iota(jnp.int32, (2048, 128), 0)
    pair_lane = lax.broadcasted_iota(jnp.int32, (2048, 128), 1)
    pairs = jnp.where(((pair_row ^ pair_lane) & 15) == 0, pairs, 0.0)
    by_group = jnp.sum(pairs.reshape(GROUP, 16, 128), axis=1)
    pick_row = lax.broadcasted_iota(jnp.int32, (8, 128), 0)
    pick = (pick_row == (lanes >> 4)).astype(F32)
    send3[...] = dot_nt(pick, by_group, HIGH)
    third = (send3, recv3, s3, r3, True)
    fft_start(*third)
    recv3[pl.ds(me, 1)] = send3[...].reshape(1, 8, 128)
    fft_wait_recv(*third)
    new_columns = recv3[0]
    for p in range(1, NFFT):
        new_columns = new_columns + recv3[p]
    new_columns = new_columns * (1.0 / math.sqrt(2 * NCOL * NZC))
    z_new = dot_nt(y_own[0:32, :], new_columns, HIGH)
    total = rows[0:32, :] + dot(z_new, rows[32:40, :], HIGH)
    sendf[...] = total.reshape(NBAND, 8, ORDER)
    final_args = (lambda to: sendf.at[to], recvf, sf, rf)
    for i in range(1, NBAND):
        band_copy(i, *final_args).start()
    recvf[pl.ds(band, 1)] = sendf[pl.ds(band, 1)]

    fft_wait_send(*first)
    fft_wait_send(*second)
    fft_wait_send(*third)
    for i in range(1, NBAND):
        band_copy(i, *bands_args).wait_send()
        band_copy(i, *gather_args).wait_send()
    for i in range(1, NBAND):
        band_arrival(i, *final_args).wait_recv()
    final = recvf[0] + recvf[1] + recvf[2] + recvf[3]
    rotated_out[...] = final[0:4]
    for i in range(1, NBAND):
        band_copy(i, *final_args).wait_send()


def main_part(*operands):
    vmem = pl.BlockSpec(memory_space=pltpu.VMEM)
    dma = pltpu.SemaphoreType.DMA
    return pl.pallas_call(
        main_kernel,
        out_shape=(
            jax.ShapeDtypeStruct((32, 128), BF16),
            jax.ShapeDtypeStruct((4, ORDER), F32),
            jax.ShapeDtypeStruct((32, 128), BF16),
        ),
        in_specs=[vmem] * len(operands),
        out_specs=(vmem,) * 3,
        scratch_shapes=[
            pltpu.VMEM((NFFT, 8, 128), F32),
            pltpu.VMEM((NFFT, 8, 128), F32),
            pltpu.VMEM((NFFT, 8, 128), F32),
            pltpu.VMEM((NFFT, 8, 128), F32),
            pltpu.VMEM((8, 128), F32),
            pltpu.VMEM((NFFT, 8, 128), F32),
            pltpu.VMEM((32, 128), BF16),
            pltpu.VMEM((NBAND, 32, 128), BF16),
            pltpu.VMEM((NBAND, 32, 128), BF16),
            pltpu.VMEM((NBAND, 8, ORDER), F32),
            pltpu.VMEM((NBAND, 8, ORDER), F32),
            pltpu.VMEM((NG, NCOL), F32),
            pltpu.VMEM((NG, NCOL), F32),
            pltpu.VMEM((2 * NCOL, 512), BF16),
            pltpu.VMEM((512, 2 * NCOL), BF16),
            pltpu.VMEM((NCOL, 128), F32),
            pltpu.VMEM((4, 8, NCOL), F32),
            pltpu.VMEM((SLAB * NG, 2 * NCOL), BF16),
            pltpu.VMEM((SLAB * NG, 512), BF16),
            pltpu.VMEM((4, 8, NCOL), F32),
        ]
        + [dma((NFFT,))] * 6
        + [dma((NBAND,))] * 6,
        compiler_params=pltpu.CompilerParams(
            collective_id=0, has_side_effects=True, vmem_limit_bytes=56 * 2**20
        ),
        name="main_part",
    )(*operands)


def per_device(basis, potential, colmap, hsub_old, inv_factor, angles):
    ids = jnp.stack([lax.axis_index("band"), lax.axis_index("fft")]).astype(jnp.int32)
    flat = basis.reshape(2048, 128)
    y_own, rows, bands_part = rotation_part(ids, angles.reshape(240, TILE), inv_factor, hsub_old, flat)
    left = y_table_left()
    hblock, rotated, bands = main_part(
        flat,
        potential,
        colmap.reshape(1, NCOL),
        jnp.asarray(z_table().astype(BF16)),
        jnp.asarray(x_table()),
        jnp.asarray(left.astype(BF16)),
        jnp.asarray(left.T.astype(BF16)),
        y_own,
        rows,
        bands_part.reshape(NBAND, 32, 128),
    )
    return (hblock.reshape(2, 16, 128), rotated, bands.reshape(2, 16, 128))


def solution(mesh):
    in_specs = (P("band", "fft", None), P("fft", None, None), P(), P("band", None), P(), P())
    out_specs = (P("band", "fft", None), P(("band", "fft"), None), P("band", "fft", None))
    return jax.shard_map(
        per_device, mesh=mesh, in_specs=in_specs, out_specs=out_specs, check_vma=False
    )
```

```python
import functools
import math

import jax
import jax.numpy as jnp
import numpy as np
from jax import lax
from jax.experimental import pallas as pl
from jax.experimental.pallas import tpu as pltpu
from jax.sharding import PartitionSpec as P

NG = 192
NZC = 64
ORDER = 512
GROUP = 128
NCOL = 512
NBAND = 4
NFFT = 32
SLAB = 6
ROUNDS = 30
TILE = 32
F32 = jnp.float32
BF16 = jnp.bfloat16
HIGH = lax.Precision.HIGHEST
MESH = pl.DeviceIdType.MESH
NT = (((1,), (1,)), ((), ()))


def dot(a, b, precision=None):
    return jnp.dot(a, b, precision=precision, preferred_element_type=F32)


def dot_nt(a, b, precision=None):
    return lax.dot_general(a, b, NT, precision=precision, preferred_element_type=F32)


def z_table():
    slot = np.arange(NZC)
    freq = np.where(slot < NZC // 2, slot, slot - NZC) % NG
    table = np.zeros((NFFT, 8, 4, NZC), np.float64)
    z = np.arange(NG).reshape(NFFT, SLAB)
    angle = 2.0 * np.pi * ((z[:, :, None] * freq) % NG) / NG
    table[:, :SLAB, 0] = np.cos(angle)
    table[:, :SLAB, 1] = -np.sin(angle)
    table[:, :SLAB, 2] = np.sin(angle)
    table[:, :SLAB, 3] = np.cos(angle)
    return table.reshape(NFFT * 8, 4 * NZC)


def plane_angles():
    ids = np.arange(NG)
    return 2.0 * np.pi * ((ids[:, None] * ids[None, :]) % NG) / NG


def x_table():
    angle = plane_angles()
    both = np.concatenate([np.cos(angle), np.sin(angle)], 0)
    high = np.asarray(both, np.float32).astype(BF16)
    low = (both - high.astype(np.float64)).astype(BF16)
    table = np.zeros((2 * NG, 512), BF16)
    table[:, :NG] = high
    table[:, 256 : 256 + NG] = low
    return table


def y_table_left():
    angle = plane_angles()
    table = np.zeros((2, 256, 2, 256), np.float64)
    table[0, :NG, 0, :NG] = np.cos(angle)
    table[0, :NG, 1, :NG] = -np.sin(angle)
    table[1, :NG, 0, :NG] = np.sin(angle)
    table[1, :NG, 1, :NG] = np.cos(angle)
    return table.reshape(512, 512)


def tile_order(turn):
    seat = [0] + [1 + ((m - 1 + turn) % 15) for m in range(1, 16)]
    return seat[:8] + seat[:7:-1]


def pair_step(state, table, r, forward):
    src, dst = state.at[r % 2], state.at[(r + 1) % 2]
    shift = r % TILE
    c = table[0, 8 * r : 8 * r + 8]
    s = table[1, 8 * r : 8 * r + 8]
    a = src[0:8]
    b = src[8:16]
    if shift:
        b = pltpu.roll(b, TILE - shift, 1)
    if forward:
        a, b = c * a - s * b, s * a + c * b
    else:
        a, b = c * a + s * b, c * b - s * a
    if shift:
        b = pltpu.roll(b, shift, 1)
    if forward:
        dst[0:1] = a[0:1]
        dst[1:7] = a[2:8]
        dst[7:8] = b[7:8]
        dst[8:9] = a[1:2]
        dst[9:16] = b[0:7]
    elif r:
        dst[0:1] = a[0:1]
        dst[2:8] = a[1:7]
        dst[15:16] = a[7:8]
        dst[1:2] = b[0:1]
        dst[8:15] = b[1:8]
    else:
        dst[0:8] = a
        dst[8:16] = b


def angle_tables(angles, table):
    ang = jnp.concatenate([angles[...], jnp.zeros((240, 128 - TILE), F32)], 1)
    ang = jnp.concatenate([ang, jnp.zeros((16, 128), F32)], 0)
    for i, part in enumerate((jnp.cos(ang).T[:TILE], jnp.sin(ang).T[:TILE])):
        for q in range(8 * ROUNDS):
            table[i, q] = jnp.broadcast_to(part[:, q : q + 1], (TILE, 128))


def rotate_back(me, state, table):
    row = lax.broadcasted_iota(jnp.int32, (TILE, 128), 0)
    lane = lax.broadcasted_iota(jnp.int32, (TILE, 128), 1)
    target = ((lane >> 3) * NFFT + me) * 4 + (lane & 7)
    target = jnp.where((lane < 32) & ((lane & 7) < 4), target, -1)
    target = jnp.where((lane >= 32) & (lane < 40), lane - 32, target)
    for p, tile in enumerate(tile_order(14)):
        state[1, p] = (row + TILE * tile == target).astype(F32)
    for r in range(ROUNDS - 1, -1, -1):
        pair_step(state, table, r, False)


def natural(state, which):
    return jnp.concatenate([state[which, p] for p in list(range(8)) + list(range(15, 7, -1))], 0)


def couple(band, state, inv, hsub, low, y_buf, y_own, z_buf):
    low[...] = inv[...].astype(BF16)
    y_buf[...] = dot(natural(state, 1).T.astype(BF16), low[...])
    own = y_buf[:, pl.ds(pl.multiple_of(band * GROUP, GROUP), GROUP)]
    y_own[...] = own[:40]
    z_old = dot_nt(hsub[...].astype(BF16), own.astype(BF16))
    lane = lax.broadcasted_iota(jnp.int32, (8, 128), 1)
    row = lax.broadcasted_iota(jnp.int32, (8, 128), 0)
    z_buf[...] = jnp.zeros_like(z_buf)
    for b in range(NBAND):
        z_buf[b * GROUP : b * GROUP + 126, :] = z_old[b * 126 : (b + 1) * 126, :]
    lanes = lax.broadcasted_iota(jnp.int32, (ORDER, 128), 1)
    rows = lax.broadcasted_iota(jnp.int32, (ORDER, 128), 0)
    fresh = ((lanes - 32) >> 1) * GROUP + 126 + (lanes & 1)
    z = jnp.where(lanes < 32, z_buf[...], 0.0)
    z = jnp.where((lanes >= 32) & (lanes < 40) & (rows == fresh), 1.0, z)
    w = dot(low[...], z.astype(BF16))
    for p, tile in enumerate(tile_order(0)):
        state[0, p] = w[TILE * tile : TILE * tile + TILE]


def rotate_on(state, table, rows):
    for r in range(ROUNDS):
        pair_step(state, table, r, True)
    rows[...] = natural(state, 0).T[:40]


def vector_weights(basis, y_own, w_buf, bands_part):
    weights = y_own[32:40, :].astype(BF16)
    spread_row = lax.broadcasted_iota(jnp.int32, (GROUP, 2048), 0)
    spread_lane = lax.broadcasted_iota(jnp.int32, (GROUP, 2048), 1)
    spread = (spread_row == (spread_lane >> 4)).astype(F32).astype(BF16)
    wide = dot(weights, spread)
    own_row = lax.broadcasted_iota(jnp.int32, (16, 2048), 0)
    own_lane = lax.broadcasted_iota(jnp.int32, (16, 2048), 1)
    keep = own_row == (own_lane & 15)
    for k in range(8):
        w_buf[16 * k : 16 * k + 16, :] = jnp.where(keep, wide[k : k + 1], 0.0).astype(BF16)
    bands_part[...] = dot(w_buf[...], basis[...]).astype(BF16).reshape(NBAND, 32, 128)


def main_kernel(
    basis_in, columns_in, angles_in, tz_in, inv_in, hsub_in, tx_in, ty_in, ty_t_in, potential_in,
    hblock_out, rotated_out, bands_out,
    basis, columns, angles, tz, inv, hsub, tx, ty, ty_t, potential,
    state, table, low, y_buf, y_own, z_buf, rows, w_buf, bands_part,
    send1, recv1, send2, recv2, send3, recv3, sendh, gath, recvb, sendf, recvf,
    a_cos, a_sin, right1, right2, radius, coef, d_buf, p_buf, g_buf,
    s1, r1, s2, r2, s3, r3, sh, rh, sb, rb, sf, rf, loads,
):
    band = lax.axis_index("band")
    me = lax.axis_index("fft")

    inputs = (
        (basis_in, basis), (tz_in, tz), (angles_in, angles), (columns_in, columns), (tx_in, tx),
        (ty_in, ty), (ty_t_in, ty_t), (inv_in, inv), (hsub_in, hsub), (potential_in, potential),
    )
    copies = [pltpu.make_async_copy(a, b, loads.at[i]) for i, (a, b) in enumerate(inputs)]
    for copy in copies:
        copy.start()

    barrier = pltpu.get_barrier_semaphore()

    def greet(i, carry):
        pl.semaphore_signal(
            barrier, inc=1, device_id=(band, lax.rem(me + i, NFFT)), device_id_type=MESH
        )
        return carry

    lax.fori_loop(1, NFFT, greet, 0)
    for i in range(1, NBAND):
        pl.semaphore_signal(
            barrier, inc=1, device_id=(lax.rem(band + i, NBAND), me), device_id_type=MESH
        )

    def fft_copy(i, send, recv, ssem, rsem, whole):
        to = lax.rem(me + i, NFFT)
        return pltpu.make_async_remote_copy(
            src_ref=send if whole else send.at[to],
            dst_ref=recv.at[me],
            send_sem=ssem.at[i],
            recv_sem=rsem.at[me],
            device_id=(band, to),
            device_id_type=MESH,
        )

    def fft_arrival(i, send, recv, ssem, rsem, whole):
        source = lax.rem(me + NFFT - i, NFFT)
        return pltpu.make_async_remote_copy(
            src_ref=send if whole else send.at[source],
            dst_ref=recv.at[source],
            send_sem=ssem.at[i],
            recv_sem=rsem.at[source],
            device_id=(band, source),
            device_id_type=MESH,
        )

    def fft_start(*args):
        def step(i, carry):
            fft_copy(i, *args).start()
            return carry

        lax.fori_loop(1, NFFT, step, 0)

    def fft_wait_recv(*args):
        def step(i, carry):
            fft_arrival(i, *args).wait_recv()
            return carry

        lax.fori_loop(1, NFFT, step, 0)

    def fft_wait_send(*args):
        def step(i, carry):
            fft_copy(i, *args).wait_send()
            return carry

        lax.fori_loop(1, NFFT, step, 0)

    def band_copy(i, src, dst, ssem, rsem):
        to = lax.rem(band + i, NBAND)
        return pltpu.make_async_remote_copy(
            src_ref=src(to),
            dst_ref=dst.at[band],
            send_sem=ssem.at[i],
            recv_sem=rsem.at[band],
            device_id=(to, me),
            device_id_type=MESH,
        )

    def band_arrival(i, src, dst, ssem, rsem):
        source = lax.rem(band + NBAND - i, NBAND)
        return pltpu.make_async_remote_copy(
            src_ref=src(source),
            dst_ref=dst.at[source],
            send_sem=ssem.at[i],
            recv_sem=rsem.at[source],
            device_id=(source, me),
            device_id_type=MESH,
        )

    copies[0].wait()
    copies[1].wait()
    new = basis[2016:2048, :]
    none = jnp.zeros((16, 128), BF16)
    right = jnp.concatenate(
        [
            jnp.concatenate([new[0:16], none], 1),
            jnp.concatenate([none, new[0:16]], 1),
            jnp.concatenate([new[16:32], none], 1),
            jnp.concatenate([none, new[16:32]], 1),
            jnp.zeros((64, 256), BF16),
        ],
        0,
    )
    send1[...] = dot_nt(tz[...], right).reshape(NFFT, 8, 128)
    first = (send1, recv1, s1, r1, False)
    copies[2].wait()
    angle_tables(angles, table)
    pl.semaphore_wait(barrier, NFFT - 1 + NBAND - 1)
    fft_start(*first)
    recv1[pl.ds(me, 1)] = send1[pl.ds(me, 1)]

    rotate_back(me, state, table)

    for i in range(3, 7):
        copies[i].wait()
    position = columns[...].astype(F32)
    pos_x = jnp.floor((position + 0.5) * (1.0 / NG))
    pos_y = position - NG * pos_x
    k_row = lax.broadcasted_iota(jnp.int32, (256, NCOL), 0).astype(F32)
    hot_x = (k_row == pos_x).astype(F32).astype(BF16)
    hot_y = (k_row == pos_y).astype(F32).astype(BF16)
    a_both = dot(tx[...], jnp.concatenate([hot_x, hot_x], 0))
    a_cos[...] = a_both[:NG]
    a_sin[...] = a_both[NG:]
    right2[:, :NCOL] = dot(ty[:, :256], hot_y).astype(BF16)
    right2[:, NCOL:] = dot(ty[:, 256:], hot_y).astype(BF16)
    wide_y = jnp.broadcast_to(pos_y, (128, NCOL)).T
    lane_k = lax.broadcasted_iota(jnp.int32, (NCOL, 128), 1).astype(F32)
    hot_yt = jnp.concatenate(
        [(wide_y == lane_k).astype(F32), (wide_y == lane_k + 128.0).astype(F32)], 1
    ).astype(BF16)
    right1[:NCOL, :] = dot(hot_yt, ty_t[:256, :]).astype(BF16)
    right1[NCOL:, :] = dot(hot_yt, ty_t[256:, :]).astype(BF16)
    freq_x = jnp.where(pos_x < NG // 2, pos_x, pos_x - NG)
    freq_y = jnp.where(pos_y < NG // 2, pos_y, pos_y - NG)
    radius[...] = jnp.broadcast_to(freq_x * freq_x + freq_y * freq_y, (128, NCOL)).T
    g_buf[...] = jnp.zeros_like(g_buf)
    p_buf[...] = jnp.zeros_like(p_buf)

    for i in range(7, 10):
        copies[i].wait()
    couple(band, state, inv, hsub, low, y_buf, y_own, z_buf)
    fft_wait_recv(*first)

    lanes = lax.broadcasted_iota(jnp.int32, (8, 128), 1)
    for q in range(4):
        for j in range(4):
            total = jnp.zeros((8, 128), F32)
            for t in range(8):
                piece = recv1[8 * j + t]
                move = (16 * t - 16 * q) % 128
                if move:
                    piece = pltpu.roll(piece, move, 1)
                total = jnp.where((lanes >> 4) == t, piece, total)
            coef[q, :, 128 * j : 128 * j + 128] = total

    def vector(v, carry):
        for z in range(SLAB):
            c_re = coef[2 * v, z : z + 1, :]
            c_im = coef[2 * v + 1, z : z + 1, :]
            d_buf[NG * z : NG * z + NG, :NCOL] = (a_cos[...] * c_re - a_sin[...] * c_im).astype(BF16)
            d_buf[NG * z : NG * z + NG, NCOL:] = (a_sin[...] * c_re + a_cos[...] * c_im).astype(BF16)
        field = dot(d_buf[...], right1[...])
        for z in range(SLAB):
            v_z = potential[z]
            p_buf[NG * z : NG * z + NG, 0:NG] = (field[NG * z : NG * z + NG, 0:NG] * v_z).astype(BF16)
            p_buf[NG * z : NG * z + NG, 256 : 256 + NG] = (
                field[NG * z : NG * z + NG, 256 : 256 + NG] * v_z
            ).astype(BF16)
        back = dot(p_buf[...], right2[...])
        for z in range(SLAB):
            u_re = back[NG * z : NG * z + NG, :NCOL]
            u_im = back[NG * z : NG * z + NG, NCOL:]
            g_buf[2 * v, z : z + 1, :] = jnp.sum(
                a_cos[...] * u_re + a_sin[...] * u_im, axis=0, keepdims=True
            )
            g_buf[2 * v + 1, z : z + 1, :] = jnp.sum(
                a_cos[...] * u_im - a_sin[...] * u_re, axis=0, keepdims=True
            )
        return carry

    lax.fori_loop(0, 2, vector, 0)

    volume = 1.0 / float(NG) ** 3
    for p in range(NFFT):
        total = jnp.zeros((8, 128), F32)
        for q in range(4):
            piece = g_buf[q, :, 128 * (p // 8) : 128 * (p // 8) + 128]
            move = (16 * q - 16 * (p % 8)) % 128
            if move:
                piece = pltpu.roll(piece, move, 1)
            total = jnp.where((lanes >> 4) == q, piece, total)
        send2[p] = total * volume
    second = (send2, recv2, s2, r2, False)
    fft_start(*second)
    recv2[pl.ds(me, 1)] = send2[pl.ds(me, 1)]

    vector_weights(basis, y_own, w_buf, bands_part)
    bands_args = (lambda to: bands_part.at[to], recvb, sb, rb)
    for i in range(1, NBAND):
        band_copy(i, *bands_args).start()
    recvb[pl.ds(band, 1)] = bands_part[pl.ds(band, 1)]
    rotate_on(state, table, rows)

    fft_wait_recv(*second)
    slabs = recv2[...].reshape(NFFT * 8, 128).T.astype(BF16)
    local = dot(slabs, tz[...])
    slot = lax.broadcasted_iota(jnp.int32, (16, 128), 1) & (NZC - 1)
    freq_z = jnp.where(slot < NZC // 2, slot, slot - NZC).astype(F32)
    own_radius = radius[pl.ds(pl.multiple_of(me * 16, 16), 16), :]
    kinetic = (own_radius + freq_z * freq_z) / (2.0 * (NG // 4) ** 2)
    for v in range(2):
        term = local[32 * v : 32 * v + 16, :128] + local[32 * v + 16 : 32 * v + 32, 128:]
        coeffs = basis[2016 + 16 * v : 2032 + 16 * v, :].astype(F32)
        sendh[16 * v : 16 * v + 16, :] = (kinetic * coeffs + term).astype(BF16)
    gather_args = (lambda to: sendh, gath, sh, rh)
    for i in range(1, NBAND):
        band_copy(i, *gather_args).start()
    gath[pl.ds(band, 1)] = sendh[...].reshape(1, 32, 128)
    hblock_out[...] = sendh[...]

    for i in range(1, NBAND):
        band_arrival(i, *bands_args).wait_recv()
    bands_total = recvb[0].astype(F32)
    for b in range(1, NBAND):
        bands_total = bands_total + recvb[b].astype(F32)
    bands_out[...] = bands_total.astype(BF16)

    for i in range(1, NBAND):
        band_arrival(i, *gather_args).wait_recv()

    pairs = dot_nt(basis[...], gath[...].reshape(128, 128))
    pair_row = lax.broadcasted_iota(jnp.int32, (2048, 128), 0)
    pair_lane = lax.broadcasted_iota(jnp.int32, (2048, 128), 1)
    pairs = jnp.where(((pair_row ^ pair_lane) & 15) == 0, pairs, 0.0)
    by_group = jnp.sum(pairs.reshape(GROUP, 16, 128), axis=1)
    pick_row = lax.broadcasted_iota(jnp.int32, (8, 128), 0)
    pick = (pick_row == (lanes >> 4)).astype(F32)
    send3[...] = dot_nt(pick, by_group, HIGH)
    third = (send3, recv3, s3, r3, True)
    fft_start(*third)
    recv3[pl.ds(me, 1)] = send3[...].reshape(1, 8, 128)
    fft_wait_recv(*third)
    new_columns = recv3[0]
    for p in range(1, NFFT):
        new_columns = new_columns + recv3[p]
    new_columns = new_columns * (1.0 / math.sqrt(2 * NCOL * NZC))
    z_new = dot_nt(y_own[0:32, :], new_columns, HIGH)
    total = rows[0:32, :] + dot(z_new, rows[32:40, :], HIGH)
    sendf[...] = total.reshape(NBAND, 8, ORDER)
    final_args = (lambda to: sendf.at[to], recvf, sf, rf)
    for i in range(1, NBAND):
        band_copy(i, *final_args).start()
    recvf[pl.ds(band, 1)] = sendf[pl.ds(band, 1)]

    fft_wait_send(*first)
    fft_wait_send(*second)
    fft_wait_send(*third)
    for i in range(1, NBAND):
        band_copy(i, *bands_args).wait_send()
        band_copy(i, *gather_args).wait_send()
    for i in range(1, NBAND):
        band_arrival(i, *final_args).wait_recv()
    final = recvf[0] + recvf[1] + recvf[2] + recvf[3]
    rotated_out[...] = final[0:4]
    for i in range(1, NBAND):
        band_copy(i, *final_args).wait_send()


def main_part(*operands):
    vmem = pl.BlockSpec(memory_space=pltpu.VMEM)
    dma = pltpu.SemaphoreType.DMA
    return pl.pallas_call(
        main_kernel,
        out_shape=(
            jax.ShapeDtypeStruct((32, 128), BF16),
            jax.ShapeDtypeStruct((4, ORDER), F32),
            jax.ShapeDtypeStruct((32, 128), BF16),
        ),
        in_specs=[pl.BlockSpec(memory_space=pl.ANY)] * len(operands),
        out_specs=(vmem,) * 3,
        scratch_shapes=[pltpu.VMEM(x.shape, x.dtype) for x in operands]
        + [
            pltpu.VMEM((2, 16, TILE, 128), F32),
            pltpu.VMEM((2, 8 * ROUNDS, TILE, 128), F32),
            pltpu.VMEM((ORDER, ORDER), BF16),
            pltpu.VMEM((128, ORDER), F32),
            pltpu.VMEM((40, GROUP), F32),
            pltpu.VMEM((ORDER, 128), F32),
            pltpu.VMEM((40, ORDER), F32),
            pltpu.VMEM((128, 2048), BF16),
            pltpu.VMEM((NBAND, 32, 128), BF16),
            pltpu.VMEM((NFFT, 8, 128), F32),
            pltpu.VMEM((NFFT, 8, 128), F32),
            pltpu.VMEM((NFFT, 8, 128), F32),
            pltpu.VMEM((NFFT, 8, 128), F32),
            pltpu.VMEM((8, 128), F32),
            pltpu.VMEM((NFFT, 8, 128), F32),
            pltpu.VMEM((32, 128), BF16),
            pltpu.VMEM((NBAND, 32, 128), BF16),
            pltpu.VMEM((NBAND, 32, 128), BF16),
            pltpu.VMEM((NBAND, 8, ORDER), F32),
            pltpu.VMEM((NBAND, 8, ORDER), F32),
            pltpu.VMEM((NG, NCOL), F32),
            pltpu.VMEM((NG, NCOL), F32),
            pltpu.VMEM((2 * NCOL, 512), BF16),
            pltpu.VMEM((512, 2 * NCOL), BF16),
            pltpu.VMEM((NCOL, 128), F32),
            pltpu.VMEM((4, 8, NCOL), F32),
            pltpu.VMEM((SLAB * NG, 2 * NCOL), BF16),
            pltpu.VMEM((SLAB * NG, 512), BF16),
            pltpu.VMEM((4, 8, NCOL), F32),
        ]
        + [dma((NFFT,))] * 6
        + [dma((NBAND,))] * 6
        + [dma((len(operands),))],
        compiler_params=pltpu.CompilerParams(
            collective_id=0, has_side_effects=True, vmem_limit_bytes=56 * 2**20
        ),
        name="main_part",
    )(*operands)


def result_kernel(*refs):
    sources, targets, sems = refs[:3], refs[3:6], refs[6]
    copies = [
        pltpu.make_async_copy(a, b, sems.at[i]) for i, (a, b) in enumerate(zip(sources, targets))
    ]
    for copy in copies:
        copy.start()
    for copy in copies:
        copy.wait()


def result_part(*operands):
    anywhere = pl.BlockSpec(memory_space=pl.ANY)
    return pl.pallas_call(
        result_kernel,
        out_shape=tuple(jax.ShapeDtypeStruct(x.shape, x.dtype) for x in operands),
        in_specs=[anywhere] * 3,
        out_specs=(anywhere,) * 3,
        scratch_shapes=[pltpu.SemaphoreType.DMA((3,))],
        compiler_params=pltpu.CompilerParams(vmem_limit_bytes=56 * 2**20),
        name="result_part",
    )(*operands)


def per_device(basis, potential, colmap, hsub_old, inv_factor, angles):
    left = y_table_left()
    results = main_part(
        basis.reshape(2048, 128),
        colmap.reshape(1, NCOL),
        angles.reshape(8 * ROUNDS, TILE),
        jnp.asarray(z_table().astype(BF16)),
        inv_factor,
        hsub_old.T,
        jnp.asarray(x_table()),
        jnp.asarray(left.astype(BF16)),
        jnp.asarray(left.T.astype(BF16)),
        potential,
    )
    hblock, rotated, bands = result_part(*results)
    return (hblock.reshape(2, 16, 128), rotated, bands.reshape(2, 16, 128))


def solution(mesh):
    in_specs = (P("band", "fft", None), P("fft", None, None), P(), P("band", None), P(), P())
    out_specs = (P("band", "fft", None), P(("band", "fft"), None), P("band", "fft", None))
    return jax.shard_map(
        per_device, mesh=mesh, in_specs=in_specs, out_specs=out_specs, check_vma=False
    )
```

```python
import functools
import math

import jax
import jax.numpy as jnp
import numpy as np
from jax import lax
from jax.experimental import pallas as pl
from jax.experimental.pallas import tpu as pltpu
from jax.sharding import PartitionSpec as P

NG = 192
NZC = 64
ORDER = 512
GROUP = 128
NCOL = 512
NBAND = 4
NFFT = 32
SLAB = 6
ROUNDS = 30
TILE = 32
F32 = jnp.float32
BF16 = jnp.bfloat16
HIGH = lax.Precision.HIGHEST
MESH = pl.DeviceIdType.MESH
NT = (((1,), (1,)), ((), ()))


def dot(a, b, precision=None):
    return jnp.dot(a, b, precision=precision, preferred_element_type=F32)


def dot_nt(a, b, precision=None):
    return lax.dot_general(a, b, NT, precision=precision, preferred_element_type=F32)


def z_table():
    slot = np.arange(NZC)
    freq = np.where(slot < NZC // 2, slot, slot - NZC) % NG
    table = np.zeros((NFFT, 8, 4, NZC), np.float64)
    z = np.arange(NG).reshape(NFFT, SLAB)
    angle = 2.0 * np.pi * ((z[:, :, None] * freq) % NG) / NG
    table[:, :SLAB, 0] = np.cos(angle)
    table[:, :SLAB, 1] = -np.sin(angle)
    table[:, :SLAB, 2] = np.sin(angle)
    table[:, :SLAB, 3] = np.cos(angle)
    return table.reshape(NFFT * 8, 4 * NZC)


def plane_angles():
    ids = np.arange(NG)
    return 2.0 * np.pi * ((ids[:, None] * ids[None, :]) % NG) / NG


def x_table():
    angle = plane_angles()
    both = np.concatenate([np.cos(angle), np.sin(angle)], 0)
    high = np.asarray(both, np.float32).astype(BF16)
    low = (both - high.astype(np.float64)).astype(BF16)
    table = np.zeros((2 * NG, 512), BF16)
    table[:, :NG] = high
    table[:, 256 : 256 + NG] = low
    return table


def y_table_left():
    angle = plane_angles()
    table = np.zeros((2, 256, 2, 256), np.float64)
    table[0, :NG, 0, :NG] = np.cos(angle)
    table[0, :NG, 1, :NG] = -np.sin(angle)
    table[1, :NG, 0, :NG] = np.sin(angle)
    table[1, :NG, 1, :NG] = np.cos(angle)
    return table.reshape(512, 512)


def tile_order(turn):
    seat = [0] + [1 + ((m - 1 + turn) % 15) for m in range(1, 16)]
    return seat[:8] + seat[:7:-1]


def pair_step(state, table, r, forward):
    src, dst = state.at[r % 2], state.at[(r + 1) % 2]
    shift = r % TILE
    c = table[0, 8 * r : 8 * r + 8]
    s = table[1, 8 * r : 8 * r + 8]
    a = src[0:8]
    b = src[8:16]
    if shift:
        b = pltpu.roll(b, TILE - shift, 1)
    if forward:
        a, b = c * a - s * b, s * a + c * b
    else:
        a, b = c * a + s * b, c * b - s * a
    if shift:
        b = pltpu.roll(b, shift, 1)
    if forward:
        dst[0:1] = a[0:1]
        dst[1:7] = a[2:8]
        dst[7:8] = b[7:8]
        dst[8:9] = a[1:2]
        dst[9:16] = b[0:7]
    elif r:
        dst[0:1] = a[0:1]
        dst[2:8] = a[1:7]
        dst[15:16] = a[7:8]
        dst[1:2] = b[0:1]
        dst[8:15] = b[1:8]
    else:
        dst[0:8] = a
        dst[8:16] = b


def angle_tables(angles, table):
    ang = jnp.concatenate([angles[...], jnp.zeros((240, 128 - TILE), F32)], 1)
    ang = jnp.concatenate([ang, jnp.zeros((16, 128), F32)], 0)
    for i, part in enumerate((jnp.cos(ang).T[:TILE], jnp.sin(ang).T[:TILE])):
        for q in range(8 * ROUNDS):
            table[i, q] = jnp.broadcast_to(part[:, q : q + 1], (TILE, 128))


def rotate_back(me, state, table):
    row = lax.broadcasted_iota(jnp.int32, (TILE, 128), 0)
    lane = lax.broadcasted_iota(jnp.int32, (TILE, 128), 1)
    target = ((lane >> 3) * NFFT + me) * 4 + (lane & 7)
    target = jnp.where((lane < 32) & ((lane & 7) < 4), target, -1)
    target = jnp.where((lane >= 32) & (lane < 40), lane - 32, target)
    for p, tile in enumerate(tile_order(14)):
        state[1, p] = (row + TILE * tile == target).astype(F32)
    for r in range(ROUNDS - 1, -1, -1):
        pair_step(state, table, r, False)


def natural(state, which):
    return jnp.concatenate([state[which, p] for p in list(range(8)) + list(range(15, 7, -1))], 0)


def couple(band, state, inv, hsub, low, y_buf, y_own, z_buf):
    low[...] = inv[...].astype(BF16)
    y_buf[...] = dot(natural(state, 1).T.astype(BF16), low[...])
    own = y_buf[:, pl.ds(pl.multiple_of(band * GROUP, GROUP), GROUP)]
    y_own[...] = own[:40]
    z_old = dot_nt(hsub[...].astype(BF16), own.astype(BF16))
    lane = lax.broadcasted_iota(jnp.int32, (8, 128), 1)
    row = lax.broadcasted_iota(jnp.int32, (8, 128), 0)
    z_buf[...] = jnp.zeros_like(z_buf)
    for b in range(NBAND):
        z_buf[b * GROUP : b * GROUP + 126, :] = z_old[b * 126 : (b + 1) * 126, :]
    lanes = lax.broadcasted_iota(jnp.int32, (ORDER, 128), 1)
    rows = lax.broadcasted_iota(jnp.int32, (ORDER, 128), 0)
    fresh = ((lanes - 32) >> 1) * GROUP + 126 + (lanes & 1)
    z = jnp.where(lanes < 32, z_buf[...], 0.0)
    z = jnp.where((lanes >= 32) & (lanes < 40) & (rows == fresh), 1.0, z)
    w = dot(low[...], z.astype(BF16))
    for p, tile in enumerate(tile_order(0)):
        state[0, p] = w[TILE * tile : TILE * tile + TILE]


def rotate_on(state, table, rows):
    for r in range(ROUNDS):
        pair_step(state, table, r, True)
    rows[...] = natural(state, 0).T[:40]


def vector_weights(basis, y_own, w_buf, bands_part):
    weights = y_own[32:40, :].astype(BF16)
    spread_row = lax.broadcasted_iota(jnp.int32, (GROUP, 2048), 0)
    spread_lane = lax.broadcasted_iota(jnp.int32, (GROUP, 2048), 1)
    spread = (spread_row == (spread_lane >> 4)).astype(F32).astype(BF16)
    wide = dot(weights, spread)
    own_row = lax.broadcasted_iota(jnp.int32, (16, 2048), 0)
    own_lane = lax.broadcasted_iota(jnp.int32, (16, 2048), 1)
    keep = own_row == (own_lane & 15)
    for k in range(8):
        w_buf[16 * k : 16 * k + 16, :] = jnp.where(keep, wide[k : k + 1], 0.0).astype(BF16)
    bands_part[...] = dot(w_buf[...], basis[...]).astype(BF16).reshape(NBAND, 32, 128)


def main_kernel(
    basis_in, columns_in, angles_in, tz_in, inv_in, hsub_in, tx_in, ty_in, ty_t_in, potential_in,
    hblock_out, rotated_out, bands_out,
    basis, columns, angles, tz, inv, hsub, tx, ty, ty_t, potential,
    state, table, low, y_buf, y_own, z_buf, rows, w_buf, bands_part,
    send1, recv1, send2, recv2, send3, recv3, sendh, gath, recvb, sendf, recvf,
    a_cos, a_sin, right1, right2, radius, coef, d_buf, p_buf, g_buf,
    s1, r1, s2, r2, s3, r3, sh, rh, sb, rb, sf, rf, loads,
):
    band = lax.axis_index("band")
    me = lax.axis_index("fft")

    inputs = (
        (basis_in, basis), (tz_in, tz), (angles_in, angles), (columns_in, columns), (tx_in, tx),
        (ty_in, ty), (ty_t_in, ty_t), (inv_in, inv), (hsub_in, hsub), (potential_in, potential),
    )
    copies = [pltpu.make_async_copy(a, b, loads.at[i]) for i, (a, b) in enumerate(inputs)]
    for copy in copies:
        copy.start()

    barrier = pltpu.get_barrier_semaphore()

    def greet(i, carry):
        pl.semaphore_signal(
            barrier, inc=1, device_id=(band, lax.rem(me + i, NFFT)), device_id_type=MESH
        )
        return carry

    lax.fori_loop(1, NFFT, greet, 0)
    for i in range(1, NBAND):
        pl.semaphore_signal(
            barrier, inc=1, device_id=(lax.rem(band + i, NBAND), me), device_id_type=MESH
        )

    def fft_start(send, recv, ssem, rsem, whole):
        def step(i, carry):
            to = lax.rem(me + i, NFFT)
            pltpu.make_async_remote_copy(
                src_ref=send if whole else send.at[to],
                dst_ref=recv.at[me],
                send_sem=ssem,
                recv_sem=rsem,
                device_id=(band, to),
                device_id_type=MESH,
            ).start()
            return carry

        lax.fori_loop(1, NFFT, step, 0)

    def fft_all(send, recv, ssem, rsem, whole):
        part = recv.at[pl.ds(0, NFFT - 1)]
        return pltpu.make_async_remote_copy(
            src_ref=part,
            dst_ref=part,
            send_sem=ssem,
            recv_sem=rsem,
            device_id=(band, lax.rem(me + 1, NFFT)),
            device_id_type=MESH,
        )

    def fft_wait_recv(*args):
        fft_all(*args).wait_recv()

    def fft_wait_send(*args):
        fft_all(*args).wait_send()

    def band_copy(i, src, dst, ssem, rsem):
        to = lax.rem(band + i, NBAND)
        return pltpu.make_async_remote_copy(
            src_ref=src(to),
            dst_ref=dst.at[band],
            send_sem=ssem.at[i],
            recv_sem=rsem.at[band],
            device_id=(to, me),
            device_id_type=MESH,
        )

    def band_arrival(i, src, dst, ssem, rsem):
        source = lax.rem(band + NBAND - i, NBAND)
        return pltpu.make_async_remote_copy(
            src_ref=src(source),
            dst_ref=dst.at[source],
            send_sem=ssem.at[i],
            recv_sem=rsem.at[source],
            device_id=(source, me),
            device_id_type=MESH,
        )

    copies[0].wait()
    copies[1].wait()
    new = basis[2016:2048, :]
    none = jnp.zeros((16, 128), BF16)
    right = jnp.concatenate(
        [
            jnp.concatenate([new[0:16], none], 1),
            jnp.concatenate([none, new[0:16]], 1),
            jnp.concatenate([new[16:32], none], 1),
            jnp.concatenate([none, new[16:32]], 1),
            jnp.zeros((64, 256), BF16),
        ],
        0,
    )
    send1[...] = dot_nt(tz[...], right).reshape(NFFT, 8, 128)
    first = (send1, recv1, s1, r1, False)
    pl.semaphore_wait(barrier, NFFT - 1 + NBAND - 1)
    fft_start(*first)
    recv1[pl.ds(me, 1)] = send1[pl.ds(me, 1)]

    copies[2].wait()
    angle_tables(angles, table)
    rotate_back(me, state, table)

    for i in range(3, 7):
        copies[i].wait()
    position = columns[...].astype(F32)
    pos_x = jnp.floor((position + 0.5) * (1.0 / NG))
    pos_y = position - NG * pos_x
    k_row = lax.broadcasted_iota(jnp.int32, (256, NCOL), 0).astype(F32)
    hot_x = (k_row == pos_x).astype(F32).astype(BF16)
    hot_y = (k_row == pos_y).astype(F32).astype(BF16)
    a_both = dot(tx[...], jnp.concatenate([hot_x, hot_x], 0))
    a_cos[...] = a_both[:NG]
    a_sin[...] = a_both[NG:]
    right2[:, :NCOL] = dot(ty[:, :256], hot_y).astype(BF16)
    right2[:, NCOL:] = dot(ty[:, 256:], hot_y).astype(BF16)
    wide_y = jnp.broadcast_to(pos_y, (128, NCOL)).T
    lane_k = lax.broadcasted_iota(jnp.int32, (NCOL, 128), 1).astype(F32)
    hot_yt = jnp.concatenate(
        [(wide_y == lane_k).astype(F32), (wide_y == lane_k + 128.0).astype(F32)], 1
    ).astype(BF16)
    right1[:NCOL, :] = dot(hot_yt, ty_t[:256, :]).astype(BF16)
    right1[NCOL:, :] = dot(hot_yt, ty_t[256:, :]).astype(BF16)
    freq_x = jnp.where(pos_x < NG // 2, pos_x, pos_x - NG)
    freq_y = jnp.where(pos_y < NG // 2, pos_y, pos_y - NG)
    radius[...] = jnp.broadcast_to(freq_x * freq_x + freq_y * freq_y, (128, NCOL)).T
    g_buf[...] = jnp.zeros_like(g_buf)
    p_buf[...] = jnp.zeros_like(p_buf)

    for i in range(7, 10):
        copies[i].wait()
    couple(band, state, inv, hsub, low, y_buf, y_own, z_buf)
    fft_wait_recv(*first)

    lanes = lax.broadcasted_iota(jnp.int32, (8, 128), 1)
    for q in range(4):
        for j in range(4):
            total = jnp.zeros((8, 128), F32)
            for t in range(8):
                piece = recv1[8 * j + t]
                move = (16 * t - 16 * q) % 128
                if move:
                    piece = pltpu.roll(piece, move, 1)
                total = jnp.where((lanes >> 4) == t, piece, total)
            coef[q, :, 128 * j : 128 * j + 128] = total

    def vector(v, carry):
        for z in range(SLAB):
            c_re = coef[2 * v, z : z + 1, :]
            c_im = coef[2 * v + 1, z : z + 1, :]
            d_buf[NG * z : NG * z + NG, :NCOL] = (a_cos[...] * c_re - a_sin[...] * c_im).astype(BF16)
            d_buf[NG * z : NG * z + NG, NCOL:] = (a_sin[...] * c_re + a_cos[...] * c_im).astype(BF16)
        field = dot(d_buf[...], right1[...])
        for z in range(SLAB):
            v_z = potential[z]
            p_buf[NG * z : NG * z + NG, 0:NG] = (field[NG * z : NG * z + NG, 0:NG] * v_z).astype(BF16)
            p_buf[NG * z : NG * z + NG, 256 : 256 + NG] = (
                field[NG * z : NG * z + NG, 256 : 256 + NG] * v_z
            ).astype(BF16)
        back = dot(p_buf[...], right2[...])
        for z in range(SLAB):
            u_re = back[NG * z : NG * z + NG, :NCOL]
            u_im = back[NG * z : NG * z + NG, NCOL:]
            g_buf[2 * v, z : z + 1, :] = jnp.sum(
                a_cos[...] * u_re + a_sin[...] * u_im, axis=0, keepdims=True
            )
            g_buf[2 * v + 1, z : z + 1, :] = jnp.sum(
                a_cos[...] * u_im - a_sin[...] * u_re, axis=0, keepdims=True
            )
        return carry

    lax.fori_loop(0, 2, vector, 0)

    volume = 1.0 / float(NG) ** 3
    for p in range(NFFT):
        total = jnp.zeros((8, 128), F32)
        for q in range(4):
            piece = g_buf[q, :, 128 * (p // 8) : 128 * (p // 8) + 128]
            move = (16 * q - 16 * (p % 8)) % 128
            if move:
                piece = pltpu.roll(piece, move, 1)
            total = jnp.where((lanes >> 4) == q, piece, total)
        send2[p] = total * volume
    second = (send2, recv2, s2, r2, False)
    fft_start(*second)
    recv2[pl.ds(me, 1)] = send2[pl.ds(me, 1)]

    vector_weights(basis, y_own, w_buf, bands_part)
    bands_args = (lambda to: bands_part.at[to], recvb, sb, rb)
    for i in range(1, NBAND):
        band_copy(i, *bands_args).start()
    recvb[pl.ds(band, 1)] = bands_part[pl.ds(band, 1)]
    rotate_on(state, table, rows)

    fft_wait_recv(*second)
    slabs = recv2[...].reshape(NFFT * 8, 128).T.astype(BF16)
    local = dot(slabs, tz[...])
    slot = lax.broadcasted_iota(jnp.int32, (16, 128), 1) & (NZC - 1)
    freq_z = jnp.where(slot < NZC // 2, slot, slot - NZC).astype(F32)
    own_radius = radius[pl.ds(pl.multiple_of(me * 16, 16), 16), :]
    kinetic = (own_radius + freq_z * freq_z) / (2.0 * (NG // 4) ** 2)
    for v in range(2):
        term = local[32 * v : 32 * v + 16, :128] + local[32 * v + 16 : 32 * v + 32, 128:]
        coeffs = basis[2016 + 16 * v : 2032 + 16 * v, :].astype(F32)
        sendh[16 * v : 16 * v + 16, :] = (kinetic * coeffs + term).astype(BF16)
    gather_args = (lambda to: sendh, gath, sh, rh)
    for i in range(1, NBAND):
        band_copy(i, *gather_args).start()
    gath[pl.ds(band, 1)] = sendh[...].reshape(1, 32, 128)
    hblock_out[...] = sendh[...]

    for i in range(1, NBAND):
        band_arrival(i, *bands_args).wait_recv()
    bands_total = recvb[0].astype(F32)
    for b in range(1, NBAND):
        bands_total = bands_total + recvb[b].astype(F32)
    bands_out[...] = bands_total.astype(BF16)

    for i in range(1, NBAND):
        band_arrival(i, *gather_args).wait_recv()

    pairs = dot_nt(basis[...], gath[...].reshape(128, 128))
    pair_row = lax.broadcasted_iota(jnp.int32, (2048, 128), 0)
    pair_lane = lax.broadcasted_iota(jnp.int32, (2048, 128), 1)
    pairs = jnp.where(((pair_row ^ pair_lane) & 15) == 0, pairs, 0.0)
    by_group = jnp.sum(pairs.reshape(GROUP, 16, 128), axis=1)
    pick_row = lax.broadcasted_iota(jnp.int32, (8, 128), 0)
    pick = (pick_row == (lanes >> 4)).astype(F32)
    send3[...] = dot_nt(pick, by_group, HIGH)
    third = (send3, recv3, s3, r3, True)
    fft_start(*third)
    recv3[pl.ds(me, 1)] = send3[...].reshape(1, 8, 128)
    fft_wait_recv(*third)
    new_columns = recv3[0]
    for p in range(1, NFFT):
        new_columns = new_columns + recv3[p]
    new_columns = new_columns * (1.0 / math.sqrt(2 * NCOL * NZC))
    z_new = dot_nt(y_own[0:32, :], new_columns, HIGH)
    total = rows[0:32, :] + dot(z_new, rows[32:40, :], HIGH)
    sendf[...] = total.reshape(NBAND, 8, ORDER)
    final_args = (lambda to: sendf.at[to], recvf, sf, rf)
    for i in range(1, NBAND):
        band_copy(i, *final_args).start()
    recvf[pl.ds(band, 1)] = sendf[pl.ds(band, 1)]

    fft_wait_send(*first)
    fft_wait_send(*second)
    fft_wait_send(*third)
    for i in range(1, NBAND):
        band_copy(i, *bands_args).wait_send()
        band_copy(i, *gather_args).wait_send()
    for i in range(1, NBAND):
        band_arrival(i, *final_args).wait_recv()
    final = recvf[0] + recvf[1] + recvf[2] + recvf[3]
    rotated_out[...] = final[0:4]
    for i in range(1, NBAND):
        band_copy(i, *final_args).wait_send()


def main_part(*operands):
    vmem = pl.BlockSpec(memory_space=pltpu.VMEM)
    dma = pltpu.SemaphoreType.DMA
    return pl.pallas_call(
        main_kernel,
        out_shape=(
            jax.ShapeDtypeStruct((32, 128), BF16),
            jax.ShapeDtypeStruct((4, ORDER), F32),
            jax.ShapeDtypeStruct((32, 128), BF16),
        ),
        in_specs=[pl.BlockSpec(memory_space=pl.ANY)] * len(operands),
        out_specs=(vmem,) * 3,
        scratch_shapes=[pltpu.VMEM(x.shape, x.dtype) for x in operands]
        + [
            pltpu.VMEM((2, 16, TILE, 128), F32),
            pltpu.VMEM((2, 8 * ROUNDS, TILE, 128), F32),
            pltpu.VMEM((ORDER, ORDER), BF16),
            pltpu.VMEM((128, ORDER), F32),
            pltpu.VMEM((40, GROUP), F32),
            pltpu.VMEM((ORDER, 128), F32),
            pltpu.VMEM((40, ORDER), F32),
            pltpu.VMEM((128, 2048), BF16),
            pltpu.VMEM((NBAND, 32, 128), BF16),
            pltpu.VMEM((NFFT, 8, 128), F32),
            pltpu.VMEM((NFFT, 8, 128), F32),
            pltpu.VMEM((NFFT, 8, 128), F32),
            pltpu.VMEM((NFFT, 8, 128), F32),
            pltpu.VMEM((8, 128), F32),
            pltpu.VMEM((NFFT, 8, 128), F32),
            pltpu.VMEM((32, 128), BF16),
            pltpu.VMEM((NBAND, 32, 128), BF16),
            pltpu.VMEM((NBAND, 32, 128), BF16),
            pltpu.VMEM((NBAND, 8, ORDER), F32),
            pltpu.VMEM((NBAND, 8, ORDER), F32),
            pltpu.VMEM((NG, NCOL), F32),
            pltpu.VMEM((NG, NCOL), F32),
            pltpu.VMEM((2 * NCOL, 512), BF16),
            pltpu.VMEM((512, 2 * NCOL), BF16),
            pltpu.VMEM((NCOL, 128), F32),
            pltpu.VMEM((4, 8, NCOL), F32),
            pltpu.VMEM((SLAB * NG, 2 * NCOL), BF16),
            pltpu.VMEM((SLAB * NG, 512), BF16),
            pltpu.VMEM((4, 8, NCOL), F32),
        ]
        + [dma] * 6
        + [dma((NBAND,))] * 6
        + [dma((len(operands),))],
        compiler_params=pltpu.CompilerParams(
            collective_id=0, has_side_effects=True, vmem_limit_bytes=56 * 2**20
        ),
        name="main_part",
    )(*operands)


def result_kernel(*refs):
    sources, targets, sems = refs[:3], refs[3:6], refs[6]
    copies = [
        pltpu.make_async_copy(a, b, sems.at[i]) for i, (a, b) in enumerate(zip(sources, targets))
    ]
    for copy in copies:
        copy.start()
    for copy in copies:
        copy.wait()


def result_part(*operands):
    anywhere = pl.BlockSpec(memory_space=pl.ANY)
    return pl.pallas_call(
        result_kernel,
        out_shape=tuple(jax.ShapeDtypeStruct(x.shape, x.dtype) for x in operands),
        in_specs=[anywhere] * 3,
        out_specs=(anywhere,) * 3,
        scratch_shapes=[pltpu.SemaphoreType.DMA((3,))],
        compiler_params=pltpu.CompilerParams(vmem_limit_bytes=56 * 2**20),
        name="result_part",
    )(*operands)


def per_device(basis, potential, colmap, hsub_old, inv_factor, angles):
    left = y_table_left()
    results = main_part(
        basis.reshape(2048, 128),
        colmap.reshape(1, NCOL),
        angles.reshape(8 * ROUNDS, TILE),
        jnp.asarray(z_table().astype(BF16)),
        inv_factor,
        hsub_old.T,
        jnp.asarray(x_table()),
        jnp.asarray(left.astype(BF16)),
        jnp.asarray(left.T.astype(BF16)),
        potential,
    )
    hblock, rotated, bands = result_part(*results)
    return (hblock.reshape(2, 16, 128), rotated, bands.reshape(2, 16, 128))


def solution(mesh):
    in_specs = (P("band", "fft", None), P("fft", None, None), P(), P("band", None), P(), P())
    out_specs = (P("band", "fft", None), P(("band", "fft"), None), P("band", "fft", None))
    return jax.shard_map(
        per_device, mesh=mesh, in_specs=in_specs, out_specs=out_specs, check_vma=False
    )
```

```python
import functools
import math

import jax
import jax.numpy as jnp
import numpy as np
from jax import lax
from jax.experimental import pallas as pl
from jax.experimental.pallas import tpu as pltpu
from jax.sharding import PartitionSpec as P

NG = 192
HALF = 96
NZC = 64
ORDER = 512
GROUP = 128
NCOL = 512
NBAND = 4
NFFT = 32
SLAB = 6
ROUNDS = 30
TILE = 32
F32 = jnp.float32
BF16 = jnp.bfloat16
HIGH = lax.Precision.HIGHEST
MESH = pl.DeviceIdType.MESH
NT = (((1,), (1,)), ((), ()))


def dot(a, b, precision=None):
    return jnp.dot(a, b, precision=precision, preferred_element_type=F32)


def dot_nt(a, b, precision=None):
    return lax.dot_general(a, b, NT, precision=precision, preferred_element_type=F32)


def z_table():
    slot = np.arange(NZC)
    freq = np.where(slot < NZC // 2, slot, slot - NZC) % NG
    table = np.zeros((NFFT, 8, 4, NZC), np.float64)
    z = np.arange(NG).reshape(NFFT, SLAB)
    angle = 2.0 * np.pi * ((z[:, :, None] * freq) % NG) / NG
    table[:, :SLAB, 0] = np.cos(angle)
    table[:, :SLAB, 1] = -np.sin(angle)
    table[:, :SLAB, 2] = np.sin(angle)
    table[:, :SLAB, 3] = np.cos(angle)
    return table.reshape(NFFT * 8, 4 * NZC)


def half_angles():
    return 2.0 * np.pi * (((2 * np.arange(HALF)[:, None] + 1) * np.arange(NG)) % (2 * NG)) / (2 * NG)


def x_table():
    angle = half_angles()
    both = np.concatenate([np.cos(angle), np.sin(angle)], 0)
    high = np.asarray(both, np.float32).astype(BF16)
    low = (both - high.astype(np.float64)).astype(BF16)
    table = np.zeros((2 * HALF, 512), BF16)
    table[:, :NG] = high
    table[:, 256 : 256 + NG] = low
    return table


def y_table():
    angle = half_angles().T
    table = np.zeros((256, 256), np.float64)
    table[:NG, :HALF] = np.cos(angle)
    table[:NG, 128 : 128 + HALF] = np.sin(angle)
    return table


def tile_order(turn):
    seat = [0] + [1 + ((m - 1 + turn) % 15) for m in range(1, 16)]
    return seat[:8] + seat[:7:-1]


def pair_step(state, table, r, forward):
    src, dst = state.at[r % 2], state.at[(r + 1) % 2]
    shift = r % TILE
    c = table[0, 8 * r : 8 * r + 8]
    s = table[1, 8 * r : 8 * r + 8]
    a = src[0:8]
    b = src[8:16]
    if shift:
        b = pltpu.roll(b, TILE - shift, 1)
    if forward:
        a, b = c * a - s * b, s * a + c * b
    else:
        a, b = c * a + s * b, c * b - s * a
    if shift:
        b = pltpu.roll(b, shift, 1)
    if forward:
        dst[0:1] = a[0:1]
        dst[1:7] = a[2:8]
        dst[7:8] = b[7:8]
        dst[8:9] = a[1:2]
        dst[9:16] = b[0:7]
    elif r:
        dst[0:1] = a[0:1]
        dst[2:8] = a[1:7]
        dst[15:16] = a[7:8]
        dst[1:2] = b[0:1]
        dst[8:15] = b[1:8]
    else:
        dst[0:8] = a
        dst[8:16] = b


def angle_tables(angles, table):
    ang = jnp.concatenate([angles[...], jnp.zeros((240, 128 - TILE), F32)], 1)
    ang = jnp.concatenate([ang, jnp.zeros((16, 128), F32)], 0)
    for i, part in enumerate((jnp.cos(ang).T[:TILE], jnp.sin(ang).T[:TILE])):
        for q in range(8 * ROUNDS):
            table[i, q] = jnp.broadcast_to(part[:, q : q + 1], (TILE, 128))


def rotate_back(me, state, table):
    row = lax.broadcasted_iota(jnp.int32, (TILE, 128), 0)
    lane = lax.broadcasted_iota(jnp.int32, (TILE, 128), 1)
    target = ((lane >> 3) * NFFT + me) * 4 + (lane & 7)
    target = jnp.where((lane < 32) & ((lane & 7) < 4), target, -1)
    target = jnp.where((lane >= 32) & (lane < 40), lane - 32, target)
    for p, tile in enumerate(tile_order(14)):
        state[1, p] = (row + TILE * tile == target).astype(F32)
    for r in range(ROUNDS - 1, -1, -1):
        pair_step(state, table, r, False)


def natural(state, which):
    return jnp.concatenate([state[which, p] for p in list(range(8)) + list(range(15, 7, -1))], 0)


def couple(band, state, inv, hsub, low, y_buf, y_own, z_buf):
    low[...] = inv[...].astype(BF16)
    y_buf[...] = dot(natural(state, 1).T.astype(BF16), low[...])
    own = y_buf[:, pl.ds(pl.multiple_of(band * GROUP, GROUP), GROUP)]
    y_own[...] = own[:40]
    z_old = dot_nt(hsub[...].astype(BF16), own.astype(BF16))
    lane = lax.broadcasted_iota(jnp.int32, (8, 128), 1)
    row = lax.broadcasted_iota(jnp.int32, (8, 128), 0)
    z_buf[...] = jnp.zeros_like(z_buf)
    for b in range(NBAND):
        z_buf[b * GROUP : b * GROUP + 126, :] = z_old[b * 126 : (b + 1) * 126, :]
    lanes = lax.broadcasted_iota(jnp.int32, (ORDER, 128), 1)
    rows = lax.broadcasted_iota(jnp.int32, (ORDER, 128), 0)
    fresh = ((lanes - 32) >> 1) * GROUP + 126 + (lanes & 1)
    z = jnp.where(lanes < 32, z_buf[...], 0.0)
    z = jnp.where((lanes >= 32) & (lanes < 40) & (rows == fresh), 1.0, z)
    w = dot(low[...], z.astype(BF16))
    for p, tile in enumerate(tile_order(0)):
        state[0, p] = w[TILE * tile : TILE * tile + TILE]


def rotate_on(state, table, rows):
    for r in range(ROUNDS):
        pair_step(state, table, r, True)
    rows[...] = natural(state, 0).T[:40]


def vector_weights(basis, y_own, w_buf, bands_part):
    weights = y_own[32:40, :].astype(BF16)
    spread_row = lax.broadcasted_iota(jnp.int32, (GROUP, 2048), 0)
    spread_lane = lax.broadcasted_iota(jnp.int32, (GROUP, 2048), 1)
    spread = (spread_row == (spread_lane >> 4)).astype(F32).astype(BF16)
    wide = dot(weights, spread)
    own_row = lax.broadcasted_iota(jnp.int32, (16, 2048), 0)
    own_lane = lax.broadcasted_iota(jnp.int32, (16, 2048), 1)
    keep = own_row == (own_lane & 15)
    for k in range(8):
        w_buf[16 * k : 16 * k + 16, :] = jnp.where(keep, wide[k : k + 1], 0.0).astype(BF16)
    bands_part[...] = dot(w_buf[...], basis[...]).astype(BF16).reshape(NBAND, 32, 128)


def split(value):
    high = value.astype(BF16)
    return high, (value - high.astype(F32)).astype(BF16)


def fold_potential(potential, folded):
    y_row = lax.broadcasted_iota(jnp.int32, (NG, 256), 0)
    y_lane = lax.broadcasted_iota(jnp.int32, (NG, 256), 1)
    wanted = jnp.where(y_lane < 128, HALF + y_lane, HALF - 1 + 128 - y_lane)
    wanted = jnp.where((y_lane & 127) < HALF, wanted, -1)
    order_y = (y_row == wanted).astype(F32).astype(BF16)
    x_row = lax.broadcasted_iota(jnp.int32, (HALF, HALF), 0)
    x_lane = lax.broadcasted_iota(jnp.int32, (HALF, HALF), 1)
    order_x = (x_row + x_lane == HALF - 1).astype(F32).astype(BF16)
    high, low = split(potential[...].reshape(SLAB * NG, NG))
    value = dot(high, order_y) + dot(low, order_y)
    for z in range(SLAB):
        high, low = split(value[NG * z : NG * z + HALF])
        low_side = dot(order_x, high) + dot(order_x, low)
        high_side = value[NG * z + HALF : NG * z + NG]
        for v in range(2):
            folded[z, 0, v] = high_side[:, 128 * v : 128 * v + 128]
            folded[z, 1, v] = low_side[:, 128 * v : 128 * v + 128]


def times_potential(q, v):
    (cc, cs), (sc, ss) = q

    def add(m, n):
        return m[0] + n[0], m[1] + n[1]

    def sub(m, n):
        return m[0] - n[0], m[1] - n[1]

    def by_i(m):
        return -m[1], m[0]

    def scaled(m, w):
        return m[0] * w, m[1] * w

    e1, o1 = sub(cc, ss), by_i(add(sc, cs))
    e2, o2 = add(cc, ss), by_i(sub(sc, cs))
    high = scaled(add(e1, o1), v[0][0])
    low = scaled(sub(e1, o1), v[1][1])
    right = scaled(add(e2, o2), v[0][1])
    left = scaled(sub(e2, o2), v[1][0])
    s1, d1, s2, d2 = add(high, low), sub(high, low), add(right, left), sub(right, left)
    odd_x, odd_y = add(d1, d2), sub(d1, d2)
    return (add(s1, s2), (odd_y[1], -odd_y[0])), ((odd_x[1], -odd_x[0]), sub(s2, s1))


def main_kernel(
    basis_in, columns_in, angles_in, tz_in, inv_in, hsub_in, tx_in, ty_in, ty_t_in, potential_in,
    hblock_out, rotated_out, bands_out,
    basis, columns, angles, tz, inv, hsub, tx, ty, ty_t, potential,
    state, table, low, y_buf, y_own, z_buf, rows, w_buf, bands_part,
    send1, recv1, send2, recv2, send3, recv3, sendh, gath, recvb, sendf, recvf,
    a_cos, a_sin, phase, folded, right1, right2, radius, coef, d_buf, p_buf, g_buf,
    s1, r1, s2, r2, s3, r3, sh, rh, sb, rb, sf, rf, loads,
):
    band = lax.axis_index("band")
    me = lax.axis_index("fft")

    inputs = (
        (basis_in, basis), (tz_in, tz), (angles_in, angles), (columns_in, columns), (tx_in, tx),
        (ty_in, ty), (ty_t_in, ty_t), (inv_in, inv), (hsub_in, hsub), (potential_in, potential),
    )
    copies = [pltpu.make_async_copy(a, b, loads.at[i]) for i, (a, b) in enumerate(inputs)]
    for copy in copies:
        copy.start()

    barrier = pltpu.get_barrier_semaphore()

    def greet(i, carry):
        pl.semaphore_signal(
            barrier, inc=1, device_id=(band, lax.rem(me + i, NFFT)), device_id_type=MESH
        )
        return carry

    lax.fori_loop(1, NFFT, greet, 0)
    for i in range(1, NBAND):
        pl.semaphore_signal(
            barrier, inc=1, device_id=(lax.rem(band + i, NBAND), me), device_id_type=MESH
        )

    def fft_start(send, recv, ssem, rsem, whole):
        def step(i, carry):
            to = lax.rem(me + i, NFFT)
            pltpu.make_async_remote_copy(
                src_ref=send if whole else send.at[to],
                dst_ref=recv.at[me],
                send_sem=ssem,
                recv_sem=rsem,
                device_id=(band, to),
                device_id_type=MESH,
            ).start()
            return carry

        lax.fori_loop(1, NFFT, step, 0)

    def fft_all(send, recv, ssem, rsem, whole):
        part = recv.at[pl.ds(0, NFFT - 1)]
        return pltpu.make_async_remote_copy(
            src_ref=part,
            dst_ref=part,
            send_sem=ssem,
            recv_sem=rsem,
            device_id=(band, lax.rem(me + 1, NFFT)),
            device_id_type=MESH,
        )

    def fft_wait_recv(*args):
        fft_all(*args).wait_recv()

    def fft_wait_send(*args):
        fft_all(*args).wait_send()

    def band_copy(i, src, dst, ssem, rsem):
        to = lax.rem(band + i, NBAND)
        return pltpu.make_async_remote_copy(
            src_ref=src(to),
            dst_ref=dst.at[band],
            send_sem=ssem.at[i],
            recv_sem=rsem.at[band],
            device_id=(to, me),
            device_id_type=MESH,
        )

    def band_arrival(i, src, dst, ssem, rsem):
        source = lax.rem(band + NBAND - i, NBAND)
        return pltpu.make_async_remote_copy(
            src_ref=src(source),
            dst_ref=dst.at[source],
            send_sem=ssem.at[i],
            recv_sem=rsem.at[source],
            device_id=(source, me),
            device_id_type=MESH,
        )

    copies[0].wait()
    copies[1].wait()
    new = basis[2016:2048, :]
    none = jnp.zeros((16, 128), BF16)
    right = jnp.concatenate(
        [
            jnp.concatenate([new[0:16], none], 1),
            jnp.concatenate([none, new[0:16]], 1),
            jnp.concatenate([new[16:32], none], 1),
            jnp.concatenate([none, new[16:32]], 1),
            jnp.zeros((64, 256), BF16),
        ],
        0,
    )
    send1[...] = dot_nt(tz[...], right).reshape(NFFT, 8, 128)
    first = (send1, recv1, s1, r1, False)
    pl.semaphore_wait(barrier, NFFT - 1 + NBAND - 1)
    fft_start(*first)
    recv1[pl.ds(me, 1)] = send1[pl.ds(me, 1)]

    copies[2].wait()
    angle_tables(angles, table)
    rotate_back(me, state, table)

    for i in range(3, 7):
        copies[i].wait()
    position = columns[...].astype(F32)
    pos_x = jnp.floor((position + 0.5) * (1.0 / NG))
    pos_y = position - NG * pos_x
    k_row = lax.broadcasted_iota(jnp.int32, (256, NCOL), 0).astype(F32)
    hot_x = (k_row == pos_x).astype(F32).astype(BF16)
    hot_y = (k_row == pos_y).astype(F32).astype(BF16)
    a_both = dot(tx[...], jnp.concatenate([hot_x, hot_x], 0))
    a_cos[...] = a_both[:HALF]
    a_sin[...] = a_both[HALF:]
    right2[...] = dot(ty_t[...], hot_y).astype(BF16)
    wide_y = jnp.broadcast_to(pos_y, (128, NCOL)).T
    lane_k = lax.broadcasted_iota(jnp.int32, (NCOL, 128), 1).astype(F32)
    hot_yt = jnp.concatenate(
        [(wide_y == lane_k).astype(F32), (wide_y == lane_k + 128.0).astype(F32)], 1
    ).astype(BF16)
    right1[...] = dot(hot_yt, ty[...]).astype(BF16)
    turns = (pos_x + pos_y) * (NG - 1.0)
    turns = turns - (2.0 * NG) * jnp.floor((turns + 0.5) * (0.5 / NG))
    center = jnp.broadcast_to(turns * (math.pi / NG), (8, NCOL))
    phase[0] = jnp.cos(center)
    phase[1] = jnp.sin(center)
    freq_x = jnp.where(pos_x < NG // 2, pos_x, pos_x - NG)
    freq_y = jnp.where(pos_y < NG // 2, pos_y, pos_y - NG)
    radius[...] = jnp.broadcast_to(freq_x * freq_x + freq_y * freq_y, (128, NCOL)).T
    g_buf[...] = jnp.zeros_like(g_buf)

    for i in range(7, 10):
        copies[i].wait()
    fold_potential(potential, folded)
    couple(band, state, inv, hsub, low, y_buf, y_own, z_buf)
    fft_wait_recv(*first)

    lanes = lax.broadcasted_iota(jnp.int32, (8, 128), 1)
    for q in range(4):
        for j in range(4):
            total = jnp.zeros((8, 128), F32)
            for t in range(8):
                piece = recv1[8 * j + t]
                move = (16 * t - 16 * q) % 128
                if move:
                    piece = pltpu.roll(piece, move, 1)
                total = jnp.where((lanes >> 4) == t, piece, total)
            coef[q, :, 128 * j : 128 * j + 128] = total

    def vector(v, carry):
        old_re, old_im = coef[2 * v], coef[2 * v + 1]
        all_re = old_re * phase[0] - old_im * phase[1]
        all_im = old_re * phase[1] + old_im * phase[0]
        for z in range(SLAB):
            for a, part in enumerate((a_cos, a_sin)):
                for i, c in enumerate((all_re, all_im)):
                    row = HALF * (4 * z + 2 * a + i)
                    d_buf[row : row + HALF, :] = (part[...] * c[z : z + 1]).astype(BF16)
        field = dot(d_buf[...], right1[...])
        for z in range(SLAB):
            q = []
            for a in range(2):
                rows_a = [field[HALF * (4 * z + 2 * a + i) :][:HALF] for i in range(2)]
                q.append([tuple(x[:, 128 * b : 128 * b + 128] for x in rows_a) for b in range(2)])
            back = times_potential(q, [[folded[z, u, w] for w in range(2)] for u in range(2)])
            for a in range(2):
                for b in range(2):
                    for i in range(2):
                        row = HALF * (4 * z + 2 * a + i)
                        p_buf[row : row + HALF, 128 * b : 128 * b + 128] = back[a][b][i].astype(BF16)
        final = dot(p_buf[...], right2[...])
        for z in range(SLAB):
            for i in range(2):
                even = final[HALF * (4 * z + i) :][:HALF]
                odd = final[HALF * (4 * z + 2 + i) :][:HALF]
                g_buf[2 * v + i, z : z + 1, :] = jnp.sum(
                    a_cos[...] * even + a_sin[...] * odd, axis=0, keepdims=True
                )
        new_re, new_im = g_buf[2 * v], g_buf[2 * v + 1]
        g_buf[2 * v] = new_re * phase[0] + new_im * phase[1]
        g_buf[2 * v + 1] = new_im * phase[0] - new_re * phase[1]
        return carry

    lax.fori_loop(0, 2, vector, 0)

    volume = 1.0 / float(NG) ** 3
    for p in range(NFFT):
        total = jnp.zeros((8, 128), F32)
        for q in range(4):
            piece = g_buf[q, :, 128 * (p // 8) : 128 * (p // 8) + 128]
            move = (16 * q - 16 * (p % 8)) % 128
            if move:
                piece = pltpu.roll(piece, move, 1)
            total = jnp.where((lanes >> 4) == q, piece, total)
        send2[p] = total * volume
    second = (send2, recv2, s2, r2, False)
    fft_start(*second)
    recv2[pl.ds(me, 1)] = send2[pl.ds(me, 1)]

    vector_weights(basis, y_own, w_buf, bands_part)
    bands_args = (lambda to: bands_part.at[to], recvb, sb, rb)
    for i in range(1, NBAND):
        band_copy(i, *bands_args).start()
    recvb[pl.ds(band, 1)] = bands_part[pl.ds(band, 1)]
    rotate_on(state, table, rows)

    fft_wait_recv(*second)
    slabs = recv2[...].reshape(NFFT * 8, 128).T.astype(BF16)
    local = dot(slabs, tz[...])
    slot = lax.broadcasted_iota(jnp.int32, (16, 128), 1) & (NZC - 1)
    freq_z = jnp.where(slot < NZC // 2, slot, slot - NZC).astype(F32)
    own_radius = radius[pl.ds(pl.multiple_of(me * 16, 16), 16), :]
    kinetic = (own_radius + freq_z * freq_z) / (2.0 * (NG // 4) ** 2)
    for v in range(2):
        term = local[32 * v : 32 * v + 16, :128] + local[32 * v + 16 : 32 * v + 32, 128:]
        coeffs = basis[2016 + 16 * v : 2032 + 16 * v, :].astype(F32)
        sendh[16 * v : 16 * v + 16, :] = (kinetic * coeffs + term).astype(BF16)
    gather_args = (lambda to: sendh, gath, sh, rh)
    for i in range(1, NBAND):
        band_copy(i, *gather_args).start()
    gath[pl.ds(band, 1)] = sendh[...].reshape(1, 32, 128)
    hblock_out[...] = sendh[...]

    for i in range(1, NBAND):
        band_arrival(i, *bands_args).wait_recv()
    bands_total = recvb[0].astype(F32)
    for b in range(1, NBAND):
        bands_total = bands_total + recvb[b].astype(F32)
    bands_out[...] = bands_total.astype(BF16)

    for i in range(1, NBAND):
        band_arrival(i, *gather_args).wait_recv()

    pairs = dot_nt(basis[...], gath[...].reshape(128, 128))
    pair_row = lax.broadcasted_iota(jnp.int32, (2048, 128), 0)
    pair_lane = lax.broadcasted_iota(jnp.int32, (2048, 128), 1)
    pairs = jnp.where(((pair_row ^ pair_lane) & 15) == 0, pairs, 0.0)
    by_group = jnp.sum(pairs.reshape(GROUP, 16, 128), axis=1)
    pick_row = lax.broadcasted_iota(jnp.int32, (8, 128), 0)
    pick = (pick_row == (lanes >> 4)).astype(F32)
    send3[...] = dot_nt(pick, by_group, HIGH)
    third = (send3, recv3, s3, r3, True)
    fft_start(*third)
    recv3[pl.ds(me, 1)] = send3[...].reshape(1, 8, 128)
    fft_wait_recv(*third)
    new_columns = recv3[0]
    for p in range(1, NFFT):
        new_columns = new_columns + recv3[p]
    new_columns = new_columns * (1.0 / math.sqrt(2 * NCOL * NZC))
    z_new = dot_nt(y_own[0:32, :], new_columns, HIGH)
    total = rows[0:32, :] + dot(z_new, rows[32:40, :], HIGH)
    sendf[...] = total.reshape(NBAND, 8, ORDER)
    final_args = (lambda to: sendf.at[to], recvf, sf, rf)
    for i in range(1, NBAND):
        band_copy(i, *final_args).start()
    recvf[pl.ds(band, 1)] = sendf[pl.ds(band, 1)]

    fft_wait_send(*first)
    fft_wait_send(*second)
    fft_wait_send(*third)
    for i in range(1, NBAND):
        band_copy(i, *bands_args).wait_send()
        band_copy(i, *gather_args).wait_send()
    for i in range(1, NBAND):
        band_arrival(i, *final_args).wait_recv()
    final = recvf[0] + recvf[1] + recvf[2] + recvf[3]
    rotated_out[...] = final[0:4]
    for i in range(1, NBAND):
        band_copy(i, *final_args).wait_send()


def main_part(*operands):
    vmem = pl.BlockSpec(memory_space=pltpu.VMEM)
    dma = pltpu.SemaphoreType.DMA
    return pl.pallas_call(
        main_kernel,
        out_shape=(
            jax.ShapeDtypeStruct((32, 128), BF16),
            jax.ShapeDtypeStruct((4, ORDER), F32),
            jax.ShapeDtypeStruct((32, 128), BF16),
        ),
        in_specs=[pl.BlockSpec(memory_space=pl.ANY)] * len(operands),
        out_specs=(vmem,) * 3,
        scratch_shapes=[pltpu.VMEM(x.shape, x.dtype) for x in operands]
        + [
            pltpu.VMEM((2, 16, TILE, 128), F32),
            pltpu.VMEM((2, 8 * ROUNDS, TILE, 128), F32),
            pltpu.VMEM((ORDER, ORDER), BF16),
            pltpu.VMEM((128, ORDER), F32),
            pltpu.VMEM((40, GROUP), F32),
            pltpu.VMEM((ORDER, 128), F32),
            pltpu.VMEM((40, ORDER), F32),
            pltpu.VMEM((128, 2048), BF16),
            pltpu.VMEM((NBAND, 32, 128), BF16),
            pltpu.VMEM((NFFT, 8, 128), F32),
            pltpu.VMEM((NFFT, 8, 128), F32),
            pltpu.VMEM((NFFT, 8, 128), F32),
            pltpu.VMEM((NFFT, 8, 128), F32),
            pltpu.VMEM((8, 128), F32),
            pltpu.VMEM((NFFT, 8, 128), F32),
            pltpu.VMEM((32, 128), BF16),
            pltpu.VMEM((NBAND, 32, 128), BF16),
            pltpu.VMEM((NBAND, 32, 128), BF16),
            pltpu.VMEM((NBAND, 8, ORDER), F32),
            pltpu.VMEM((NBAND, 8, ORDER), F32),
            pltpu.VMEM((HALF, NCOL), F32),
            pltpu.VMEM((HALF, NCOL), F32),
            pltpu.VMEM((2, 8, NCOL), F32),
            pltpu.VMEM((SLAB, 2, 2, HALF, 128), F32),
            pltpu.VMEM((NCOL, 256), BF16),
            pltpu.VMEM((256, NCOL), BF16),
            pltpu.VMEM((NCOL, 128), F32),
            pltpu.VMEM((4, 8, NCOL), F32),
            pltpu.VMEM((4 * SLAB * HALF, NCOL), BF16),
            pltpu.VMEM((4 * SLAB * HALF, 256), BF16),
            pltpu.VMEM((4, 8, NCOL), F32),
        ]
        + [dma] * 6
        + [dma((NBAND,))] * 6
        + [dma((len(operands),))],
        compiler_params=pltpu.CompilerParams(
            collective_id=0, has_side_effects=True, vmem_limit_bytes=56 * 2**20
        ),
        name="main_part",
    )(*operands)


def result_kernel(*refs):
    sources, targets, sems = refs[:3], refs[3:6], refs[6]
    copies = [
        pltpu.make_async_copy(a, b, sems.at[i]) for i, (a, b) in enumerate(zip(sources, targets))
    ]
    for copy in copies:
        copy.start()
    for copy in copies:
        copy.wait()


def result_part(*operands):
    anywhere = pl.BlockSpec(memory_space=pl.ANY)
    return pl.pallas_call(
        result_kernel,
        out_shape=tuple(jax.ShapeDtypeStruct(x.shape, x.dtype) for x in operands),
        in_specs=[anywhere] * 3,
        out_specs=(anywhere,) * 3,
        scratch_shapes=[pltpu.SemaphoreType.DMA((3,))],
        compiler_params=pltpu.CompilerParams(vmem_limit_bytes=56 * 2**20),
        name="result_part",
    )(*operands)


def per_device(basis, potential, colmap, hsub_old, inv_factor, angles):
    table = y_table()
    results = main_part(
        basis.reshape(2048, 128),
        colmap.reshape(1, NCOL),
        angles.reshape(8 * ROUNDS, TILE),
        jnp.asarray(z_table().astype(BF16)),
        inv_factor,
        hsub_old.T,
        jnp.asarray(x_table()),
        jnp.asarray(table.astype(BF16)),
        jnp.asarray(table.T.astype(BF16)),
        potential,
    )
    hblock, rotated, bands = result_part(*results)
    return (hblock.reshape(2, 16, 128), rotated, bands.reshape(2, 16, 128))


def solution(mesh):
    in_specs = (P("band", "fft", None), P("fft", None, None), P(), P("band", None), P(), P())
    out_specs = (P("band", "fft", None), P(("band", "fft"), None), P("band", "fft", None))
    return jax.shard_map(
        per_device, mesh=mesh, in_specs=in_specs, out_specs=out_specs, check_vma=False
    )
```

```python
import functools
import math

import jax
import jax.numpy as jnp
import numpy as np
from jax import lax
from jax.experimental import pallas as pl
from jax.experimental.pallas import tpu as pltpu
from jax.sharding import PartitionSpec as P

NG = 192
HALF = 96
NZC = 64
ORDER = 512
GROUP = 128
NCOL = 512
NBAND = 4
NFFT = 32
SLAB = 6
ROUNDS = 30
TILE = 32
F32 = jnp.float32
BF16 = jnp.bfloat16
HIGH = lax.Precision.HIGHEST
MESH = pl.DeviceIdType.MESH
NT = (((1,), (1,)), ((), ()))


def dot(a, b, precision=None):
    return jnp.dot(a, b, precision=precision, preferred_element_type=F32)


def dot_nt(a, b, precision=None):
    return lax.dot_general(a, b, NT, precision=precision, preferred_element_type=F32)


def z_table():
    slot = np.arange(NZC)
    freq = np.where(slot < NZC // 2, slot, slot - NZC) % NG
    table = np.zeros((NFFT, 8, 4, NZC), np.float64)
    z = np.arange(NG).reshape(NFFT, SLAB)
    angle = 2.0 * np.pi * ((z[:, :, None] * freq) % NG) / NG
    table[:, :SLAB, 0] = np.cos(angle)
    table[:, :SLAB, 1] = -np.sin(angle)
    table[:, :SLAB, 2] = np.sin(angle)
    table[:, :SLAB, 3] = np.cos(angle)
    return table.reshape(NFFT * 8, 4 * NZC)


def half_angles():
    return 2.0 * np.pi * (((2 * np.arange(HALF)[:, None] + 1) * np.arange(NG)) % (2 * NG)) / (2 * NG)


def x_table():
    angle = half_angles()
    both = np.concatenate([np.cos(angle), np.sin(angle)], 0)
    high = np.asarray(both, np.float32).astype(BF16)
    low = (both - high.astype(np.float64)).astype(BF16)
    table = np.zeros((2 * HALF, 512), BF16)
    table[:, :NG] = high
    table[:, 256 : 256 + NG] = low
    return table


def y_table():
    angle = half_angles().T
    table = np.zeros((256, 256), np.float64)
    table[:NG, :HALF] = np.cos(angle)
    table[:NG, 128 : 128 + HALF] = np.sin(angle)
    return table


def tile_order(turn):
    seat = [0] + [1 + ((m - 1 + turn) % 15) for m in range(1, 16)]
    return seat[:8] + seat[:7:-1]


def pair_step(state, table, r, forward):
    src, dst = state.at[r % 2], state.at[(r + 1) % 2]
    shift = r % TILE
    c = table[0, 8 * r : 8 * r + 8]
    s = table[1, 8 * r : 8 * r + 8]
    a = src[0:8]
    b = src[8:16]
    if shift:
        b = pltpu.roll(b, TILE - shift, 1)
    if forward:
        a, b = c * a - s * b, s * a + c * b
    else:
        a, b = c * a + s * b, c * b - s * a
    if shift:
        b = pltpu.roll(b, shift, 1)
    if forward:
        dst[0:1] = a[0:1]
        dst[1:7] = a[2:8]
        dst[7:8] = b[7:8]
        dst[8:9] = a[1:2]
        dst[9:16] = b[0:7]
    elif r:
        dst[0:1] = a[0:1]
        dst[2:8] = a[1:7]
        dst[15:16] = a[7:8]
        dst[1:2] = b[0:1]
        dst[8:15] = b[1:8]
    else:
        dst[0:8] = a
        dst[8:16] = b


def angle_tables(angles, table):
    ang = jnp.concatenate([angles[...], jnp.zeros((240, 128 - TILE), F32)], 1)
    ang = jnp.concatenate([ang, jnp.zeros((16, 128), F32)], 0)
    for i, part in enumerate((jnp.cos(ang).T[:TILE], jnp.sin(ang).T[:TILE])):
        for q in range(8 * ROUNDS):
            table[i, q] = jnp.broadcast_to(part[:, q : q + 1], (TILE, 128))


def rotate_back(me, state, table):
    row = lax.broadcasted_iota(jnp.int32, (TILE, 128), 0)
    lane = lax.broadcasted_iota(jnp.int32, (TILE, 128), 1)
    target = ((lane >> 3) * NFFT + me) * 4 + (lane & 7)
    target = jnp.where((lane < 32) & ((lane & 7) < 4), target, -1)
    target = jnp.where((lane >= 32) & (lane < 40), lane - 32, target)
    for p, tile in enumerate(tile_order(14)):
        state[1, p] = (row + TILE * tile == target).astype(F32)
    for r in range(ROUNDS - 1, -1, -1):
        pair_step(state, table, r, False)


def natural(state, which):
    return jnp.concatenate([state[which, p] for p in list(range(8)) + list(range(15, 7, -1))], 0)


def couple(band, state, inv, hsub, low, y_buf, y_own, z_buf):
    low[...] = inv[...].astype(BF16)
    y_buf[...] = dot(natural(state, 1).T.astype(BF16), low[...])
    own = y_buf[:, pl.ds(pl.multiple_of(band * GROUP, GROUP), GROUP)]
    y_own[...] = own[:40]
    z_old = dot_nt(hsub[...].astype(BF16), own.astype(BF16))
    lane = lax.broadcasted_iota(jnp.int32, (8, 128), 1)
    row = lax.broadcasted_iota(jnp.int32, (8, 128), 0)
    z_buf[...] = jnp.zeros_like(z_buf)
    for b in range(NBAND):
        z_buf[b * GROUP : b * GROUP + 126, :] = z_old[b * 126 : (b + 1) * 126, :]
    lanes = lax.broadcasted_iota(jnp.int32, (ORDER, 128), 1)
    rows = lax.broadcasted_iota(jnp.int32, (ORDER, 128), 0)
    fresh = ((lanes - 32) >> 1) * GROUP + 126 + (lanes & 1)
    z = jnp.where(lanes < 32, z_buf[...], 0.0)
    z = jnp.where((lanes >= 32) & (lanes < 40) & (rows == fresh), 1.0, z)
    w = dot(low[...], z.astype(BF16))
    for p, tile in enumerate(tile_order(0)):
        state[0, p] = w[TILE * tile : TILE * tile + TILE]


def rotate_on(state, table, rows):
    for r in range(ROUNDS):
        pair_step(state, table, r, True)
    rows[...] = natural(state, 0).T[:40]


def vector_weights(basis, y_own, w_buf, bands_part):
    weights = y_own[32:40, :].astype(BF16)
    spread_row = lax.broadcasted_iota(jnp.int32, (GROUP, 2048), 0)
    spread_lane = lax.broadcasted_iota(jnp.int32, (GROUP, 2048), 1)
    spread = (spread_row == (spread_lane >> 4)).astype(F32).astype(BF16)
    wide = dot(weights, spread)
    own_row = lax.broadcasted_iota(jnp.int32, (16, 2048), 0)
    own_lane = lax.broadcasted_iota(jnp.int32, (16, 2048), 1)
    keep = own_row == (own_lane & 15)
    for k in range(8):
        w_buf[16 * k : 16 * k + 16, :] = jnp.where(keep, wide[k : k + 1], 0.0).astype(BF16)
    bands_part[...] = dot(w_buf[...], basis[...]).astype(BF16).reshape(NBAND, 32, 128)


def split(value):
    high = value.astype(BF16)
    return high, (value - high.astype(F32)).astype(BF16)


def fold_potential(potential, folded):
    y_row = lax.broadcasted_iota(jnp.int32, (NG, 256), 0)
    y_lane = lax.broadcasted_iota(jnp.int32, (NG, 256), 1)
    wanted = jnp.where(y_lane < 128, HALF + y_lane, HALF - 1 + 128 - y_lane)
    wanted = jnp.where((y_lane & 127) < HALF, wanted, -1)
    order_y = (y_row == wanted).astype(F32).astype(BF16)
    x_row = lax.broadcasted_iota(jnp.int32, (HALF, HALF), 0)
    x_lane = lax.broadcasted_iota(jnp.int32, (HALF, HALF), 1)
    order_x = (x_row + x_lane == HALF - 1).astype(F32).astype(BF16)
    high, low = split(potential[...].reshape(SLAB * NG, NG))
    value = dot(high, order_y) + dot(low, order_y)
    for z in range(SLAB):
        high, low = split(value[NG * z : NG * z + HALF])
        low_side = dot(order_x, high) + dot(order_x, low)
        high_side = value[NG * z + HALF : NG * z + NG]
        for v in range(2):
            folded[z, 0, v] = high_side[:, 128 * v : 128 * v + 128]
            folded[z, 1, v] = low_side[:, 128 * v : 128 * v + 128]


def times_potential(q, v):
    (cc, cs), (sc, ss) = q

    def add(m, n):
        return m[0] + n[0], m[1] + n[1]

    def sub(m, n):
        return m[0] - n[0], m[1] - n[1]

    def by_i(m):
        return -m[1], m[0]

    def scaled(m, w):
        return m[0] * w, m[1] * w

    e1, o1 = sub(cc, ss), by_i(add(sc, cs))
    e2, o2 = add(cc, ss), by_i(sub(sc, cs))
    high = scaled(add(e1, o1), v[0][0])
    low = scaled(sub(e1, o1), v[1][1])
    right = scaled(add(e2, o2), v[0][1])
    left = scaled(sub(e2, o2), v[1][0])
    s1, d1, s2, d2 = add(high, low), sub(high, low), add(right, left), sub(right, left)
    odd_x, odd_y = add(d1, d2), sub(d1, d2)
    return (add(s1, s2), (odd_y[1], -odd_y[0])), ((odd_x[1], -odd_x[0]), sub(s2, s1))


def main_kernel(
    basis_in, columns_in, angles_in, tz_in, inv_in, hsub_in, tx_in, ty_in, ty_t_in, potential_in,
    hblock_out, rotated_out, bands_out,
    basis, columns, angles, tz, inv, hsub, tx, ty, ty_t, potential,
    state, table, low, y_buf, y_own, z_buf, rows, w_buf, bands_part,
    send1, recv1, send2, recv2, send3, recv3, sendh, gath, recvb, sendf, recvf,
    q_buf, u_buf, a_cos, a_sin, phase, folded, right1, right2, radius, coef, d_buf, p_buf, g_buf,
    s1, r1, s2, r2, s3, r3, sh, rh, sb, rb, sf, rf, loads,
):
    band = lax.axis_index("band")
    me = lax.axis_index("fft")

    inputs = (
        (basis_in, basis), (tz_in, tz), (angles_in, angles), (columns_in, columns), (tx_in, tx),
        (ty_in, ty), (ty_t_in, ty_t), (inv_in, inv), (hsub_in, hsub), (potential_in, potential),
    )
    copies = [pltpu.make_async_copy(a, b, loads.at[i]) for i, (a, b) in enumerate(inputs)]
    for copy in copies:
        copy.start()

    barrier = pltpu.get_barrier_semaphore()

    def greet(i, carry):
        pl.semaphore_signal(
            barrier, inc=1, device_id=(band, lax.rem(me + i, NFFT)), device_id_type=MESH
        )
        return carry

    lax.fori_loop(1, NFFT, greet, 0)
    for i in range(1, NBAND):
        pl.semaphore_signal(
            barrier, inc=1, device_id=(lax.rem(band + i, NBAND), me), device_id_type=MESH
        )

    def fft_start(send, recv, ssem, rsem, whole):
        def step(i, carry):
            to = lax.rem(me + i, NFFT)
            pltpu.make_async_remote_copy(
                src_ref=send if whole else send.at[to],
                dst_ref=recv.at[me],
                send_sem=ssem,
                recv_sem=rsem,
                device_id=(band, to),
                device_id_type=MESH,
            ).start()
            return carry

        lax.fori_loop(1, NFFT, step, 0)

    def fft_all(send, recv, ssem, rsem, whole):
        part = recv.at[pl.ds(0, NFFT - 1)]
        return pltpu.make_async_remote_copy(
            src_ref=part,
            dst_ref=part,
            send_sem=ssem,
            recv_sem=rsem,
            device_id=(band, lax.rem(me + 1, NFFT)),
            device_id_type=MESH,
        )

    def fft_wait_recv(*args):
        fft_all(*args).wait_recv()

    def fft_wait_send(*args):
        fft_all(*args).wait_send()

    def band_copy(i, src, dst, ssem, rsem):
        to = lax.rem(band + i, NBAND)
        return pltpu.make_async_remote_copy(
            src_ref=src(to),
            dst_ref=dst.at[band],
            send_sem=ssem.at[i],
            recv_sem=rsem.at[band],
            device_id=(to, me),
            device_id_type=MESH,
        )

    def band_arrival(i, src, dst, ssem, rsem):
        source = lax.rem(band + NBAND - i, NBAND)
        return pltpu.make_async_remote_copy(
            src_ref=src(source),
            dst_ref=dst.at[source],
            send_sem=ssem.at[i],
            recv_sem=rsem.at[source],
            device_id=(source, me),
            device_id_type=MESH,
        )

    copies[0].wait()
    copies[1].wait()
    new = basis[2016:2048, :]
    none = jnp.zeros((16, 128), BF16)
    right = jnp.concatenate(
        [
            jnp.concatenate([new[0:16], none], 1),
            jnp.concatenate([none, new[0:16]], 1),
            jnp.concatenate([new[16:32], none], 1),
            jnp.concatenate([none, new[16:32]], 1),
            jnp.zeros((64, 256), BF16),
        ],
        0,
    )
    send1[...] = dot_nt(tz[...], right).reshape(NFFT, 8, 128)
    first = (send1, recv1, s1, r1, False)
    pl.semaphore_wait(barrier, NFFT - 1 + NBAND - 1)
    fft_start(*first)
    recv1[pl.ds(me, 1)] = send1[pl.ds(me, 1)]

    copies[2].wait()
    angle_tables(angles, table)

    for i in range(3, 7):
        copies[i].wait()
    position = columns[...].astype(F32)
    pos_x = jnp.floor((position + 0.5) * (1.0 / NG))
    pos_y = position - NG * pos_x
    k_row = lax.broadcasted_iota(jnp.int32, (256, NCOL), 0).astype(F32)
    hot_x = (k_row == pos_x).astype(F32).astype(BF16)
    hot_y = (k_row == pos_y).astype(F32).astype(BF16)
    a_both = dot(tx[...], jnp.concatenate([hot_x, hot_x], 0))
    a_cos[...] = a_both[:HALF]
    a_sin[...] = a_both[HALF:]
    right2[...] = dot(ty_t[...], hot_y).astype(BF16)
    wide_y = jnp.broadcast_to(pos_y, (128, NCOL)).T
    lane_k = lax.broadcasted_iota(jnp.int32, (NCOL, 128), 1).astype(F32)
    hot_yt = jnp.concatenate(
        [(wide_y == lane_k).astype(F32), (wide_y == lane_k + 128.0).astype(F32)], 1
    ).astype(BF16)
    right1[...] = dot(hot_yt, ty[...]).astype(BF16)
    turns = (pos_x + pos_y) * (NG - 1.0)
    turns = turns - (2.0 * NG) * jnp.floor((turns + 0.5) * (0.5 / NG))
    center = jnp.broadcast_to(turns * (math.pi / NG), (8, NCOL))
    phase[0] = jnp.cos(center)
    phase[1] = jnp.sin(center)
    freq_x = jnp.where(pos_x < NG // 2, pos_x, pos_x - NG)
    freq_y = jnp.where(pos_y < NG // 2, pos_y, pos_y - NG)
    radius[...] = jnp.broadcast_to(freq_x * freq_x + freq_y * freq_y, (128, NCOL)).T
    g_buf[...] = jnp.zeros_like(g_buf)

    for i in range(7, 10):
        copies[i].wait()
    fold_potential(potential, folded)
    fft_wait_recv(*first)

    lanes = lax.broadcasted_iota(jnp.int32, (8, 128), 1)
    for q in range(4):
        for j in range(4):
            total = jnp.zeros((8, 128), F32)
            for t in range(8):
                piece = recv1[8 * j + t]
                move = (16 * t - 16 * q) % 128
                if move:
                    piece = pltpu.roll(piece, move, 1)
                total = jnp.where((lanes >> 4) == t, piece, total)
            coef[q, :, 128 * j : 128 * j + 128] = total

    def mix(v):
        old_re, old_im = coef[2 * v], coef[2 * v + 1]
        coef[2 * v] = old_re * phase[0] - old_im * phase[1]
        coef[2 * v + 1] = old_re * phase[1] + old_im * phase[0]

    def unmix(v):
        new_re, new_im = g_buf[2 * v], g_buf[2 * v + 1]
        g_buf[2 * v] = new_re * phase[0] + new_im * phase[1]
        g_buf[2 * v + 1] = new_im * phase[0] - new_re * phase[1]

    def block(z, a, i):
        return pl.ds(HALF * (4 * z + 2 * a + i), HALF)

    def plane(z):
        return pl.ds(4 * HALF * z, 4 * HALF)

    def spread(v, z):
        for a, part in enumerate((a_cos, a_sin)):
            for i in range(2):
                d_buf[block(z, a, i), :] = (part[...] * coef[2 * v + i, z : z + 1, :]).astype(BF16)

    def to_field(v, z):
        q_buf[plane(z), :] = dot(d_buf[plane(z), :], right1[...])

    def multiply(v, z):
        q = [
            [tuple(q_buf[block(z, a, i), 128 * b : 128 * b + 128] for i in range(2)) for b in range(2)]
            for a in range(2)
        ]
        back = times_potential(q, [[folded[z, u, w] for w in range(2)] for u in range(2)])
        for a in range(2):
            for b in range(2):
                for i in range(2):
                    p_buf[block(z, a, i), 128 * b : 128 * b + 128] = back[a][b][i].astype(BF16)

    def from_field(v, z):
        u_buf[plane(z), :] = dot(p_buf[plane(z), :], right2[...])

    def collect(v, z):
        for i in range(2):
            g_buf[2 * v + i, z : z + 1, :] = jnp.sum(
                a_cos[...] * u_buf[block(z, 0, i), :] + a_sin[...] * u_buf[block(z, 1, i), :],
                axis=0,
                keepdims=True,
            )

    steps = (spread, to_field, multiply, from_field, collect)

    for v in range(2):
        mix(v)
    for t in range(2 * SLAB + len(steps) - 1):
        for s, step in enumerate(steps):
            if 0 <= t - s < 2 * SLAB:
                step((t - s) // SLAB, (t - s) % SLAB)
    for v in range(2):
        unmix(v)

    volume = 1.0 / float(NG) ** 3
    for p in range(NFFT):
        total = jnp.zeros((8, 128), F32)
        for q in range(4):
            piece = g_buf[q, :, 128 * (p // 8) : 128 * (p // 8) + 128]
            move = (16 * q - 16 * (p % 8)) % 128
            if move:
                piece = pltpu.roll(piece, move, 1)
            total = jnp.where((lanes >> 4) == q, piece, total)
        send2[p] = total * volume
    second = (send2, recv2, s2, r2, False)
    fft_start(*second)
    recv2[pl.ds(me, 1)] = send2[pl.ds(me, 1)]

    rotate_back(me, state, table)
    couple(band, state, inv, hsub, low, y_buf, y_own, z_buf)

    fft_wait_recv(*second)
    slabs = recv2[...].reshape(NFFT * 8, 128).T.astype(BF16)
    local = dot(slabs, tz[...])
    slot = lax.broadcasted_iota(jnp.int32, (16, 128), 1) & (NZC - 1)
    freq_z = jnp.where(slot < NZC // 2, slot, slot - NZC).astype(F32)
    own_radius = radius[pl.ds(pl.multiple_of(me * 16, 16), 16), :]
    kinetic = (own_radius + freq_z * freq_z) / (2.0 * (NG // 4) ** 2)
    for v in range(2):
        term = local[32 * v : 32 * v + 16, :128] + local[32 * v + 16 : 32 * v + 32, 128:]
        coeffs = basis[2016 + 16 * v : 2032 + 16 * v, :].astype(F32)
        sendh[16 * v : 16 * v + 16, :] = (kinetic * coeffs + term).astype(BF16)
    gather_args = (lambda to: sendh, gath, sh, rh)
    for i in range(1, NBAND):
        band_copy(i, *gather_args).start()
    gath[pl.ds(band, 1)] = sendh[...].reshape(1, 32, 128)
    hblock_out[...] = sendh[...]

    vector_weights(basis, y_own, w_buf, bands_part)
    bands_args = (lambda to: bands_part.at[to], recvb, sb, rb)
    for i in range(1, NBAND):
        band_copy(i, *bands_args).start()
    recvb[pl.ds(band, 1)] = bands_part[pl.ds(band, 1)]

    for i in range(1, NBAND):
        band_arrival(i, *gather_args).wait_recv()

    pairs = dot_nt(basis[...], gath[...].reshape(128, 128))
    pair_row = lax.broadcasted_iota(jnp.int32, (2048, 128), 0)
    pair_lane = lax.broadcasted_iota(jnp.int32, (2048, 128), 1)
    pairs = jnp.where(((pair_row ^ pair_lane) & 15) == 0, pairs, 0.0)
    by_group = jnp.sum(pairs.reshape(GROUP, 16, 128), axis=1)
    pick_row = lax.broadcasted_iota(jnp.int32, (8, 128), 0)
    pick = (pick_row == (lanes >> 4)).astype(F32)
    send3[...] = dot_nt(pick, by_group, HIGH)
    third = (send3, recv3, s3, r3, True)
    fft_start(*third)
    recv3[pl.ds(me, 1)] = send3[...].reshape(1, 8, 128)
    rotate_on(state, table, rows)
    for i in range(1, NBAND):
        band_arrival(i, *bands_args).wait_recv()
    bands_total = recvb[0].astype(F32)
    for b in range(1, NBAND):
        bands_total = bands_total + recvb[b].astype(F32)
    bands_out[...] = bands_total.astype(BF16)
    fft_wait_recv(*third)
    new_columns = recv3[0]
    for p in range(1, NFFT):
        new_columns = new_columns + recv3[p]
    new_columns = new_columns * (1.0 / math.sqrt(2 * NCOL * NZC))
    z_new = dot_nt(y_own[0:32, :], new_columns, HIGH)
    total = rows[0:32, :] + dot(z_new, rows[32:40, :], HIGH)
    sendf[...] = total.reshape(NBAND, 8, ORDER)
    final_args = (lambda to: sendf.at[to], recvf, sf, rf)
    for i in range(1, NBAND):
        band_copy(i, *final_args).start()
    recvf[pl.ds(band, 1)] = sendf[pl.ds(band, 1)]

    fft_wait_send(*first)
    fft_wait_send(*second)
    fft_wait_send(*third)
    for i in range(1, NBAND):
        band_copy(i, *bands_args).wait_send()
        band_copy(i, *gather_args).wait_send()
    for i in range(1, NBAND):
        band_arrival(i, *final_args).wait_recv()
    final = recvf[0] + recvf[1] + recvf[2] + recvf[3]
    rotated_out[...] = final[0:4]
    for i in range(1, NBAND):
        band_copy(i, *final_args).wait_send()


def main_part(*operands):
    vmem = pl.BlockSpec(memory_space=pltpu.VMEM)
    dma = pltpu.SemaphoreType.DMA
    return pl.pallas_call(
        main_kernel,
        out_shape=(
            jax.ShapeDtypeStruct((32, 128), BF16),
            jax.ShapeDtypeStruct((4, ORDER), F32),
            jax.ShapeDtypeStruct((32, 128), BF16),
        ),
        in_specs=[pl.BlockSpec(memory_space=pl.ANY)] * len(operands),
        out_specs=(vmem,) * 3,
        scratch_shapes=[pltpu.VMEM(x.shape, x.dtype) for x in operands]
        + [
            pltpu.VMEM((2, 16, TILE, 128), F32),
            pltpu.VMEM((2, 8 * ROUNDS, TILE, 128), F32),
            pltpu.VMEM((ORDER, ORDER), BF16),
            pltpu.VMEM((128, ORDER), F32),
            pltpu.VMEM((40, GROUP), F32),
            pltpu.VMEM((ORDER, 128), F32),
            pltpu.VMEM((40, ORDER), F32),
            pltpu.VMEM((128, 2048), BF16),
            pltpu.VMEM((NBAND, 32, 128), BF16),
            pltpu.VMEM((NFFT, 8, 128), F32),
            pltpu.VMEM((NFFT, 8, 128), F32),
            pltpu.VMEM((NFFT, 8, 128), F32),
            pltpu.VMEM((NFFT, 8, 128), F32),
            pltpu.VMEM((8, 128), F32),
            pltpu.VMEM((NFFT, 8, 128), F32),
            pltpu.VMEM((32, 128), BF16),
            pltpu.VMEM((NBAND, 32, 128), BF16),
            pltpu.VMEM((NBAND, 32, 128), BF16),
            pltpu.VMEM((NBAND, 8, ORDER), F32),
            pltpu.VMEM((NBAND, 8, ORDER), F32),
            pltpu.VMEM((4 * SLAB * HALF, 256), F32),
            pltpu.VMEM((4 * SLAB * HALF, NCOL), F32),
            pltpu.VMEM((HALF, NCOL), F32),
            pltpu.VMEM((HALF, NCOL), F32),
            pltpu.VMEM((2, 8, NCOL), F32),
            pltpu.VMEM((SLAB, 2, 2, HALF, 128), F32),
            pltpu.VMEM((NCOL, 256), BF16),
            pltpu.VMEM((256, NCOL), BF16),
            pltpu.VMEM((NCOL, 128), F32),
            pltpu.VMEM((4, 8, NCOL), F32),
            pltpu.VMEM((4 * SLAB * HALF, NCOL), BF16),
            pltpu.VMEM((4 * SLAB * HALF, 256), BF16),
            pltpu.VMEM((4, 8, NCOL), F32),
        ]
        + [dma] * 6
        + [dma((NBAND,))] * 6
        + [dma((len(operands),))],
        compiler_params=pltpu.CompilerParams(
            collective_id=0, has_side_effects=True, vmem_limit_bytes=56 * 2**20
        ),
        name="main_part",
    )(*operands)


def result_kernel(*refs):
    sources, targets, sems = refs[:3], refs[3:6], refs[6]
    copies = [
        pltpu.make_async_copy(a, b, sems.at[i]) for i, (a, b) in enumerate(zip(sources, targets))
    ]
    for copy in copies:
        copy.start()
    for copy in copies:
        copy.wait()


def result_part(*operands):
    anywhere = pl.BlockSpec(memory_space=pl.ANY)
    return pl.pallas_call(
        result_kernel,
        out_shape=tuple(jax.ShapeDtypeStruct(x.shape, x.dtype) for x in operands),
        in_specs=[anywhere] * 3,
        out_specs=(anywhere,) * 3,
        scratch_shapes=[pltpu.SemaphoreType.DMA((3,))],
        compiler_params=pltpu.CompilerParams(vmem_limit_bytes=56 * 2**20),
        name="result_part",
    )(*operands)


def per_device(basis, potential, colmap, hsub_old, inv_factor, angles):
    table = y_table()
    results = main_part(
        basis.reshape(2048, 128),
        colmap.reshape(1, NCOL),
        angles.reshape(8 * ROUNDS, TILE),
        jnp.asarray(z_table().astype(BF16)),
        inv_factor,
        hsub_old.T,
        jnp.asarray(x_table()),
        jnp.asarray(table.astype(BF16)),
        jnp.asarray(table.T.astype(BF16)),
        potential,
    )
    hblock, rotated, bands = result_part(*results)
    return (hblock.reshape(2, 16, 128), rotated, bands.reshape(2, 16, 128))


def solution(mesh):
    in_specs = (P("band", "fft", None), P("fft", None, None), P(), P("band", None), P(), P())
    out_specs = (P("band", "fft", None), P(("band", "fft"), None), P("band", "fft", None))
    return jax.shard_map(
        per_device, mesh=mesh, in_specs=in_specs, out_specs=out_specs, check_vma=False
    )
```

```python
import functools
import math

import jax
import jax.numpy as jnp
import numpy as np
from jax import lax
from jax.experimental import pallas as pl
from jax.experimental.pallas import tpu as pltpu
from jax.sharding import PartitionSpec as P

NG = 192
HALF = 96
NZC = 64
ORDER = 512
GROUP = 128
NCOL = 512
NBAND = 4
NFFT = 32
SLAB = 6
ROUNDS = 30
TILE = 32
F32 = jnp.float32
BF16 = jnp.bfloat16
HIGH = lax.Precision.HIGHEST
MESH = pl.DeviceIdType.MESH
NT = (((1,), (1,)), ((), ()))


def dot(a, b, precision=None):
    return jnp.dot(a, b, precision=precision, preferred_element_type=F32)


def dot_nt(a, b, precision=None):
    return lax.dot_general(a, b, NT, precision=precision, preferred_element_type=F32)


def z_table():
    slot = np.arange(NZC)
    freq = np.where(slot < NZC // 2, slot, slot - NZC) % NG
    table = np.zeros((NFFT, 8, 4, NZC), np.float64)
    z = np.arange(NG).reshape(NFFT, SLAB)
    angle = 2.0 * np.pi * ((z[:, :, None] * freq) % NG) / NG
    table[:, :SLAB, 0] = np.cos(angle)
    table[:, :SLAB, 1] = -np.sin(angle)
    table[:, :SLAB, 2] = np.sin(angle)
    table[:, :SLAB, 3] = np.cos(angle)
    return table.reshape(NFFT * 8, 4 * NZC)


def z_table_back():
    table = z_table().reshape(NFFT, 4, 2, 4 * NZC)
    return np.transpose(table, (1, 0, 2, 3)).reshape(4 * NFFT, 8 * NZC)


def half_angles():
    return 2.0 * np.pi * (((2 * np.arange(HALF)[:, None] + 1) * np.arange(NG)) % (2 * NG)) / (2 * NG)


def x_table():
    angle = half_angles()
    both = np.concatenate([np.cos(angle), np.sin(angle)], 0)
    high = np.asarray(both, np.float32).astype(BF16)
    low = (both - high.astype(np.float64)).astype(BF16)
    table = np.zeros((2 * HALF, 512), BF16)
    table[:, :NG] = high
    table[:, 256 : 256 + NG] = low
    return table


def y_table():
    angle = half_angles().T
    table = np.zeros((256, 256), np.float64)
    table[:NG, :HALF] = np.cos(angle)
    table[:NG, 128 : 128 + HALF] = np.sin(angle)
    return table


def tile_order(turn):
    seat = [0] + [1 + ((m - 1 + turn) % 15) for m in range(1, 16)]
    return seat[:8] + seat[:7:-1]


def pair_step(state, table, r, forward):
    src, dst = state.at[r % 2], state.at[(r + 1) % 2]
    shift = r % TILE
    c = table[0, 8 * r : 8 * r + 8]
    s = table[1, 8 * r : 8 * r + 8]
    a = src[0:8]
    b = src[8:16]
    if shift:
        b = pltpu.roll(b, TILE - shift, 1)
    if forward:
        a, b = c * a - s * b, s * a + c * b
    else:
        a, b = c * a + s * b, c * b - s * a
    if shift:
        b = pltpu.roll(b, shift, 1)
    if forward:
        dst[0:1] = a[0:1]
        dst[1:7] = a[2:8]
        dst[7:8] = b[7:8]
        dst[8:9] = a[1:2]
        dst[9:16] = b[0:7]
    elif r:
        dst[0:1] = a[0:1]
        dst[2:8] = a[1:7]
        dst[15:16] = a[7:8]
        dst[1:2] = b[0:1]
        dst[8:15] = b[1:8]
    else:
        dst[0:8] = a
        dst[8:16] = b


def angle_tables(angles, table):
    ang = jnp.concatenate([angles[...], jnp.zeros((240, 128 - TILE), F32)], 1)
    ang = jnp.concatenate([ang, jnp.zeros((16, 128), F32)], 0)
    for i, part in enumerate((jnp.cos(ang).T[:TILE], jnp.sin(ang).T[:TILE])):
        for q in range(8 * ROUNDS):
            table[i, q] = jnp.broadcast_to(part[:, q : q + 1], (TILE, 128))


def rotate_back(me, state, table):
    row = lax.broadcasted_iota(jnp.int32, (TILE, 128), 0)
    lane = lax.broadcasted_iota(jnp.int32, (TILE, 128), 1)
    target = ((lane >> 3) * NFFT + me) * 4 + (lane & 7)
    target = jnp.where((lane < 32) & ((lane & 7) < 4), target, -1)
    target = jnp.where((lane >= 32) & (lane < 40), lane - 32, target)
    for p, tile in enumerate(tile_order(14)):
        state[1, p] = (row + TILE * tile == target).astype(F32)
    for r in range(ROUNDS - 1, -1, -1):
        pair_step(state, table, r, False)


def natural(state, which):
    return jnp.concatenate([state[which, p] for p in list(range(8)) + list(range(15, 7, -1))], 0)


def couple(band, state, inv, hsub, low, y_buf, y_own, z_buf):
    low[...] = inv[...].astype(BF16)
    y_buf[...] = dot(natural(state, 1).T.astype(BF16), low[...])
    own = y_buf[:, pl.ds(pl.multiple_of(band * GROUP, GROUP), GROUP)]
    y_own[...] = own[:40]
    z_old = dot_nt(hsub[...].astype(BF16), own.astype(BF16))
    lane = lax.broadcasted_iota(jnp.int32, (8, 128), 1)
    row = lax.broadcasted_iota(jnp.int32, (8, 128), 0)
    z_buf[...] = jnp.zeros_like(z_buf)
    for b in range(NBAND):
        z_buf[b * GROUP : b * GROUP + 126, :] = z_old[b * 126 : (b + 1) * 126, :]
    lanes = lax.broadcasted_iota(jnp.int32, (ORDER, 128), 1)
    rows = lax.broadcasted_iota(jnp.int32, (ORDER, 128), 0)
    fresh = ((lanes - 32) >> 1) * GROUP + 126 + (lanes & 1)
    z = jnp.where(lanes < 32, z_buf[...], 0.0)
    z = jnp.where((lanes >= 32) & (lanes < 40) & (rows == fresh), 1.0, z)
    w = dot(low[...], z.astype(BF16))
    for p, tile in enumerate(tile_order(0)):
        state[0, p] = w[TILE * tile : TILE * tile + TILE]


def rotate_on(state, table, rows):
    for r in range(ROUNDS):
        pair_step(state, table, r, True)
    rows[...] = natural(state, 0).T[:40]


def vector_weights(basis, y_own, w_buf, bands_part):
    weights = y_own[32:40, :].astype(BF16)
    spread_row = lax.broadcasted_iota(jnp.int32, (GROUP, 2048), 0)
    spread_lane = lax.broadcasted_iota(jnp.int32, (GROUP, 2048), 1)
    spread = (spread_row == (spread_lane >> 4)).astype(F32).astype(BF16)
    wide = dot(weights, spread)
    own_row = lax.broadcasted_iota(jnp.int32, (16, 2048), 0)
    own_lane = lax.broadcasted_iota(jnp.int32, (16, 2048), 1)
    keep = own_row == (own_lane & 15)
    for k in range(8):
        w_buf[16 * k : 16 * k + 16, :] = jnp.where(keep, wide[k : k + 1], 0.0).astype(BF16)
    bands_part[...] = dot(w_buf[...], basis[...]).astype(BF16).reshape(NBAND, 32, 128)


def split(value):
    high = value.astype(BF16)
    return high, (value - high.astype(F32)).astype(BF16)


def fold_potential(potential, folded):
    y_row = lax.broadcasted_iota(jnp.int32, (NG, 256), 0)
    y_lane = lax.broadcasted_iota(jnp.int32, (NG, 256), 1)
    wanted = jnp.where(y_lane < 128, HALF + y_lane, HALF - 1 + 128 - y_lane)
    wanted = jnp.where((y_lane & 127) < HALF, wanted, -1)
    order_y = (y_row == wanted).astype(F32).astype(BF16)
    x_row = lax.broadcasted_iota(jnp.int32, (HALF, HALF), 0)
    x_lane = lax.broadcasted_iota(jnp.int32, (HALF, HALF), 1)
    order_x = (x_row + x_lane == HALF - 1).astype(F32).astype(BF16)
    high, low = split(potential[...].reshape(SLAB * NG, NG))
    value = dot(high, order_y) + dot(low, order_y)
    for z in range(SLAB):
        high, low = split(value[NG * z : NG * z + HALF])
        low_side = dot(order_x, high) + dot(order_x, low)
        high_side = value[NG * z + HALF : NG * z + NG]
        for v in range(2):
            folded[z, 0, v] = high_side[:, 128 * v : 128 * v + 128]
            folded[z, 1, v] = low_side[:, 128 * v : 128 * v + 128]


def times_potential(q, v):
    (cc, cs), (sc, ss) = q

    def add(m, n):
        return m[0] + n[0], m[1] + n[1]

    def sub(m, n):
        return m[0] - n[0], m[1] - n[1]

    def by_i(m):
        return -m[1], m[0]

    def scaled(m, w):
        return m[0] * w, m[1] * w

    e1, o1 = sub(cc, ss), by_i(add(sc, cs))
    e2, o2 = add(cc, ss), by_i(sub(sc, cs))
    high = scaled(add(e1, o1), v[0][0])
    low = scaled(sub(e1, o1), v[1][1])
    right = scaled(add(e2, o2), v[0][1])
    left = scaled(sub(e2, o2), v[1][0])
    s1, d1, s2, d2 = add(high, low), sub(high, low), add(right, left), sub(right, left)
    odd_x, odd_y = add(d1, d2), sub(d1, d2)
    return (add(s1, s2), (odd_y[1], -odd_y[0])), ((odd_x[1], -odd_x[0]), sub(s2, s1))


def main_kernel(
    basis_in, columns_in, angles_in, tz_in, inv_in, hsub_in, tx_in, ty_in, ty_t_in, potential_in, tb_in,
    hblock_out, rotated_out, bands_out,
    basis, columns, angles, tz, inv, hsub, tx, ty, ty_t, potential, tb,
    state, table, low, y_buf, y_own, z_buf, rows, w_buf, bands_part,
    send1, recv1, send2, recv2, send3, recv3, new_own, news, hall, recvb, sendf, recvf,
    q_buf, u_buf, a_cos, a_sin, phase, phase_out, folded, right1, right2, radius, coef, d_buf, p_buf, g_buf,
    s1, r1, s2, r2, s3, r3, sh, rh, sb, rb, sf, rf, loads,
):
    band = lax.axis_index("band")
    me = lax.axis_index("fft")

    inputs = (
        (basis_in, basis), (tz_in, tz), (angles_in, angles), (columns_in, columns), (tx_in, tx),
        (ty_in, ty), (ty_t_in, ty_t), (inv_in, inv), (potential_in, potential), (tb_in, tb), (hsub_in, hsub),
    )
    copies = [pltpu.make_async_copy(a, b, loads.at[i]) for i, (a, b) in enumerate(inputs)]
    for copy in copies:
        copy.start()

    barrier = pltpu.get_barrier_semaphore()

    def greet(i, carry):
        pl.semaphore_signal(
            barrier, inc=1, device_id=(band, lax.rem(me + i, NFFT)), device_id_type=MESH
        )
        return carry

    lax.fori_loop(1, NFFT, greet, 0)
    for i in range(1, NBAND):
        pl.semaphore_signal(
            barrier, inc=1, device_id=(lax.rem(band + i, NBAND), me), device_id_type=MESH
        )

    def fft_start(send, recv, ssem, rsem, whole):
        def step(i, carry):
            to = lax.rem(me + i, NFFT)
            pltpu.make_async_remote_copy(
                src_ref=send if whole else send.at[to],
                dst_ref=recv.at[me],
                send_sem=ssem,
                recv_sem=rsem,
                device_id=(band, to),
                device_id_type=MESH,
            ).start()
            return carry

        lax.fori_loop(1, NFFT, step, 0)

    def fft_all(send, recv, ssem, rsem, whole):
        part = recv.at[pl.ds(0, NFFT - 1)]
        return pltpu.make_async_remote_copy(
            src_ref=part,
            dst_ref=part,
            send_sem=ssem,
            recv_sem=rsem,
            device_id=(band, lax.rem(me + 1, NFFT)),
            device_id_type=MESH,
        )

    def fft_wait_recv(*args):
        fft_all(*args).wait_recv()

    def fft_wait_send(*args):
        fft_all(*args).wait_send()

    def band_copy(i, src, dst, ssem, rsem):
        to = lax.rem(band + i, NBAND)
        return pltpu.make_async_remote_copy(
            src_ref=src(to),
            dst_ref=dst.at[band],
            send_sem=ssem.at[i],
            recv_sem=rsem.at[band],
            device_id=(to, me),
            device_id_type=MESH,
        )

    def band_arrival(i, src, dst, ssem, rsem):
        source = lax.rem(band + NBAND - i, NBAND)
        return pltpu.make_async_remote_copy(
            src_ref=src(source),
            dst_ref=dst.at[source],
            send_sem=ssem.at[i],
            recv_sem=rsem.at[source],
            device_id=(source, me),
            device_id_type=MESH,
        )

    copies[0].wait()
    copies[1].wait()
    new = basis[2016:2048, :]
    none = jnp.zeros((16, 128), BF16)
    right = jnp.concatenate(
        [
            jnp.concatenate([new[0:16], none], 1),
            jnp.concatenate([none, new[0:16]], 1),
            jnp.concatenate([new[16:32], none], 1),
            jnp.concatenate([none, new[16:32]], 1),
            jnp.zeros((64, 256), BF16),
        ],
        0,
    )
    send1[...] = dot_nt(tz[...], right).reshape(NFFT, 8, 128)
    first = (send1, recv1, s1, r1, False)
    pl.semaphore_wait(barrier, NFFT - 1 + NBAND - 1)
    fft_start(*first)
    recv1[pl.ds(me, 1)] = send1[pl.ds(me, 1)]

    copies[2].wait()
    angle_tables(angles, table)

    new_args = (lambda to: new_own, news, sh, rh)
    new_own[...] = basis[2016:2048, :]
    for i in range(1, NBAND):
        band_copy(i, *new_args).start()
    news[pl.ds(band, 1)] = new_own[...].reshape(1, 32, 128)

    for i in range(3, 7):
        copies[i].wait()
    position = columns[...].astype(F32)
    pos_x = jnp.floor((position + 0.5) * (1.0 / NG))
    pos_y = position - NG * pos_x
    k_row = lax.broadcasted_iota(jnp.int32, (256, NCOL), 0).astype(F32)
    hot_x = (k_row == pos_x).astype(F32).astype(BF16)
    hot_y = (k_row == pos_y).astype(F32).astype(BF16)
    a_both = dot(tx[...], jnp.concatenate([hot_x, hot_x], 0))
    a_cos[...] = a_both[:HALF]
    a_sin[...] = a_both[HALF:]
    right2[...] = dot(ty_t[...], hot_y).astype(BF16)
    wide_y = jnp.broadcast_to(pos_y, (128, NCOL)).T
    lane_k = lax.broadcasted_iota(jnp.int32, (NCOL, 128), 1).astype(F32)
    hot_yt = jnp.concatenate(
        [(wide_y == lane_k).astype(F32), (wide_y == lane_k + 128.0).astype(F32)], 1
    ).astype(BF16)
    right1[...] = dot(hot_yt, ty[...]).astype(BF16)
    turns = (pos_x + pos_y) * (NG - 1.0)
    turns = turns - (2.0 * NG) * jnp.floor((turns + 0.5) * (0.5 / NG))
    center = jnp.broadcast_to(turns * (math.pi / NG), (8, NCOL))
    phase[0] = jnp.cos(center)
    phase[1] = jnp.sin(center)
    for j in range(4):
        phase_out[:, 4 * j : 4 * j + 4, :] = phase[:, 0:4, 128 * j : 128 * j + 128]
    freq_x = jnp.where(pos_x < NG // 2, pos_x, pos_x - NG)
    freq_y = jnp.where(pos_y < NG // 2, pos_y, pos_y - NG)
    radius[...] = jnp.broadcast_to(freq_x * freq_x + freq_y * freq_y, (128, NCOL)).T
    g_buf[...] = jnp.zeros_like(g_buf)

    for i in range(7, 11):
        copies[i].wait()
    fold_potential(potential, folded)
    fft_wait_recv(*first)

    lanes = lax.broadcasted_iota(jnp.int32, (8, 128), 1)
    for q in range(4):
        for j in range(4):
            total = jnp.zeros((8, 128), F32)
            for t in range(8):
                piece = recv1[8 * j + t]
                move = (16 * t - 16 * q) % 128
                if move:
                    piece = pltpu.roll(piece, move, 1)
                total = jnp.where((lanes >> 4) == t, piece, total)
            coef[q, :, 128 * j : 128 * j + 128] = total

    def mix(v):
        old_re, old_im = coef[2 * v], coef[2 * v + 1]
        coef[2 * v] = old_re * phase[0] - old_im * phase[1]
        coef[2 * v + 1] = old_re * phase[1] + old_im * phase[0]

    def unmix(v):
        for q in (2 * v, 2 * v + 4):
            new_re, new_im = g_buf[q], g_buf[q + 1]
            g_buf[q] = new_re * phase_out[0] + new_im * phase_out[1]
            g_buf[q + 1] = new_im * phase_out[0] - new_re * phase_out[1]

    def block(z, a, i):
        return pl.ds(HALF * (4 * z + 2 * a + i), HALF)

    def plane(z):
        return pl.ds(4 * HALF * z, 4 * HALF)

    def spread(v, z):
        for a, part in enumerate((a_cos, a_sin)):
            for i in range(2):
                d_buf[block(z, a, i), :] = (part[...] * coef[2 * v + i, z : z + 1, :]).astype(BF16)

    def to_field(v, z):
        q_buf[plane(z), :] = dot(d_buf[plane(z), :], right1[...])

    def multiply(v, z):
        q = [
            [tuple(q_buf[block(z, a, i), 128 * b : 128 * b + 128] for i in range(2)) for b in range(2)]
            for a in range(2)
        ]
        back = times_potential(q, [[folded[z, u, w] for w in range(2)] for u in range(2)])
        for a in range(2):
            for b in range(2):
                for i in range(2):
                    p_buf[block(z, a, i), 128 * b : 128 * b + 128] = back[a][b][i].astype(BF16)

    def from_field(v, z):
        u_buf[plane(z), :] = dot(p_buf[plane(z), :], right2[...])

    def collect(v, z):
        for i in range(2):
            total = jnp.sum(
                a_cos[...] * u_buf[block(z, 0, i), :] + a_sin[...] * u_buf[block(z, 1, i), :],
                axis=0,
                keepdims=True,
            )
            for j in range(4):
                g_buf[4 * (z % 2) + 2 * v + i, 4 * j + z // 2 : 4 * j + z // 2 + 1, :] = total[
                    :, 128 * j : 128 * j + 128
                ]

    steps = (spread, to_field, multiply, from_field, collect)

    for v in range(2):
        mix(v)
    for t in range(2 * SLAB + len(steps) - 1):
        for s, step in enumerate(steps):
            if 0 <= t - s < 2 * SLAB:
                step((t - s) // SLAB, (t - s) % SLAB)
    for v in range(2):
        unmix(v)

    volume = 1.0 / float(NG) ** 3
    wide_lanes = lax.broadcasted_iota(jnp.int32, (16, 128), 1)
    for t in range(8):
        total = jnp.zeros((16, 128), F32)
        for q in range(8):
            piece = g_buf[q]
            move = (16 * q - 16 * t) % 128
            if move:
                piece = pltpu.roll(piece, move, 1)
            total = jnp.where((wide_lanes >> 4) == q, piece, total)
        total = total * volume
        for j in range(4):
            send2[8 * j + t] = total[4 * j : 4 * j + 4]
    own = band * NFFT + me

    def spread_back(i, carry):
        to = lax.rem(own + i, NBAND * NFFT)
        pltpu.make_async_remote_copy(
            src_ref=send2.at[lax.rem(to, NFFT)],
            dst_ref=recv2.at[own],
            send_sem=s2,
            recv_sem=r2,
            device_id=(to // NFFT, lax.rem(to, NFFT)),
            device_id_type=MESH,
        ).start()
        return carry

    lax.fori_loop(1, NBAND * NFFT, spread_back, 0)
    back_part = recv2.at[pl.ds(0, NBAND * NFFT - 1)]
    back_all = pltpu.make_async_remote_copy(
        src_ref=back_part,
        dst_ref=back_part,
        send_sem=s2,
        recv_sem=r2,
        device_id=(band, lax.rem(me + 1, NFFT)),
        device_id_type=MESH,
    )
    recv2[pl.ds(own, 1)] = send2[pl.ds(me, 1)]
    rotate_back(me, state, table)
    couple(band, state, inv, hsub, low, y_buf, y_own, z_buf)

    vector_weights(basis, y_own, w_buf, bands_part)
    bands_args = (lambda to: bands_part.at[to], recvb, sb, rb)
    for i in range(1, NBAND):
        band_copy(i, *bands_args).start()
    recvb[pl.ds(band, 1)] = bands_part[pl.ds(band, 1)]
    for i in range(1, NBAND):
        band_arrival(i, *new_args).wait_recv()
    slot = lax.broadcasted_iota(jnp.int32, (16, 128), 1) & (NZC - 1)
    freq_z = jnp.where(slot < NZC // 2, slot, slot - NZC).astype(F32)
    own_radius = radius[pl.ds(pl.multiple_of(me * 16, 16), 16), :]
    kinetic = (own_radius + freq_z * freq_z) / (2.0 * (NG // 4) ** 2)

    back_all.wait_recv()
    slabs = []
    for b in range(NBAND):
        parts = [recv2[NFFT * b : NFFT * b + NFFT, r, :] for r in range(3)]
        parts.append(jnp.zeros((NFFT, 128), F32))
        slabs.append(jnp.concatenate(parts, 0).T.astype(BF16))
    local = dot(jnp.concatenate(slabs, 0), tb[...])
    for b in range(NBAND):
        for v in range(2):
            term = jnp.zeros((16, 128), F32)
            for n in range(2):
                row, lane = 128 * b + 64 * n + 32 * v, 256 * n
                term = term + local[row : row + 16, lane : lane + 128]
                term = term + local[row + 16 : row + 32, lane + 128 : lane + 256]
            coeffs = news[b, 16 * v : 16 * v + 16, :].astype(F32)
            hall[b, 16 * v : 16 * v + 16, :] = (kinetic * coeffs + term).astype(BF16)

    pairs = dot_nt(basis[...], hall[...].reshape(128, 128))
    pair_row = lax.broadcasted_iota(jnp.int32, (2048, 128), 0)
    pair_lane = lax.broadcasted_iota(jnp.int32, (2048, 128), 1)
    pairs = jnp.where(((pair_row ^ pair_lane) & 15) == 0, pairs, 0.0)
    by_group = jnp.sum(pairs.reshape(GROUP, 16, 128), axis=1)
    pick_row = lax.broadcasted_iota(jnp.int32, (8, 128), 0)
    pick = (pick_row == (lanes >> 4)).astype(F32)
    send3[...] = dot_nt(pick, by_group, HIGH)
    third = (send3, recv3, s3, r3, True)
    fft_start(*third)
    recv3[pl.ds(me, 1)] = send3[...].reshape(1, 8, 128)
    rotate_on(state, table, rows)
    hblock_out[...] = hall[pl.ds(band, 1)].reshape(32, 128)
    for i in range(1, NBAND):
        band_arrival(i, *bands_args).wait_recv()
    bands_total = recvb[0].astype(F32)
    for b in range(1, NBAND):
        bands_total = bands_total + recvb[b].astype(F32)
    bands_out[...] = bands_total.astype(BF16)
    fft_wait_recv(*third)
    new_columns = recv3[0]
    for p in range(1, NFFT):
        new_columns = new_columns + recv3[p]
    new_columns = new_columns * (1.0 / math.sqrt(2 * NCOL * NZC))
    z_new = dot_nt(y_own[0:32, :], new_columns, HIGH)
    total = rows[0:32, :] + dot(z_new, rows[32:40, :], HIGH)
    sendf[...] = total.reshape(NBAND, 8, ORDER)
    final_args = (lambda to: sendf.at[to], recvf, sf, rf)
    for i in range(1, NBAND):
        band_copy(i, *final_args).start()
    recvf[pl.ds(band, 1)] = sendf[pl.ds(band, 1)]

    fft_wait_send(*first)
    back_all.wait_send()
    fft_wait_send(*third)
    for i in range(1, NBAND):
        band_copy(i, *bands_args).wait_send()
        band_copy(i, *new_args).wait_send()
    for i in range(1, NBAND):
        band_arrival(i, *final_args).wait_recv()
    final = recvf[0] + recvf[1] + recvf[2] + recvf[3]
    rotated_out[...] = final[0:4]
    for i in range(1, NBAND):
        band_copy(i, *final_args).wait_send()


def main_part(*operands):
    vmem = pl.BlockSpec(memory_space=pltpu.VMEM)
    dma = pltpu.SemaphoreType.DMA
    return pl.pallas_call(
        main_kernel,
        out_shape=(
            jax.ShapeDtypeStruct((32, 128), BF16),
            jax.ShapeDtypeStruct((4, ORDER), F32),
            jax.ShapeDtypeStruct((32, 128), BF16),
        ),
        in_specs=[pl.BlockSpec(memory_space=pl.ANY)] * len(operands),
        out_specs=(vmem,) * 3,
        scratch_shapes=[pltpu.VMEM(x.shape, x.dtype) for x in operands]
        + [
            pltpu.VMEM((2, 16, TILE, 128), F32),
            pltpu.VMEM((2, 8 * ROUNDS, TILE, 128), F32),
            pltpu.VMEM((ORDER, ORDER), BF16),
            pltpu.VMEM((128, ORDER), F32),
            pltpu.VMEM((40, GROUP), F32),
            pltpu.VMEM((ORDER, 128), F32),
            pltpu.VMEM((40, ORDER), F32),
            pltpu.VMEM((128, 2048), BF16),
            pltpu.VMEM((NBAND, 32, 128), BF16),
            pltpu.VMEM((NFFT, 8, 128), F32),
            pltpu.VMEM((NFFT, 8, 128), F32),
            pltpu.VMEM((NFFT, 4, 128), F32),
            pltpu.VMEM((NBAND * NFFT, 4, 128), F32),
            pltpu.VMEM((8, 128), F32),
            pltpu.VMEM((NFFT, 8, 128), F32),
            pltpu.VMEM((32, 128), BF16),
            pltpu.VMEM((NBAND, 32, 128), BF16),
            pltpu.VMEM((NBAND, 32, 128), BF16),
            pltpu.VMEM((NBAND, 32, 128), BF16),
            pltpu.VMEM((NBAND, 8, ORDER), F32),
            pltpu.VMEM((NBAND, 8, ORDER), F32),
            pltpu.VMEM((4 * SLAB * HALF, 256), F32),
            pltpu.VMEM((4 * SLAB * HALF, NCOL), F32),
            pltpu.VMEM((HALF, NCOL), F32),
            pltpu.VMEM((HALF, NCOL), F32),
            pltpu.VMEM((2, 8, NCOL), F32),
            pltpu.VMEM((2, 16, 128), F32),
            pltpu.VMEM((SLAB, 2, 2, HALF, 128), F32),
            pltpu.VMEM((NCOL, 256), BF16),
            pltpu.VMEM((256, NCOL), BF16),
            pltpu.VMEM((NCOL, 128), F32),
            pltpu.VMEM((4, 8, NCOL), F32),
            pltpu.VMEM((4 * SLAB * HALF, NCOL), BF16),
            pltpu.VMEM((4 * SLAB * HALF, 256), BF16),
            pltpu.VMEM((8, 16, 128), F32),
        ]
        + [dma] * 6
        + [dma((NBAND,))] * 6
        + [dma((len(operands),))],
        compiler_params=pltpu.CompilerParams(
            collective_id=0, has_side_effects=True, vmem_limit_bytes=56 * 2**20
        ),
        name="main_part",
    )(*operands)


def result_kernel(*refs):
    sources, targets, sems = refs[:3], refs[3:6], refs[6]
    copies = [
        pltpu.make_async_copy(a, b, sems.at[i]) for i, (a, b) in enumerate(zip(sources, targets))
    ]
    for copy in copies:
        copy.start()
    for copy in copies:
        copy.wait()


def result_part(*operands):
    anywhere = pl.BlockSpec(memory_space=pl.ANY)
    return pl.pallas_call(
        result_kernel,
        out_shape=tuple(jax.ShapeDtypeStruct(x.shape, x.dtype) for x in operands),
        in_specs=[anywhere] * 3,
        out_specs=(anywhere,) * 3,
        scratch_shapes=[pltpu.SemaphoreType.DMA((3,))],
        compiler_params=pltpu.CompilerParams(vmem_limit_bytes=56 * 2**20),
        name="result_part",
    )(*operands)


def per_device(basis, potential, colmap, hsub_old, inv_factor, angles):
    table = y_table()
    results = main_part(
        basis.reshape(2048, 128),
        colmap.reshape(1, NCOL),
        angles.reshape(8 * ROUNDS, TILE),
        jnp.asarray(z_table().astype(BF16)),
        inv_factor,
        hsub_old.T,
        jnp.asarray(x_table()),
        jnp.asarray(table.astype(BF16)),
        jnp.asarray(table.T.astype(BF16)),
        potential,
        jnp.asarray(z_table_back().astype(BF16)),
    )
    hblock, rotated, bands = result_part(*results)
    return (hblock.reshape(2, 16, 128), rotated, bands.reshape(2, 16, 128))


def solution(mesh):
    in_specs = (P("band", "fft", None), P("fft", None, None), P(), P("band", None), P(), P())
    out_specs = (P("band", "fft", None), P(("band", "fft"), None), P("band", "fft", None))
    return jax.shard_map(
        per_device, mesh=mesh, in_specs=in_specs, out_specs=out_specs, check_vma=False
    )
```

```python
import functools
import math

import jax
import jax.numpy as jnp
import numpy as np
from jax import lax
from jax.experimental import pallas as pl
from jax.experimental.pallas import tpu as pltpu
from jax.sharding import PartitionSpec as P

NG = 192
HALF = 96
NZC = 64
ORDER = 512
GROUP = 128
NCOL = 512
NBAND = 4
NFFT = 32
SLAB = 6
ROUNDS = 30
TILE = 32
F32 = jnp.float32
BF16 = jnp.bfloat16
HIGH = lax.Precision.HIGHEST
MESH = pl.DeviceIdType.MESH
NT = (((1,), (1,)), ((), ()))


def dot(a, b, precision=None):
    return jnp.dot(a, b, precision=precision, preferred_element_type=F32)


def dot_nt(a, b, precision=None):
    return lax.dot_general(a, b, NT, precision=precision, preferred_element_type=F32)


def z_table():
    slot = np.arange(NZC)
    freq = np.where(slot < NZC // 2, slot, slot - NZC) % NG
    table = np.zeros((NFFT, 8, 4, NZC), np.float64)
    z = np.arange(NG).reshape(NFFT, SLAB)
    angle = 2.0 * np.pi * ((z[:, :, None] * freq) % NG) / NG
    table[:, :SLAB, 0] = np.cos(angle)
    table[:, :SLAB, 1] = -np.sin(angle)
    table[:, :SLAB, 2] = np.sin(angle)
    table[:, :SLAB, 3] = np.cos(angle)
    return table.reshape(NFFT * 8, 4 * NZC)


def z_table_back():
    table = z_table().reshape(NFFT, 4, 2, 4 * NZC)
    return np.transpose(table, (1, 0, 2, 3)).reshape(4 * NFFT, 8 * NZC)


def half_angles():
    return 2.0 * np.pi * (((2 * np.arange(HALF)[:, None] + 1) * np.arange(NG)) % (2 * NG)) / (2 * NG)


def x_table():
    angle = half_angles()
    both = np.concatenate([np.cos(angle), np.sin(angle)], 0)
    high = np.asarray(both, np.float32).astype(BF16)
    low = (both - high.astype(np.float64)).astype(BF16)
    table = np.zeros((2 * HALF, 512), BF16)
    table[:, :NG] = high
    table[:, 256 : 256 + NG] = low
    return table


def y_table():
    angle = half_angles().T
    table = np.zeros((256, 256), np.float64)
    table[:NG, :HALF] = np.cos(angle)
    table[:NG, 128 : 128 + HALF] = np.sin(angle)
    return table


def tile_order(turn):
    seat = [0] + [1 + ((m - 1 + turn) % 15) for m in range(1, 16)]
    return seat[:8] + seat[:7:-1]


def pair_step(state, table, r):
    src, dst = state.at[r % 2], state.at[(r + 1) % 2]
    shift = r % TILE
    c = table[0, 8 * r : 8 * r + 8]
    s = table[1, 8 * r : 8 * r + 8]
    a = src[0:8]
    b = src[8:16]
    if shift:
        b = pltpu.roll(b, TILE - shift, 1)
    a, b = c * a - s * b, s * a + c * b
    if shift:
        b = pltpu.roll(b, shift, 1)
    dst[0:1] = a[0:1]
    dst[1:7] = a[2:8]
    dst[7:8] = b[7:8]
    dst[8:9] = a[1:2]
    dst[9:16] = b[0:7]


def angle_tables(angles, table):
    ang = jnp.concatenate([angles[...], jnp.zeros((240, 128 - TILE), F32)], 1)
    ang = jnp.concatenate([ang, jnp.zeros((16, 128), F32)], 0)
    for i, part in enumerate((jnp.cos(ang).T[:TILE], jnp.sin(ang).T[:TILE])):
        for q in range(8 * ROUNDS):
            table[i, q] = jnp.broadcast_to(part[:, q : q + 1], (TILE, 128))


def rotate_factor(band, state, table, inv, factor):
    own = inv[:, pl.ds(pl.multiple_of(band * GROUP, GROUP), GROUP)]
    for p, tile in enumerate(tile_order(0)):
        state[0, p] = own[TILE * tile : TILE * tile + TILE]
    for r in range(ROUNDS):
        pair_step(state, table, r)
    factor[...] = natural(state, 0)


def natural(state, which):
    return jnp.concatenate([state[which, p] for p in list(range(8)) + list(range(15, 7, -1))], 0)


def couple(me, state, inv, hsub, low, factor, factor_wide, y_own, z_buf):
    low[...] = inv[...].astype(BF16)
    for j in range(4):
        factor_wide[:, GROUP * j : GROUP * j + GROUP] = factor[pl.ds(j, 128, stride=4), :].astype(BF16)
    line = lax.broadcasted_iota(jnp.int32, (128, ORDER), 0)
    column = lax.broadcasted_iota(jnp.int32, (128, ORDER), 1)
    target = ((line >> 3) * NFFT + me) * 4 + (line & 7)
    target = jnp.where((line < 32) & ((line & 7) < 4), target, -1)
    target = jnp.where((line >= 32) & (line < 40), line - 32, target)
    own = dot((column == target).astype(F32).astype(BF16), factor[...].astype(BF16))
    y_own[...] = own[:40]
    z_old = dot_nt(hsub[...].astype(BF16), own.astype(BF16))
    z_buf[...] = jnp.zeros_like(z_buf)
    for b in range(NBAND):
        z_buf[b * GROUP : b * GROUP + 126, :] = z_old[b * 126 : (b + 1) * 126, :]
    lanes = lax.broadcasted_iota(jnp.int32, (ORDER, 128), 1)
    rows = lax.broadcasted_iota(jnp.int32, (ORDER, 128), 0)
    fresh = ((lanes - 32) >> 1) * GROUP + 126 + (lanes & 1)
    z = jnp.where(lanes < 32, z_buf[...], 0.0)
    z = jnp.where((lanes >= 32) & (lanes < 40) & (rows == fresh), 1.0, z)
    w = dot(low[...], z.astype(BF16))
    for p, tile in enumerate(tile_order(0)):
        state[0, p] = w[TILE * tile : TILE * tile + TILE]


def rotate_on(state, table, rows):
    for r in range(ROUNDS):
        pair_step(state, table, r)
    rows[...] = natural(state, 0).T[:40]


def vector_weights(basis, y_own, w_buf, bands_part):
    weights = y_own[32:40, :].astype(BF16)
    spread_row = lax.broadcasted_iota(jnp.int32, (GROUP, 2048), 0)
    spread_lane = lax.broadcasted_iota(jnp.int32, (GROUP, 2048), 1)
    spread = (spread_row == (spread_lane >> 4)).astype(F32).astype(BF16)
    wide = dot(weights, spread)
    own_row = lax.broadcasted_iota(jnp.int32, (16, 2048), 0)
    own_lane = lax.broadcasted_iota(jnp.int32, (16, 2048), 1)
    keep = own_row == (own_lane & 15)
    for k in range(8):
        w_buf[16 * k : 16 * k + 16, :] = jnp.where(keep, wide[k : k + 1], 0.0).astype(BF16)
    bands_part[...] = dot(w_buf[...], basis[...]).astype(BF16).reshape(NBAND, 32, 128)


def split(value):
    high = value.astype(BF16)
    return high, (value - high.astype(F32)).astype(BF16)


def fold_potential(potential, folded):
    y_row = lax.broadcasted_iota(jnp.int32, (NG, 256), 0)
    y_lane = lax.broadcasted_iota(jnp.int32, (NG, 256), 1)
    wanted = jnp.where(y_lane < 128, HALF + y_lane, HALF - 1 + 128 - y_lane)
    wanted = jnp.where((y_lane & 127) < HALF, wanted, -1)
    order_y = (y_row == wanted).astype(F32).astype(BF16)
    x_row = lax.broadcasted_iota(jnp.int32, (HALF, HALF), 0)
    x_lane = lax.broadcasted_iota(jnp.int32, (HALF, HALF), 1)
    order_x = (x_row + x_lane == HALF - 1).astype(F32).astype(BF16)
    high, low = split(potential[...].reshape(SLAB * NG, NG))
    value = dot(high, order_y) + dot(low, order_y)
    for z in range(SLAB):
        high, low = split(value[NG * z : NG * z + HALF])
        low_side = dot(order_x, high) + dot(order_x, low)
        high_side = value[NG * z + HALF : NG * z + NG]
        for v in range(2):
            folded[z, 0, v] = high_side[:, 128 * v : 128 * v + 128]
            folded[z, 1, v] = low_side[:, 128 * v : 128 * v + 128]


def times_potential(q, v):
    (cc, cs), (sc, ss) = q

    def add(m, n):
        return m[0] + n[0], m[1] + n[1]

    def sub(m, n):
        return m[0] - n[0], m[1] - n[1]

    def by_i(m):
        return -m[1], m[0]

    def scaled(m, w):
        return m[0] * w, m[1] * w

    e1, o1 = sub(cc, ss), by_i(add(sc, cs))
    e2, o2 = add(cc, ss), by_i(sub(sc, cs))
    high = scaled(add(e1, o1), v[0][0])
    low = scaled(sub(e1, o1), v[1][1])
    right = scaled(add(e2, o2), v[0][1])
    left = scaled(sub(e2, o2), v[1][0])
    s1, d1, s2, d2 = add(high, low), sub(high, low), add(right, left), sub(right, left)
    odd_x, odd_y = add(d1, d2), sub(d1, d2)
    return (add(s1, s2), (odd_y[1], -odd_y[0])), ((odd_x[1], -odd_x[0]), sub(s2, s1))


def hops(steps):
    z_hi, core, z_lo, x, y = steps
    return (1 if z_lo else 2 * z_hi) + min(x, 4 - x) + min(y, 4 - y)


def all_steps(bands):
    found = [
        (z_hi, core, z_lo, x, y)
        for z_hi in range(bands)
        for core in range(bands)
        for z_lo in range(2)
        for x in range(4)
        for y in range(4)
    ]
    found.remove((0, 0, 0, 0, 0))
    return sorted(found, key=lambda s: -hops(s))


def main_kernel(
    basis_in, columns_in, angles_in, tz_in, inv_in, hsub_in, tx_in, ty_in, ty_t_in, potential_in, tb_in,
    hblock_out, rotated_out, bands_out,
    basis, columns, angles, tz, inv, hsub, tx, ty, ty_t, potential, tb,
    state, table, low, factor, factor_wide, y_own, z_buf, rows, w_buf, bands_part,
    send1, recv1, send2, recv2, send3, recv3, new_own, news, hall, recvb, sendf, recvf,
    q_buf, u_buf, a_cos, a_sin, phase, phase_out, folded, right1, right2, radius, coef, d_buf, p_buf, g_buf,
    s1, r1, s2, r2, s3, r3, sh, rh, sb, rb, sf, rf, loads,
):
    band = lax.axis_index("band")
    me = lax.axis_index("fft")

    inputs = (
        (basis_in, basis), (tz_in, tz), (angles_in, angles), (columns_in, columns), (tx_in, tx),
        (ty_in, ty), (ty_t_in, ty_t), (inv_in, inv), (potential_in, potential), (tb_in, tb), (hsub_in, hsub),
    )
    copies = [pltpu.make_async_copy(a, b, loads.at[i]) for i, (a, b) in enumerate(inputs)]
    copies[0].start()
    copies[1].start()

    def peer(steps):
        z_hi, core, z_lo, x, y = steps
        to_fft = (((me >> 4) ^ z_lo) << 4) | ((((me >> 2) + x) & 3) << 2) | ((me + y) & 3)
        return (band ^ (2 * z_hi + core), to_fft)

    near, every = all_steps(1), all_steps(2)

    barrier = pltpu.get_barrier_semaphore()

    for steps in near:
        pl.semaphore_signal(barrier, inc=1, device_id=peer(steps), device_id_type=MESH)
    for i in range(1, NBAND):
        pl.semaphore_signal(
            barrier, inc=1, device_id=(lax.rem(band + i, NBAND), me), device_id_type=MESH
        )

    for copy in copies[2:]:
        copy.start()

    def fft_start(send, recv, ssem, rsem, whole):
        for steps in near:
            to = peer(steps)
            pltpu.make_async_remote_copy(
                src_ref=send if whole else send.at[to[1]],
                dst_ref=recv.at[me],
                send_sem=ssem,
                recv_sem=rsem,
                device_id=to,
                device_id_type=MESH,
            ).start()

    def fft_all(send, recv, ssem, rsem, whole):
        part = recv.at[pl.ds(0, NFFT - 1)]
        return pltpu.make_async_remote_copy(
            src_ref=part,
            dst_ref=part,
            send_sem=ssem,
            recv_sem=rsem,
            device_id=(band, lax.rem(me + 1, NFFT)),
            device_id_type=MESH,
        )

    def fft_wait_recv(*args):
        fft_all(*args).wait_recv()

    def fft_wait_send(*args):
        fft_all(*args).wait_send()

    def band_copy(i, src, dst, ssem, rsem):
        to = lax.rem(band + i, NBAND)
        return pltpu.make_async_remote_copy(
            src_ref=src(to),
            dst_ref=dst.at[band],
            send_sem=ssem.at[i],
            recv_sem=rsem.at[band],
            device_id=(to, me),
            device_id_type=MESH,
        )

    def band_arrival(i, src, dst, ssem, rsem):
        source = lax.rem(band + NBAND - i, NBAND)
        return pltpu.make_async_remote_copy(
            src_ref=src(source),
            dst_ref=dst.at[source],
            send_sem=ssem.at[i],
            recv_sem=rsem.at[source],
            device_id=(source, me),
            device_id_type=MESH,
        )

    copies[0].wait()
    copies[1].wait()
    new = basis[2016:2048, :]
    none = jnp.zeros((16, 128), BF16)
    right = jnp.concatenate(
        [
            jnp.concatenate([new[0:16], none], 1),
            jnp.concatenate([none, new[0:16]], 1),
            jnp.concatenate([new[16:32], none], 1),
            jnp.concatenate([none, new[16:32]], 1),
            jnp.zeros((64, 256), BF16),
        ],
        0,
    )
    send1[...] = dot_nt(tz[...], right).reshape(NFFT, 8, 128)
    first = (send1, recv1, s1, r1, False)
    pl.semaphore_wait(barrier, NFFT - 1 + NBAND - 1)
    fft_start(*first)
    recv1[pl.ds(me, 1)] = send1[pl.ds(me, 1)]

    copies[2].wait()
    angle_tables(angles, table)

    new_args = (lambda to: new_own, news, sh, rh)
    new_own[...] = basis[2016:2048, :]
    for i in range(1, NBAND):
        band_copy(i, *new_args).start()
    news[pl.ds(band, 1)] = new_own[...].reshape(1, 32, 128)

    for i in range(3, 7):
        copies[i].wait()
    position = columns[...].astype(F32)
    pos_x = jnp.floor((position + 0.5) * (1.0 / NG))
    pos_y = position - NG * pos_x
    k_row = lax.broadcasted_iota(jnp.int32, (256, NCOL), 0).astype(F32)
    hot_x = (k_row == pos_x).astype(F32).astype(BF16)
    hot_y = (k_row == pos_y).astype(F32).astype(BF16)
    a_both = dot(tx[...], jnp.concatenate([hot_x, hot_x], 0))
    a_cos[...] = a_both[:HALF]
    a_sin[...] = a_both[HALF:]
    right2[...] = dot(ty_t[...], hot_y).astype(BF16)
    wide_y = jnp.broadcast_to(pos_y, (128, NCOL)).T
    lane_k = lax.broadcasted_iota(jnp.int32, (NCOL, 128), 1).astype(F32)
    hot_yt = jnp.concatenate(
        [(wide_y == lane_k).astype(F32), (wide_y == lane_k + 128.0).astype(F32)], 1
    ).astype(BF16)
    right1[...] = dot(hot_yt, ty[...]).astype(BF16)
    turns = (pos_x + pos_y) * (NG - 1.0)
    turns = turns - (2.0 * NG) * jnp.floor((turns + 0.5) * (0.5 / NG))
    center = jnp.broadcast_to(turns * (math.pi / NG), (8, NCOL))
    phase[0] = jnp.cos(center)
    phase[1] = jnp.sin(center)
    for j in range(4):
        phase_out[:, 4 * j : 4 * j + 4, :] = phase[:, 0:4, 128 * j : 128 * j + 128]
    freq_x = jnp.where(pos_x < NG // 2, pos_x, pos_x - NG)
    freq_y = jnp.where(pos_y < NG // 2, pos_y, pos_y - NG)
    radius[...] = jnp.broadcast_to(freq_x * freq_x + freq_y * freq_y, (128, NCOL)).T
    g_buf[...] = jnp.zeros_like(g_buf)

    for i in range(7, 11):
        copies[i].wait()
    fold_potential(potential, folded)
    fft_wait_recv(*first)

    lanes = lax.broadcasted_iota(jnp.int32, (8, 128), 1)
    for q in range(4):
        for j in range(4):
            total = jnp.zeros((8, 128), F32)
            for t in range(8):
                piece = recv1[8 * j + t]
                move = (16 * t - 16 * q) % 128
                if move:
                    piece = pltpu.roll(piece, move, 1)
                total = jnp.where((lanes >> 4) == t, piece, total)
            coef[q, :, 128 * j : 128 * j + 128] = total

    def mix(v):
        old_re, old_im = coef[2 * v], coef[2 * v + 1]
        coef[2 * v] = old_re * phase[0] - old_im * phase[1]
        coef[2 * v + 1] = old_re * phase[1] + old_im * phase[0]

    def unmix(v):
        for q in (2 * v, 2 * v + 4):
            new_re, new_im = g_buf[q], g_buf[q + 1]
            g_buf[q] = new_re * phase_out[0] + new_im * phase_out[1]
            g_buf[q + 1] = new_im * phase_out[0] - new_re * phase_out[1]

    def block(z, a, i):
        return pl.ds(HALF * (4 * z + 2 * a + i), HALF)

    def plane(z):
        return pl.ds(4 * HALF * z, 4 * HALF)

    def spread(v, z):
        for a, part in enumerate((a_cos, a_sin)):
            for i in range(2):
                d_buf[block(z, a, i), :] = (part[...] * coef[2 * v + i, z : z + 1, :]).astype(BF16)

    def to_field(v, z):
        q_buf[plane(z), :] = dot(d_buf[plane(z), :], right1[...])

    def multiply(v, z):
        q = [
            [tuple(q_buf[block(z, a, i), 128 * b : 128 * b + 128] for i in range(2)) for b in range(2)]
            for a in range(2)
        ]
        back = times_potential(q, [[folded[z, u, w] for w in range(2)] for u in range(2)])
        for a in range(2):
            for b in range(2):
                for i in range(2):
                    p_buf[block(z, a, i), 128 * b : 128 * b + 128] = back[a][b][i].astype(BF16)

    def from_field(v, z):
        u_buf[plane(z), :] = dot(p_buf[plane(z), :], right2[...])

    def collect(v, z):
        for i in range(2):
            total = jnp.sum(
                a_cos[...] * u_buf[block(z, 0, i), :] + a_sin[...] * u_buf[block(z, 1, i), :],
                axis=0,
                keepdims=True,
            )
            for j in range(4):
                g_buf[4 * (z % 2) + 2 * v + i, 4 * j + z // 2 : 4 * j + z // 2 + 1, :] = total[
                    :, 128 * j : 128 * j + 128
                ]

    steps = (spread, to_field, multiply, from_field, collect)

    for v in range(2):
        mix(v)
    for t in range(2 * SLAB + len(steps) - 1):
        for s, step in enumerate(steps):
            if 0 <= t - s < 2 * SLAB:
                step((t - s) // SLAB, (t - s) % SLAB)
    for v in range(2):
        unmix(v)

    volume = 1.0 / float(NG) ** 3
    wide_lanes = lax.broadcasted_iota(jnp.int32, (16, 128), 1)
    for t in range(8):
        total = jnp.zeros((16, 128), F32)
        for q in range(8):
            piece = g_buf[q]
            move = (16 * q - 16 * t) % 128
            if move:
                piece = pltpu.roll(piece, move, 1)
            total = jnp.where((wide_lanes >> 4) == q, piece, total)
        total = total * volume
        for j in range(4):
            send2[8 * j + t] = total[4 * j : 4 * j + 4]
    own = band * NFFT + me

    for steps in every:
        to = peer(steps)
        pltpu.make_async_remote_copy(
            src_ref=send2.at[to[1]],
            dst_ref=recv2.at[own],
            send_sem=s2,
            recv_sem=r2,
            device_id=to,
            device_id_type=MESH,
        ).start()
    back_part = recv2.at[pl.ds(0, NBAND * NFFT - 1)]
    back_all = pltpu.make_async_remote_copy(
        src_ref=back_part,
        dst_ref=back_part,
        send_sem=s2,
        recv_sem=r2,
        device_id=(band, lax.rem(me + 1, NFFT)),
        device_id_type=MESH,
    )
    recv2[pl.ds(own, 1)] = send2[pl.ds(me, 1)]
    rotate_factor(band, state, table, inv, factor)
    couple(me, state, inv, hsub, low, factor, factor_wide, y_own, z_buf)
    rotate_on(state, table, rows)
    sendf[...] = rows[0:32, :].reshape(NBAND, 8, ORDER)
    final_args = (lambda to: sendf.at[to], recvf, sf, rf)
    for i in range(1, NBAND):
        band_copy(i, *final_args).start()
    recvf[pl.ds(band, 1)] = sendf[pl.ds(band, 1)]

    for i in range(1, NBAND):
        band_arrival(i, *new_args).wait_recv()
    slot = lax.broadcasted_iota(jnp.int32, (16, 128), 1) & (NZC - 1)
    freq_z = jnp.where(slot < NZC // 2, slot, slot - NZC).astype(F32)
    own_radius = radius[pl.ds(pl.multiple_of(me * 16, 16), 16), :]
    kinetic = (own_radius + freq_z * freq_z) / (2.0 * (NG // 4) ** 2)

    back_all.wait_recv()
    slabs = []
    for b in range(NBAND):
        parts = [recv2[NFFT * b : NFFT * b + NFFT, r, :] for r in range(3)]
        parts.append(jnp.zeros((NFFT, 128), F32))
        slabs.append(jnp.concatenate(parts, 0).T.astype(BF16))
    local = dot(jnp.concatenate(slabs, 0), tb[...])
    for b in range(NBAND):
        for v in range(2):
            term = jnp.zeros((16, 128), F32)
            for n in range(2):
                row, lane = 128 * b + 64 * n + 32 * v, 256 * n
                term = term + local[row : row + 16, lane : lane + 128]
                term = term + local[row + 16 : row + 32, lane + 128 : lane + 256]
            coeffs = news[b, 16 * v : 16 * v + 16, :].astype(F32)
            hall[b, 16 * v : 16 * v + 16, :] = (kinetic * coeffs + term).astype(BF16)

    pairs = dot_nt(basis[...], hall[...].reshape(128, 128))
    pair_row = lax.broadcasted_iota(jnp.int32, (2048, 128), 0)
    pair_lane = lax.broadcasted_iota(jnp.int32, (2048, 128), 1)
    pairs = jnp.where(((pair_row ^ pair_lane) & 15) == 0, pairs, 0.0)
    by_group = jnp.sum(pairs.reshape(GROUP, 16, 128), axis=1)
    pick_row = lax.broadcasted_iota(jnp.int32, (128, 512), 0)
    pick_lane = lax.broadcasted_iota(jnp.int32, (128, 512), 1)
    slot_of = pick_lane & 127
    picked = ((slot_of >> 3) == (pick_lane >> 7)) & ((slot_of & 7) == (pick_row >> 4))
    pick = picked.astype(F32).astype(BF16)
    high, low_part = split(by_group)
    fresh = dot(high, pick) + dot(low_part, pick)
    fresh = jnp.concatenate([fresh[:, 128 * j : 128 * j + 128] for j in range(4)], 0).astype(BF16)
    send3[...] = dot(factor_wide[...], fresh).reshape(NBAND * NFFT, 1, 128)
    for steps in every:
        to = peer(steps)
        pltpu.make_async_remote_copy(
            src_ref=send3.at[to[0] * NFFT + to[1]],
            dst_ref=recv3.at[own],
            send_sem=s3,
            recv_sem=r3,
            device_id=to,
            device_id_type=MESH,
        ).start()
    sum_part = recv3.at[pl.ds(0, NBAND * NFFT - 1)]
    sum_all = pltpu.make_async_remote_copy(
        src_ref=sum_part,
        dst_ref=sum_part,
        send_sem=s3,
        recv_sem=r3,
        device_id=(band, lax.rem(me + 1, NFFT)),
        device_id_type=MESH,
    )
    recv3[pl.ds(own, 1)] = send3[pl.ds(own, 1)]
    vector_weights(basis, y_own, w_buf, bands_part)
    bands_args = (lambda to: bands_part.at[to], recvb, sb, rb)
    for i in range(1, NBAND):
        band_copy(i, *bands_args).start()
    recvb[pl.ds(band, 1)] = bands_part[pl.ds(band, 1)]
    hblock_out[...] = hall[pl.ds(band, 1)].reshape(32, 128)
    for i in range(1, NBAND):
        band_arrival(i, *bands_args).wait_recv()
    bands_total = recvb[0].astype(F32)
    for b in range(1, NBAND):
        bands_total = bands_total + recvb[b].astype(F32)
    bands_out[...] = bands_total.astype(BF16)
    for i in range(1, NBAND):
        band_arrival(i, *final_args).wait_recv()
    old_part = recvf[0] + recvf[1] + recvf[2] + recvf[3]
    wide_rows = jnp.concatenate([rows[32:40, :]] * 4 + [jnp.zeros((96, ORDER), F32)], 0).astype(BF16)
    fft_wait_send(*first)
    back_all.wait_send()
    for i in range(1, NBAND):
        band_copy(i, *bands_args).wait_send()
        band_copy(i, *new_args).wait_send()
        band_copy(i, *final_args).wait_send()

    sum_all.wait_recv()
    total = jnp.sum(recv3[...].reshape(NBAND * NFFT, 128), axis=0, keepdims=True)
    total = total * (1.0 / math.sqrt(2 * NCOL * NZC))
    spread_rows = lax.broadcasted_iota(jnp.int32, (8, 128), 0)
    total = jnp.where((lanes >> 3) == spread_rows, total, 0.0)
    new_part = dot(total.astype(BF16), wide_rows)
    rotated_out[...] = (old_part + new_part)[0:4]
    sum_all.wait_send()


def main_part(*operands):
    vmem = pl.BlockSpec(memory_space=pltpu.VMEM)
    dma = pltpu.SemaphoreType.DMA
    return pl.pallas_call(
        main_kernel,
        out_shape=(
            jax.ShapeDtypeStruct((32, 128), BF16),
            jax.ShapeDtypeStruct((4, ORDER), F32),
            jax.ShapeDtypeStruct((32, 128), BF16),
        ),
        in_specs=[pl.BlockSpec(memory_space=pl.ANY)] * len(operands),
        out_specs=(vmem,) * 3,
        scratch_shapes=[pltpu.VMEM(x.shape, x.dtype) for x in operands]
        + [
            pltpu.VMEM((2, 16, TILE, 128), F32),
            pltpu.VMEM((2, 8 * ROUNDS, TILE, 128), F32),
            pltpu.VMEM((ORDER, ORDER), BF16),
            pltpu.VMEM((ORDER, 128), F32),
            pltpu.VMEM((128, ORDER), BF16),
            pltpu.VMEM((40, GROUP), F32),
            pltpu.VMEM((ORDER, 128), F32),
            pltpu.VMEM((40, ORDER), F32),
            pltpu.VMEM((128, 2048), BF16),
            pltpu.VMEM((NBAND, 32, 128), BF16),
            pltpu.VMEM((NFFT, 8, 128), F32),
            pltpu.VMEM((NFFT, 8, 128), F32),
            pltpu.VMEM((NFFT, 4, 128), F32),
            pltpu.VMEM((NBAND * NFFT, 4, 128), F32),
            pltpu.VMEM((NBAND * NFFT, 1, 128), F32),
            pltpu.VMEM((NBAND * NFFT, 1, 128), F32),
            pltpu.VMEM((32, 128), BF16),
            pltpu.VMEM((NBAND, 32, 128), BF16),
            pltpu.VMEM((NBAND, 32, 128), BF16),
            pltpu.VMEM((NBAND, 32, 128), BF16),
            pltpu.VMEM((NBAND, 8, ORDER), F32),
            pltpu.VMEM((NBAND, 8, ORDER), F32),
            pltpu.VMEM((4 * SLAB * HALF, 256), F32),
            pltpu.VMEM((4 * SLAB * HALF, NCOL), F32),
            pltpu.VMEM((HALF, NCOL), F32),
            pltpu.VMEM((HALF, NCOL), F32),
            pltpu.VMEM((2, 8, NCOL), F32),
            pltpu.VMEM((2, 16, 128), F32),
            pltpu.VMEM((SLAB, 2, 2, HALF, 128), F32),
            pltpu.VMEM((NCOL, 256), BF16),
            pltpu.VMEM((256, NCOL), BF16),
            pltpu.VMEM((NCOL, 128), F32),
            pltpu.VMEM((4, 8, NCOL), F32),
            pltpu.VMEM((4 * SLAB * HALF, NCOL), BF16),
            pltpu.VMEM((4 * SLAB * HALF, 256), BF16),
            pltpu.VMEM((8, 16, 128), F32),
        ]
        + [dma] * 6
        + [dma((NBAND,))] * 6
        + [dma((len(operands),))],
        compiler_params=pltpu.CompilerParams(
            collective_id=0, has_side_effects=True, vmem_limit_bytes=56 * 2**20
        ),
        name="main_part",
    )(*operands)


def result_kernel(*refs):
    sources, targets, sems = refs[:3], refs[3:6], refs[6]
    copies = [
        pltpu.make_async_copy(a, b, sems.at[i]) for i, (a, b) in enumerate(zip(sources, targets))
    ]
    for copy in copies:
        copy.start()
    for copy in copies:
        copy.wait()


def result_part(*operands):
    anywhere = pl.BlockSpec(memory_space=pl.ANY)
    return pl.pallas_call(
        result_kernel,
        out_shape=tuple(jax.ShapeDtypeStruct(x.shape, x.dtype) for x in operands),
        in_specs=[anywhere] * 3,
        out_specs=(anywhere,) * 3,
        scratch_shapes=[pltpu.SemaphoreType.DMA((3,))],
        compiler_params=pltpu.CompilerParams(vmem_limit_bytes=56 * 2**20),
        name="result_part",
    )(*operands)


def per_device(basis, potential, colmap, hsub_old, inv_factor, angles):
    table = y_table()
    results = main_part(
        basis.reshape(2048, 128),
        colmap.reshape(1, NCOL),
        angles.reshape(8 * ROUNDS, TILE),
        jnp.asarray(z_table().astype(BF16)),
        inv_factor,
        hsub_old.T,
        jnp.asarray(x_table()),
        jnp.asarray(table.astype(BF16)),
        jnp.asarray(table.T.astype(BF16)),
        potential,
        jnp.asarray(z_table_back().astype(BF16)),
    )
    hblock, rotated, bands = result_part(*results)
    return (hblock.reshape(2, 16, 128), rotated, bands.reshape(2, 16, 128))


def solution(mesh):
    in_specs = (P("band", "fft", None), P("fft", None, None), P(), P("band", None), P(), P())
    out_specs = (P("band", "fft", None), P(("band", "fft"), None), P("band", "fft", None))
    return jax.shard_map(
        per_device, mesh=mesh, in_specs=in_specs, out_specs=out_specs, check_vma=False
    )
```

```python
import functools
import math

import jax
import jax.numpy as jnp
import numpy as np
from jax import lax
from jax.experimental import pallas as pl
from jax.experimental.pallas import tpu as pltpu
from jax.sharding import PartitionSpec as P

NG = 192
HALF = 96
NZC = 64
ORDER = 512
GROUP = 128
NCOL = 512
NBAND = 4
NFFT = 32
SLAB = 6
ROUNDS = 30
SPLIT = 15
TILE = 32
F32 = jnp.float32
BF16 = jnp.bfloat16
HIGH = lax.Precision.HIGHEST
MESH = pl.DeviceIdType.MESH
NT = (((1,), (1,)), ((), ()))


def dot(a, b, precision=None):
    return jnp.dot(a, b, precision=precision, preferred_element_type=F32)


def dot_nt(a, b, precision=None):
    return lax.dot_general(a, b, NT, precision=precision, preferred_element_type=F32)


def z_table():
    slot = np.arange(NZC)
    freq = np.where(slot < NZC // 2, slot, slot - NZC) % NG
    table = np.zeros((NFFT, 8, 4, NZC), np.float64)
    z = np.arange(NG).reshape(NFFT, SLAB)
    angle = 2.0 * np.pi * ((z[:, :, None] * freq) % NG) / NG
    table[:, :SLAB, 0] = np.cos(angle)
    table[:, :SLAB, 1] = -np.sin(angle)
    table[:, :SLAB, 2] = np.sin(angle)
    table[:, :SLAB, 3] = np.cos(angle)
    return table.reshape(NFFT * 8, 4 * NZC)


def z_table_back():
    table = z_table().reshape(NFFT, 4, 2, 4 * NZC)
    return np.transpose(table, (1, 0, 2, 3)).reshape(4 * NFFT, 8 * NZC)


def half_angles():
    return 2.0 * np.pi * (((2 * np.arange(HALF)[:, None] + 1) * np.arange(NG)) % (2 * NG)) / (2 * NG)


def x_table():
    angle = half_angles()
    both = np.concatenate([np.cos(angle), np.sin(angle)], 0)
    high = np.asarray(both, np.float32).astype(BF16)
    low = (both - high.astype(np.float64)).astype(BF16)
    table = np.zeros((2 * HALF, 512), BF16)
    table[:, :NG] = high
    table[:, 256 : 256 + NG] = low
    return table


def y_table():
    angle = half_angles().T
    table = np.zeros((256, 256), np.float64)
    table[:NG, :HALF] = np.cos(angle)
    table[:NG, 128 : 128 + HALF] = np.sin(angle)
    return table


def tile_order(turn):
    seat = [0] + [1 + ((m - 1 + turn) % 15) for m in range(1, 16)]
    return seat[:8] + seat[:7:-1]


def pair_step(state, table, r):
    src, dst = state.at[r % 2], state.at[(r + 1) % 2]
    shift = r % TILE
    c = table[0, 8 * r : 8 * r + 8]
    s = table[1, 8 * r : 8 * r + 8]
    a = src[0:8]
    b = src[8:16]
    if shift:
        b = pltpu.roll(b, TILE - shift, 1)
    a, b = c * a - s * b, s * a + c * b
    if shift:
        b = pltpu.roll(b, shift, 1)
    dst[0:1] = a[0:1]
    dst[1:7] = a[2:8]
    dst[7:8] = b[7:8]
    dst[8:9] = a[1:2]
    dst[9:16] = b[0:7]


def turn_angles(angles, turned):
    ang = jnp.concatenate([angles[...], jnp.zeros((240, 128 - TILE), F32)], 1)
    ang = jnp.concatenate([ang, jnp.zeros((16, 128), F32)], 0)
    turned[0] = jnp.cos(ang).T[:TILE]
    turned[1] = jnp.sin(ang).T[:TILE]


def angle_tables(turned, table, start, stop):
    for i in range(2):
        for q in range(8 * start, 8 * stop):
            table[i, q] = jnp.broadcast_to(turned[i, :, q : q + 1], (TILE, 128))


def rotate_factor(band, state, table, inv, factor):
    own = inv[:, pl.ds(pl.multiple_of(band * GROUP, GROUP), GROUP)]
    for p, tile in enumerate(tile_order(0)):
        state[0, p] = own[TILE * tile : TILE * tile + TILE]
    for r in range(ROUNDS):
        pair_step(state, table, r)
    factor[...] = natural(state, 0)


def natural(state, which):
    return jnp.concatenate([state[which, p] for p in list(range(8)) + list(range(15, 7, -1))], 0)


def couple(me, hsub, factor, factor_wide, y_own, z_buf, sendz, sendr):
    for j in range(4):
        factor_wide[:, GROUP * j : GROUP * j + GROUP] = factor[pl.ds(j, 128, stride=4), :].astype(BF16)
    line = lax.broadcasted_iota(jnp.int32, (128, ORDER), 0)
    column = lax.broadcasted_iota(jnp.int32, (128, ORDER), 1)
    target = ((line >> 3) * NFFT + me) * 4 + (line & 7)
    target = jnp.where((line < 32) & ((line & 7) < 4), target, -1)
    target = jnp.where((line >= 32) & (line < 40), line - 32, target)
    own = dot((column == target).astype(F32).astype(BF16), factor[...].astype(BF16))
    y_own[...] = own[:40]
    z_old = dot_nt(hsub[...].astype(BF16), own.astype(BF16))
    z_buf[...] = jnp.zeros_like(z_buf)
    for b in range(NBAND):
        z_buf[b * GROUP : b * GROUP + 126, :] = z_old[b * 126 : (b + 1) * 126, :]
    z_rows = z_buf[...].T[:32]
    for b in range(NBAND):
        sendz[b] = z_rows[:, GROUP * b : GROUP * b + GROUP]
    sendr[...] = factor[...].T[120:128]


def vector_weights(basis, y_own, w_buf, bands_part):
    weights = y_own[32:40, :].astype(BF16)
    spread_row = lax.broadcasted_iota(jnp.int32, (GROUP, 2048), 0)
    spread_lane = lax.broadcasted_iota(jnp.int32, (GROUP, 2048), 1)
    spread = (spread_row == (spread_lane >> 4)).astype(F32).astype(BF16)
    wide = dot(weights, spread)
    own_row = lax.broadcasted_iota(jnp.int32, (16, 2048), 0)
    own_lane = lax.broadcasted_iota(jnp.int32, (16, 2048), 1)
    keep = own_row == (own_lane & 15)
    for k in range(8):
        w_buf[16 * k : 16 * k + 16, :] = jnp.where(keep, wide[k : k + 1], 0.0).astype(BF16)
    bands_part[...] = dot(w_buf[...], basis[...]).astype(BF16).reshape(NBAND, 32, 128)


def split(value):
    high = value.astype(BF16)
    return high, (value - high.astype(F32)).astype(BF16)


def fold_potential(potential, folded):
    y_row = lax.broadcasted_iota(jnp.int32, (NG, 256), 0)
    y_lane = lax.broadcasted_iota(jnp.int32, (NG, 256), 1)
    wanted = jnp.where(y_lane < 128, HALF + y_lane, HALF - 1 + 128 - y_lane)
    wanted = jnp.where((y_lane & 127) < HALF, wanted, -1)
    order_y = (y_row == wanted).astype(F32).astype(BF16)
    x_row = lax.broadcasted_iota(jnp.int32, (HALF, HALF), 0)
    x_lane = lax.broadcasted_iota(jnp.int32, (HALF, HALF), 1)
    order_x = (x_row + x_lane == HALF - 1).astype(F32).astype(BF16)
    high, low = split(potential[...].reshape(SLAB * NG, NG))
    value = dot(high, order_y) + dot(low, order_y)
    for z in range(SLAB):
        high, low = split(value[NG * z : NG * z + HALF])
        low_side = dot(order_x, high) + dot(order_x, low)
        high_side = value[NG * z + HALF : NG * z + NG]
        for v in range(2):
            folded[z, 0, v] = high_side[:, 128 * v : 128 * v + 128]
            folded[z, 1, v] = low_side[:, 128 * v : 128 * v + 128]


def times_potential(q, v):
    (cc, cs), (sc, ss) = q

    def add(m, n):
        return m[0] + n[0], m[1] + n[1]

    def sub(m, n):
        return m[0] - n[0], m[1] - n[1]

    def by_i(m):
        return -m[1], m[0]

    def scaled(m, w):
        return m[0] * w, m[1] * w

    e1, o1 = sub(cc, ss), by_i(add(sc, cs))
    e2, o2 = add(cc, ss), by_i(sub(sc, cs))
    high = scaled(add(e1, o1), v[0][0])
    low = scaled(sub(e1, o1), v[1][1])
    right = scaled(add(e2, o2), v[0][1])
    left = scaled(sub(e2, o2), v[1][0])
    s1, d1, s2, d2 = add(high, low), sub(high, low), add(right, left), sub(right, left)
    odd_x, odd_y = add(d1, d2), sub(d1, d2)
    return (add(s1, s2), (odd_y[1], -odd_y[0])), ((odd_x[1], -odd_x[0]), sub(s2, s1))


def hops(steps):
    z_hi, core, z_lo, x, y = steps
    return (1 if z_lo else 2 * z_hi) + min(x, 4 - x) + min(y, 4 - y)


def all_steps(bands):
    found = [
        (z_hi, core, z_lo, x, y)
        for z_hi in range(bands)
        for core in range(bands)
        for z_lo in range(2)
        for x in range(4)
        for y in range(4)
    ]
    found.remove((0, 0, 0, 0, 0))
    return sorted(found, key=lambda s: -hops(s))


def main_kernel(
    basis_in, columns_in, angles_in, tz_in, inv_in, hsub_in, tx_in, ty_in, ty_t_in, potential_in, tb_in,
    hblock_out, rotated_out, bands_out,
    basis, columns, angles, tz, inv, hsub, tx, ty, ty_t, potential, tb,
    state, turned, table, factor, factor_wide, y_own, z_buf, sendz, recvz, sendr, recvr, w_buf, bands_part,
    send1, recv1, send2, recv2, send3, recv3, new_own, news, hall, recvb, sendf, recvf,
    q_buf, u_buf, a_cos, a_sin, phase, phase_out, folded, right1, right2, radius, coef, d_buf, p_buf, g_buf,
    s1, r1, s2, r2, s3, r3, sh, rh, sb, rb, sf, rf, sz, rz, sr, rr, loads,
):
    band = lax.axis_index("band")
    me = lax.axis_index("fft")

    inputs = (
        (basis_in, basis), (tz_in, tz), (angles_in, angles), (columns_in, columns), (tx_in, tx),
        (ty_in, ty), (ty_t_in, ty_t), (inv_in, inv), (potential_in, potential), (tb_in, tb), (hsub_in, hsub),
    )
    copies = [pltpu.make_async_copy(a, b, loads.at[i]) for i, (a, b) in enumerate(inputs)]
    copies[0].start()
    copies[1].start()

    def peer(steps):
        z_hi, core, z_lo, x, y = steps
        to_fft = (((me >> 4) ^ z_lo) << 4) | ((((me >> 2) + x) & 3) << 2) | ((me + y) & 3)
        return (band ^ (2 * z_hi + core), to_fft)

    near, every = all_steps(1), all_steps(2)

    barrier = pltpu.get_barrier_semaphore()

    for steps in near:
        pl.semaphore_signal(barrier, inc=1, device_id=peer(steps), device_id_type=MESH)
    for i in range(1, NBAND):
        pl.semaphore_signal(
            barrier, inc=1, device_id=(lax.rem(band + i, NBAND), me), device_id_type=MESH
        )

    for copy in copies[2:]:
        copy.start()

    def fft_start(send, recv, ssem, rsem, whole):
        for steps in near:
            to = peer(steps)
            pltpu.make_async_remote_copy(
                src_ref=send if whole else send.at[to[1]],
                dst_ref=recv.at[me],
                send_sem=ssem,
                recv_sem=rsem,
                device_id=to,
                device_id_type=MESH,
            ).start()

    def fft_all(send, recv, ssem, rsem, whole):
        part = recv.at[pl.ds(0, NFFT - 1)]
        return pltpu.make_async_remote_copy(
            src_ref=part,
            dst_ref=part,
            send_sem=ssem,
            recv_sem=rsem,
            device_id=(band, lax.rem(me + 1, NFFT)),
            device_id_type=MESH,
        )

    def fft_wait_recv(*args):
        fft_all(*args).wait_recv()

    def fft_wait_send(*args):
        fft_all(*args).wait_send()

    def band_copy(i, src, dst, ssem, rsem):
        to = lax.rem(band + i, NBAND)
        return pltpu.make_async_remote_copy(
            src_ref=src(to),
            dst_ref=dst.at[band],
            send_sem=ssem.at[i],
            recv_sem=rsem.at[band],
            device_id=(to, me),
            device_id_type=MESH,
        )

    def band_arrival(i, src, dst, ssem, rsem):
        source = lax.rem(band + NBAND - i, NBAND)
        return pltpu.make_async_remote_copy(
            src_ref=src(source),
            dst_ref=dst.at[source],
            send_sem=ssem.at[i],
            recv_sem=rsem.at[source],
            device_id=(source, me),
            device_id_type=MESH,
        )

    copies[0].wait()
    copies[1].wait()
    new = basis[2016:2048, :]
    none = jnp.zeros((16, 128), BF16)
    right = jnp.concatenate(
        [
            jnp.concatenate([new[0:16], none], 1),
            jnp.concatenate([none, new[0:16]], 1),
            jnp.concatenate([new[16:32], none], 1),
            jnp.concatenate([none, new[16:32]], 1),
            jnp.zeros((64, 256), BF16),
        ],
        0,
    )
    send1[...] = dot_nt(tz[...], right).reshape(NFFT, 8, 128)
    first = (send1, recv1, s1, r1, False)
    pl.semaphore_wait(barrier, NFFT - 1 + NBAND - 1)
    fft_start(*first)
    recv1[pl.ds(me, 1)] = send1[pl.ds(me, 1)]

    copies[2].wait()
    turn_angles(angles, turned)
    angle_tables(turned, table, 0, SPLIT)

    new_args = (lambda to: new_own, news, sh, rh)
    new_own[...] = basis[2016:2048, :]
    for i in range(1, NBAND):
        band_copy(i, *new_args).start()
    news[pl.ds(band, 1)] = new_own[...].reshape(1, 32, 128)

    for i in range(3, 7):
        copies[i].wait()
    position = columns[...].astype(F32)
    pos_x = jnp.floor((position + 0.5) * (1.0 / NG))
    pos_y = position - NG * pos_x
    k_row = lax.broadcasted_iota(jnp.int32, (256, NCOL), 0).astype(F32)
    hot_x = (k_row == pos_x).astype(F32).astype(BF16)
    hot_y = (k_row == pos_y).astype(F32).astype(BF16)
    a_both = dot(tx[...], jnp.concatenate([hot_x, hot_x], 0))
    a_cos[...] = a_both[:HALF]
    a_sin[...] = a_both[HALF:]
    right2[...] = dot(ty_t[...], hot_y).astype(BF16)
    wide_y = jnp.broadcast_to(pos_y, (128, NCOL)).T
    lane_k = lax.broadcasted_iota(jnp.int32, (NCOL, 128), 1).astype(F32)
    hot_yt = jnp.concatenate(
        [(wide_y == lane_k).astype(F32), (wide_y == lane_k + 128.0).astype(F32)], 1
    ).astype(BF16)
    right1[...] = dot(hot_yt, ty[...]).astype(BF16)
    turns = (pos_x + pos_y) * (NG - 1.0)
    turns = turns - (2.0 * NG) * jnp.floor((turns + 0.5) * (0.5 / NG))
    center = jnp.broadcast_to(turns * (math.pi / NG), (8, NCOL))
    phase[0] = jnp.cos(center)
    phase[1] = jnp.sin(center)
    for j in range(4):
        phase_out[:, 4 * j : 4 * j + 4, :] = phase[:, 0:4, 128 * j : 128 * j + 128]
    freq_x = jnp.where(pos_x < NG // 2, pos_x, pos_x - NG)
    freq_y = jnp.where(pos_y < NG // 2, pos_y, pos_y - NG)
    radius[...] = jnp.broadcast_to(freq_x * freq_x + freq_y * freq_y, (128, NCOL)).T
    g_buf[...] = jnp.zeros_like(g_buf)

    for i in range(7, 11):
        copies[i].wait()
    fold_potential(potential, folded)
    fft_wait_recv(*first)

    lanes = lax.broadcasted_iota(jnp.int32, (8, 128), 1)
    for q in range(4):
        for j in range(4):
            total = jnp.zeros((8, 128), F32)
            for t in range(8):
                piece = recv1[8 * j + t]
                move = (16 * t - 16 * q) % 128
                if move:
                    piece = pltpu.roll(piece, move, 1)
                total = jnp.where((lanes >> 4) == t, piece, total)
            coef[q, :, 128 * j : 128 * j + 128] = total

    def mix(v):
        old_re, old_im = coef[2 * v], coef[2 * v + 1]
        coef[2 * v] = old_re * phase[0] - old_im * phase[1]
        coef[2 * v + 1] = old_re * phase[1] + old_im * phase[0]

    def unmix(v):
        for q in (2 * v, 2 * v + 4):
            new_re, new_im = g_buf[q], g_buf[q + 1]
            g_buf[q] = new_re * phase_out[0] + new_im * phase_out[1]
            g_buf[q + 1] = new_im * phase_out[0] - new_re * phase_out[1]

    def block(z, a, i):
        return pl.ds(HALF * (4 * z + 2 * a + i), HALF)

    def plane(z):
        return pl.ds(4 * HALF * z, 4 * HALF)

    def spread(v, z):
        for a, part in enumerate((a_cos, a_sin)):
            for i in range(2):
                d_buf[block(z, a, i), :] = (part[...] * coef[2 * v + i, z : z + 1, :]).astype(BF16)

    def to_field(v, z):
        q_buf[plane(z), :] = dot(d_buf[plane(z), :], right1[...])

    def multiply(v, z):
        q = [
            [tuple(q_buf[block(z, a, i), 128 * b : 128 * b + 128] for i in range(2)) for b in range(2)]
            for a in range(2)
        ]
        back = times_potential(q, [[folded[z, u, w] for w in range(2)] for u in range(2)])
        for a in range(2):
            for b in range(2):
                for i in range(2):
                    p_buf[block(z, a, i), 128 * b : 128 * b + 128] = back[a][b][i].astype(BF16)

    def from_field(v, z):
        u_buf[plane(z), :] = dot(p_buf[plane(z), :], right2[...])

    def collect(v, z):
        for i in range(2):
            total = jnp.sum(
                a_cos[...] * u_buf[block(z, 0, i), :] + a_sin[...] * u_buf[block(z, 1, i), :],
                axis=0,
                keepdims=True,
            )
            for j in range(4):
                g_buf[4 * (z % 2) + 2 * v + i, 4 * j + z // 2 : 4 * j + z // 2 + 1, :] = total[
                    :, 128 * j : 128 * j + 128
                ]

    steps = (spread, to_field, multiply, from_field, collect)

    for v in range(2):
        mix(v)
    for t in range(2 * SLAB + len(steps) - 1):
        for s, step in enumerate(steps):
            if 0 <= t - s < 2 * SLAB:
                step((t - s) // SLAB, (t - s) % SLAB)
    for v in range(2):
        unmix(v)

    volume = 1.0 / float(NG) ** 3
    wide_lanes = lax.broadcasted_iota(jnp.int32, (16, 128), 1)
    for t in range(8):
        total = jnp.zeros((16, 128), F32)
        for q in range(8):
            piece = g_buf[q]
            move = (16 * q - 16 * t) % 128
            if move:
                piece = pltpu.roll(piece, move, 1)
            total = jnp.where((wide_lanes >> 4) == q, piece, total)
        total = total * volume
        for j in range(4):
            send2[8 * j + t] = total[4 * j : 4 * j + 4]
    own = band * NFFT + me

    for steps in every:
        to = peer(steps)
        pltpu.make_async_remote_copy(
            src_ref=send2.at[to[1], pl.ds(0, 3)],
            dst_ref=recv2.at[own, pl.ds(0, 3)],
            send_sem=s2,
            recv_sem=r2,
            device_id=to,
            device_id_type=MESH,
        ).start()
    back_part = recv2.at[pl.ds(0, NBAND * NFFT - 1), pl.ds(0, 3)]
    back_all = pltpu.make_async_remote_copy(
        src_ref=back_part,
        dst_ref=back_part,
        send_sem=s2,
        recv_sem=r2,
        device_id=(band, lax.rem(me + 1, NFFT)),
        device_id_type=MESH,
    )
    recv2[pl.ds(own, 1)] = send2[pl.ds(me, 1)]
    angle_tables(turned, table, SPLIT, ROUNDS)
    rotate_factor(band, state, table, inv, factor)
    couple(me, hsub, factor, factor_wide, y_own, z_buf, sendz, sendr)
    z_args = (lambda to: sendz.at[to], recvz, sz, rz)
    row_args = (lambda to: sendr, recvr, sr, rr)
    for i in range(1, NBAND):
        band_copy(i, *z_args).start()
    for i in range(1, NBAND):
        band_copy(i, *row_args).start()
    recvz[pl.ds(band, 1)] = sendz[pl.ds(band, 1)]
    recvr[pl.ds(band, 1)] = sendr[...].reshape(1, 8, ORDER)

    vector_weights(basis, y_own, w_buf, bands_part)
    bands_args = (lambda to: bands_part.at[to], recvb, sb, rb)
    for i in range(1, NBAND):
        band_copy(i, *bands_args).start()
    recvb[pl.ds(band, 1)] = bands_part[pl.ds(band, 1)]
    for i in range(1, NBAND):
        band_arrival(i, *new_args).wait_recv()
    slot = lax.broadcasted_iota(jnp.int32, (16, 128), 1) & (NZC - 1)
    freq_z = jnp.where(slot < NZC // 2, slot, slot - NZC).astype(F32)
    own_radius = radius[pl.ds(pl.multiple_of(me * 16, 16), 16), :]
    kinetic = (own_radius + freq_z * freq_z) / (2.0 * (NG // 4) ** 2)

    back_all.wait_recv()
    slabs = []
    for b in range(NBAND):
        parts = [recv2[NFFT * b : NFFT * b + NFFT, r, :] for r in range(3)]
        parts.append(jnp.zeros((NFFT, 128), F32))
        slabs.append(jnp.concatenate(parts, 0).T.astype(BF16))
    local = dot(jnp.concatenate(slabs, 0), tb[...])
    for b in range(NBAND):
        for v in range(2):
            term = jnp.zeros((16, 128), F32)
            for n in range(2):
                row, lane = 128 * b + 64 * n + 32 * v, 256 * n
                term = term + local[row : row + 16, lane : lane + 128]
                term = term + local[row + 16 : row + 32, lane + 128 : lane + 256]
            coeffs = news[b, 16 * v : 16 * v + 16, :].astype(F32)
            hall[b, 16 * v : 16 * v + 16, :] = (kinetic * coeffs + term).astype(BF16)

    pairs = dot_nt(basis[...], hall[...].reshape(128, 128))
    pair_row = lax.broadcasted_iota(jnp.int32, (2048, 128), 0)
    pair_lane = lax.broadcasted_iota(jnp.int32, (2048, 128), 1)
    pairs = jnp.where(((pair_row ^ pair_lane) & 15) == 0, pairs, 0.0)
    by_group = jnp.sum(pairs.reshape(GROUP, 16, 128), axis=1)
    pick_row = lax.broadcasted_iota(jnp.int32, (128, 512), 0)
    pick_lane = lax.broadcasted_iota(jnp.int32, (128, 512), 1)
    slot_of = pick_lane & 127
    picked = ((slot_of >> 3) == (pick_lane >> 7)) & ((slot_of & 7) == (pick_row >> 4))
    pick = picked.astype(F32).astype(BF16)
    high, low_part = split(by_group)
    fresh = dot(high, pick) + dot(low_part, pick)
    fresh = jnp.concatenate([fresh[:, 128 * j : 128 * j + 128] for j in range(4)], 0).astype(BF16)
    send3[...] = dot(factor_wide[...], fresh).reshape(NBAND * NFFT, 1, 128)
    for steps in every:
        to = peer(steps)
        pltpu.make_async_remote_copy(
            src_ref=send3.at[to[0] * NFFT + to[1]],
            dst_ref=recv3.at[own],
            send_sem=s3,
            recv_sem=r3,
            device_id=to,
            device_id_type=MESH,
        ).start()
    sum_part = recv3.at[pl.ds(0, NBAND * NFFT - 1)]
    sum_all = pltpu.make_async_remote_copy(
        src_ref=sum_part,
        dst_ref=sum_part,
        send_sem=s3,
        recv_sem=r3,
        device_id=(band, lax.rem(me + 1, NFFT)),
        device_id_type=MESH,
    )
    recv3[pl.ds(own, 1)] = send3[pl.ds(own, 1)]
    for i in range(1, NBAND):
        band_arrival(i, *z_args).wait_recv()
    z_sum = recvz[0] + recvz[1] + recvz[2] + recvz[3]
    old = dot_nt(z_sum.astype(BF16), factor[...].astype(BF16))
    sendf[...] = old.reshape(NBAND, 8, ORDER)
    final_args = (lambda to: sendf.at[to], recvf, sf, rf)
    for i in range(1, NBAND):
        band_copy(i, *final_args).start()
    recvf[pl.ds(band, 1)] = sendf[pl.ds(band, 1)]

    hblock_out[...] = hall[pl.ds(band, 1)].reshape(32, 128)
    for i in range(1, NBAND):
        band_arrival(i, *bands_args).wait_recv()
    bands_total = recvb[0].astype(F32)
    for b in range(1, NBAND):
        bands_total = bands_total + recvb[b].astype(F32)
    bands_out[...] = bands_total.astype(BF16)
    for i in range(1, NBAND):
        band_arrival(i, *final_args).wait_recv()
    old_part = recvf[0] + recvf[1] + recvf[2] + recvf[3]
    for i in range(1, NBAND):
        band_arrival(i, *row_args).wait_recv()
    new_rows = jnp.concatenate([recvr[b, 6:8, :] for b in range(NBAND)], 0)
    wide_rows = jnp.concatenate([new_rows] * 4 + [jnp.zeros((96, ORDER), F32)], 0).astype(BF16)
    fft_wait_send(*first)
    back_all.wait_send()
    for i in range(1, NBAND):
        band_copy(i, *bands_args).wait_send()
        band_copy(i, *new_args).wait_send()
        band_copy(i, *final_args).wait_send()
        band_copy(i, *z_args).wait_send()
        band_copy(i, *row_args).wait_send()

    sum_all.wait_recv()
    total = jnp.sum(recv3[...].reshape(NBAND * NFFT, 128), axis=0, keepdims=True)
    total = total * (1.0 / math.sqrt(2 * NCOL * NZC))
    spread_rows = lax.broadcasted_iota(jnp.int32, (8, 128), 0)
    total = jnp.where((lanes >> 3) == spread_rows, total, 0.0)
    new_part = dot(total.astype(BF16), wide_rows)
    rotated_out[...] = (old_part + new_part)[0:4]
    sum_all.wait_send()


def main_part(*operands):
    vmem = pl.BlockSpec(memory_space=pltpu.VMEM)
    dma = pltpu.SemaphoreType.DMA
    return pl.pallas_call(
        main_kernel,
        out_shape=(
            jax.ShapeDtypeStruct((32, 128), BF16),
            jax.ShapeDtypeStruct((4, ORDER), F32),
            jax.ShapeDtypeStruct((32, 128), BF16),
        ),
        in_specs=[pl.BlockSpec(memory_space=pl.ANY)] * len(operands),
        out_specs=(vmem,) * 3,
        scratch_shapes=[pltpu.VMEM(x.shape, x.dtype) for x in operands]
        + [
            pltpu.VMEM((2, 16, TILE, 128), F32),
            pltpu.VMEM((2, TILE, 256), F32),
            pltpu.VMEM((2, 8 * ROUNDS, TILE, 128), F32),
            pltpu.VMEM((ORDER, 128), F32),
            pltpu.VMEM((128, ORDER), BF16),
            pltpu.VMEM((40, GROUP), F32),
            pltpu.VMEM((ORDER, 128), F32),
            pltpu.VMEM((NBAND, 32, GROUP), F32),
            pltpu.VMEM((NBAND, 32, GROUP), F32),
            pltpu.VMEM((8, ORDER), F32),
            pltpu.VMEM((NBAND, 8, ORDER), F32),
            pltpu.VMEM((128, 2048), BF16),
            pltpu.VMEM((NBAND, 32, 128), BF16),
            pltpu.VMEM((NFFT, 8, 128), F32),
            pltpu.VMEM((NFFT, 8, 128), F32),
            pltpu.VMEM((NFFT, 4, 128), F32),
            pltpu.VMEM((NBAND * NFFT, 4, 128), F32),
            pltpu.VMEM((NBAND * NFFT, 1, 128), F32),
            pltpu.VMEM((NBAND * NFFT, 1, 128), F32),
            pltpu.VMEM((32, 128), BF16),
            pltpu.VMEM((NBAND, 32, 128), BF16),
            pltpu.VMEM((NBAND, 32, 128), BF16),
            pltpu.VMEM((NBAND, 32, 128), BF16),
            pltpu.VMEM((NBAND, 8, ORDER), F32),
            pltpu.VMEM((NBAND, 8, ORDER), F32),
            pltpu.VMEM((4 * SLAB * HALF, 256), F32),
            pltpu.VMEM((4 * SLAB * HALF, NCOL), F32),
            pltpu.VMEM((HALF, NCOL), F32),
            pltpu.VMEM((HALF, NCOL), F32),
            pltpu.VMEM((2, 8, NCOL), F32),
            pltpu.VMEM((2, 16, 128), F32),
            pltpu.VMEM((SLAB, 2, 2, HALF, 128), F32),
            pltpu.VMEM((NCOL, 256), BF16),
            pltpu.VMEM((256, NCOL), BF16),
            pltpu.VMEM((NCOL, 128), F32),
            pltpu.VMEM((4, 8, NCOL), F32),
            pltpu.VMEM((4 * SLAB * HALF, NCOL), BF16),
            pltpu.VMEM((4 * SLAB * HALF, 256), BF16),
            pltpu.VMEM((8, 16, 128), F32),
        ]
        + [dma] * 6
        + [dma((NBAND,))] * 10
        + [dma((len(operands),))],
        compiler_params=pltpu.CompilerParams(
            collective_id=0, has_side_effects=True, vmem_limit_bytes=56 * 2**20
        ),
        name="main_part",
    )(*operands)


def result_kernel(*refs):
    sources, targets, sems = refs[:3], refs[3:6], refs[6]
    copies = [
        pltpu.make_async_copy(a, b, sems.at[i]) for i, (a, b) in enumerate(zip(sources, targets))
    ]
    for copy in copies:
        copy.start()
    for copy in copies:
        copy.wait()


def result_part(*operands):
    anywhere = pl.BlockSpec(memory_space=pl.ANY)
    return pl.pallas_call(
        result_kernel,
        out_shape=tuple(jax.ShapeDtypeStruct(x.shape, x.dtype) for x in operands),
        in_specs=[anywhere] * 3,
        out_specs=(anywhere,) * 3,
        scratch_shapes=[pltpu.SemaphoreType.DMA((3,))],
        compiler_params=pltpu.CompilerParams(vmem_limit_bytes=56 * 2**20),
        name="result_part",
    )(*operands)


def per_device(basis, potential, colmap, hsub_old, inv_factor, angles):
    table = y_table()
    results = main_part(
        basis.reshape(2048, 128),
        colmap.reshape(1, NCOL),
        angles.reshape(8 * ROUNDS, TILE),
        jnp.asarray(z_table().astype(BF16)),
        inv_factor,
        hsub_old.T,
        jnp.asarray(x_table()),
        jnp.asarray(table.astype(BF16)),
        jnp.asarray(table.T.astype(BF16)),
        potential,
        jnp.asarray(z_table_back().astype(BF16)),
    )
    hblock, rotated, bands = result_part(*results)
    return (hblock.reshape(2, 16, 128), rotated, bands.reshape(2, 16, 128))


def solution(mesh):
    in_specs = (P("band", "fft", None), P("fft", None, None), P(), P("band", None), P(), P())
    out_specs = (P("band", "fft", None), P(("band", "fft"), None), P("band", "fft", None))
    return jax.shard_map(
        per_device, mesh=mesh, in_specs=in_specs, out_specs=out_specs, check_vma=False
    )
```

```python
import functools
import math

import jax
import jax.numpy as jnp
import numpy as np
from jax import lax
from jax.experimental import pallas as pl
from jax.experimental.pallas import tpu as pltpu
from jax.sharding import PartitionSpec as P

NG = 192
HALF = 96
NZC = 64
ORDER = 512
GROUP = 128
NCOL = 512
NBAND = 4
NFFT = 32
SLAB = 6
ROUNDS = 30
SPLIT = 15
TILE = 32
F32 = jnp.float32
BF16 = jnp.bfloat16
HIGH = lax.Precision.HIGHEST
MESH = pl.DeviceIdType.MESH
NT = (((1,), (1,)), ((), ()))


def dot(a, b, precision=None):
    return jnp.dot(a, b, precision=precision, preferred_element_type=F32)


def dot_nt(a, b, precision=None):
    return lax.dot_general(a, b, NT, precision=precision, preferred_element_type=F32)


def z_table():
    slot = np.arange(NZC)
    freq = np.where(slot < NZC // 2, slot, slot - NZC) % NG
    table = np.zeros((NFFT, 8, 4, NZC), np.float64)
    z = np.arange(NG).reshape(NFFT, SLAB)
    angle = 2.0 * np.pi * ((z[:, :, None] * freq) % NG) / NG
    table[:, :SLAB, 0] = np.cos(angle)
    table[:, :SLAB, 1] = -np.sin(angle)
    table[:, :SLAB, 2] = np.sin(angle)
    table[:, :SLAB, 3] = np.cos(angle)
    return table.reshape(NFFT * 8, 4 * NZC)


def z_table_back():
    table = z_table().reshape(NFFT, 4, 2, 4 * NZC)
    return np.transpose(table, (1, 0, 2, 3)).reshape(4 * NFFT, 8 * NZC)


def half_angles():
    return 2.0 * np.pi * (((2 * np.arange(HALF)[:, None] + 1) * np.arange(NG)) % (2 * NG)) / (2 * NG)


def x_table():
    angle = half_angles()
    both = np.concatenate([np.cos(angle), np.sin(angle)], 0)
    high = np.asarray(both, np.float32).astype(BF16)
    low = (both - high.astype(np.float64)).astype(BF16)
    table = np.zeros((2 * HALF, 512), BF16)
    table[:, :NG] = high
    table[:, 256 : 256 + NG] = low
    return table


def y_table():
    angle = half_angles().T
    table = np.zeros((256, 256), np.float64)
    table[:NG, :HALF] = np.cos(angle)
    table[:NG, 128 : 128 + HALF] = np.sin(angle)
    return table


def tile_order(turn):
    seat = [0] + [1 + ((m - 1 + turn) % 15) for m in range(1, 16)]
    return seat[:8] + seat[:7:-1]


def pair_step(state, table, r):
    src, dst = state.at[r % 2], state.at[(r + 1) % 2]
    shift = r % TILE
    c = table[0, 8 * r : 8 * r + 8]
    s = table[1, 8 * r : 8 * r + 8]
    a = src[0:8]
    b = src[8:16]
    if shift:
        b = pltpu.roll(b, TILE - shift, 1)
    a, b = c * a - s * b, s * a + c * b
    if shift:
        b = pltpu.roll(b, shift, 1)
    dst[0:1] = a[0:1]
    dst[1:7] = a[2:8]
    dst[7:8] = b[7:8]
    dst[8:9] = a[1:2]
    dst[9:16] = b[0:7]


def turn_angles(angles, turned):
    ang = jnp.concatenate([angles[...], jnp.zeros((240, 128 - TILE), F32)], 1)
    ang = jnp.concatenate([ang, jnp.zeros((16, 128), F32)], 0)
    turned[0] = jnp.cos(ang).T[:TILE]
    turned[1] = jnp.sin(ang).T[:TILE]


def angle_tables(turned, table, start, stop):
    for i in range(2):
        for q in range(8 * start, 8 * stop):
            table[i, q] = jnp.broadcast_to(turned[i, :, q : q + 1], (TILE, 128))


def rotate_factor(band, state, table, inv, factor):
    own = inv[:, pl.ds(pl.multiple_of(band * GROUP, GROUP), GROUP)]
    for p, tile in enumerate(tile_order(0)):
        state[0, p] = own[TILE * tile : TILE * tile + TILE]
    for r in range(ROUNDS):
        pair_step(state, table, r)
    factor[...] = natural(state, 0)


def natural(state, which):
    return jnp.concatenate([state[which, p] for p in list(range(8)) + list(range(15, 7, -1))], 0)


def couple(me, hsub, factor, factor_wide, y_own, z_buf, sendz, sendr):
    for j in range(4):
        factor_wide[:, GROUP * j : GROUP * j + GROUP] = factor[pl.ds(j, 128, stride=4), :].astype(BF16)
    line = lax.broadcasted_iota(jnp.int32, (128, ORDER), 0)
    column = lax.broadcasted_iota(jnp.int32, (128, ORDER), 1)
    target = ((line >> 3) * NFFT + me) * 4 + (line & 7)
    target = jnp.where((line < 32) & ((line & 7) < 4), target, -1)
    target = jnp.where((line >= 32) & (line < 40), line - 32, target)
    own = dot((column == target).astype(F32).astype(BF16), factor[...].astype(BF16))
    y_own[...] = own[:40]
    z_old = dot_nt(hsub[...].astype(BF16), own.astype(BF16))
    z_buf[...] = jnp.zeros_like(z_buf)
    for b in range(NBAND):
        z_buf[b * GROUP : b * GROUP + 126, :] = z_old[b * 126 : (b + 1) * 126, :]
    z_rows = z_buf[...].T[:32]
    for b in range(NBAND):
        sendz[b] = z_rows[:, GROUP * b : GROUP * b + GROUP]
    sendr[...] = factor[...].T[120:128]


def vector_weights(basis, y_own, w_buf, bands_part):
    weights = y_own[32:40, :].astype(BF16)
    spread_row = lax.broadcasted_iota(jnp.int32, (GROUP, 2048), 0)
    spread_lane = lax.broadcasted_iota(jnp.int32, (GROUP, 2048), 1)
    spread = (spread_row == (spread_lane >> 4)).astype(F32).astype(BF16)
    wide = dot(weights, spread)
    own_row = lax.broadcasted_iota(jnp.int32, (16, 2048), 0)
    own_lane = lax.broadcasted_iota(jnp.int32, (16, 2048), 1)
    keep = own_row == (own_lane & 15)
    for k in range(8):
        w_buf[16 * k : 16 * k + 16, :] = jnp.where(keep, wide[k : k + 1], 0.0).astype(BF16)
    bands_part[...] = dot(w_buf[...], basis[...]).astype(BF16).reshape(NBAND, 32, 128)


def split(value):
    high = value.astype(BF16)
    return high, (value - high.astype(F32)).astype(BF16)


def fold_potential(potential, folded):
    y_row = lax.broadcasted_iota(jnp.int32, (NG, 256), 0)
    y_lane = lax.broadcasted_iota(jnp.int32, (NG, 256), 1)
    wanted = jnp.where(y_lane < 128, HALF + y_lane, HALF - 1 + 128 - y_lane)
    wanted = jnp.where((y_lane & 127) < HALF, wanted, -1)
    order_y = (y_row == wanted).astype(F32).astype(BF16)
    x_row = lax.broadcasted_iota(jnp.int32, (HALF, HALF), 0)
    x_lane = lax.broadcasted_iota(jnp.int32, (HALF, HALF), 1)
    order_x = (x_row + x_lane == HALF - 1).astype(F32).astype(BF16)
    high, low = split(potential[...].reshape(SLAB * NG, NG))
    value = dot(high, order_y) + dot(low, order_y)
    for z in range(SLAB):
        high, low = split(value[NG * z : NG * z + HALF])
        low_side = dot(order_x, high) + dot(order_x, low)
        high_side = value[NG * z + HALF : NG * z + NG]
        for v in range(2):
            folded[z, 0, v] = high_side[:, 128 * v : 128 * v + 128]
            folded[z, 1, v] = low_side[:, 128 * v : 128 * v + 128]


def times_potential(q, v):
    (cc, cs), (sc, ss) = q

    def add(m, n):
        return m[0] + n[0], m[1] + n[1]

    def sub(m, n):
        return m[0] - n[0], m[1] - n[1]

    def by_i(m):
        return -m[1], m[0]

    def scaled(m, w):
        return m[0] * w, m[1] * w

    e1, o1 = sub(cc, ss), by_i(add(sc, cs))
    e2, o2 = add(cc, ss), by_i(sub(sc, cs))
    high = scaled(add(e1, o1), v[0][0])
    low = scaled(sub(e1, o1), v[1][1])
    right = scaled(add(e2, o2), v[0][1])
    left = scaled(sub(e2, o2), v[1][0])
    s1, d1, s2, d2 = add(high, low), sub(high, low), add(right, left), sub(right, left)
    odd_x, odd_y = add(d1, d2), sub(d1, d2)
    return (add(s1, s2), (odd_y[1], -odd_y[0])), ((odd_x[1], -odd_x[0]), sub(s2, s1))


def hops(steps):
    z_hi, core, z_lo, x, y = steps
    return (1 if z_lo else 2 * z_hi) + min(x, 4 - x) + min(y, 4 - y)


def all_steps(bands):
    found = [
        (z_hi, core, z_lo, x, y)
        for z_hi in range(bands)
        for core in range(bands)
        for z_lo in range(2)
        for x in range(4)
        for y in range(4)
    ]
    found.remove((0, 0, 0, 0, 0))
    return sorted(found, key=lambda s: -hops(s))


def main_kernel(
    basis_in, columns_in, angles_in, inv_in, hsub_in, tx_in, ty_in, ty_t_in, potential_in, tb_in,
    hblock_out, rotated_out, bands_out,
    basis, columns, angles, inv, hsub, tx, ty, ty_t, potential, tb,
    state, turned, table, factor, factor_wide, y_own, z_buf, sendz, recvz, sendr, recvr, w_buf, bands_part,
    send1, recv1, send2, recv2, send3, recv3, new_own, news, hall, recvb, sendf, recvf,
    q_buf, u_buf, a_cos, a_sin, phase, phase_out, folded, right1, right2, radius, coef, d_buf, p_buf, g_buf,
    s1, r1, s2, r2, s3, r3, sh, rh, sb, rb, sf, rf, sz, rz, sr, rr, loads,
):
    band = lax.axis_index("band")
    me = lax.axis_index("fft")

    inputs = (
        (basis_in, basis), (tb_in, tb), (angles_in, angles), (columns_in, columns), (tx_in, tx),
        (ty_in, ty), (ty_t_in, ty_t), (inv_in, inv), (potential_in, potential), (hsub_in, hsub),
    )
    copies = [pltpu.make_async_copy(a, b, loads.at[i]) for i, (a, b) in enumerate(inputs)]
    copies[0].start()
    copies[1].start()

    def peer(steps):
        z_hi, core, z_lo, x, y = steps
        to_fft = (((me >> 4) ^ z_lo) << 4) | ((((me >> 2) + x) & 3) << 2) | ((me + y) & 3)
        return (band ^ (2 * z_hi + core), to_fft)

    near, every = all_steps(1), all_steps(2)

    barrier = pltpu.get_barrier_semaphore()

    for steps in near:
        pl.semaphore_signal(barrier, inc=1, device_id=peer(steps), device_id_type=MESH)
    for i in range(1, NBAND):
        pl.semaphore_signal(
            barrier, inc=1, device_id=(lax.rem(band + i, NBAND), me), device_id_type=MESH
        )

    for copy in copies[2:]:
        copy.start()

    def fft_start(send, recv, ssem, rsem, whole):
        for steps in near:
            to = peer(steps)
            pltpu.make_async_remote_copy(
                src_ref=send.at[to[1], pl.ds(0, 3)],
                dst_ref=recv.at[me, pl.ds(0, 3)],
                send_sem=ssem,
                recv_sem=rsem,
                device_id=to,
                device_id_type=MESH,
            ).start()

    def fft_all(send, recv, ssem, rsem, whole):
        part = recv.at[pl.ds(0, NFFT - 1), pl.ds(0, 3)]
        return pltpu.make_async_remote_copy(
            src_ref=part,
            dst_ref=part,
            send_sem=ssem,
            recv_sem=rsem,
            device_id=(band, lax.rem(me + 1, NFFT)),
            device_id_type=MESH,
        )

    def fft_wait_recv(*args):
        fft_all(*args).wait_recv()

    def fft_wait_send(*args):
        fft_all(*args).wait_send()

    def band_copy(i, src, dst, ssem, rsem):
        to = lax.rem(band + i, NBAND)
        return pltpu.make_async_remote_copy(
            src_ref=src(to),
            dst_ref=dst.at[band],
            send_sem=ssem.at[i],
            recv_sem=rsem.at[band],
            device_id=(to, me),
            device_id_type=MESH,
        )

    def band_arrival(i, src, dst, ssem, rsem):
        source = lax.rem(band + NBAND - i, NBAND)
        return pltpu.make_async_remote_copy(
            src_ref=src(source),
            dst_ref=dst.at[source],
            send_sem=ssem.at[i],
            recv_sem=rsem.at[source],
            device_id=(source, me),
            device_id_type=MESH,
        )

    copies[0].wait()
    copies[1].wait()
    new = basis[2016:2048, :]
    none = jnp.zeros((16, 128), BF16)
    right = jnp.concatenate(
        [
            jnp.concatenate([new[0:16], none], 1),
            jnp.concatenate([none, new[0:16]], 1),
            jnp.concatenate([new[16:32], none], 1),
            jnp.concatenate([none, new[16:32]], 1),
        ],
        0,
    )
    blank = jnp.zeros((64, 256), BF16)
    right = jnp.concatenate(
        [jnp.concatenate([right, blank], 1), jnp.concatenate([blank, right], 1)], 0
    )
    pencils = dot_nt(tb[...], right)
    for r in range(3):
        send1[:, r, :] = pencils[NFFT * r : NFFT * r + NFFT]
    first = (send1, recv1, s1, r1, False)
    pl.semaphore_wait(barrier, NFFT - 1 + NBAND - 1)
    fft_start(*first)
    recv1[pl.ds(me, 1)] = send1[pl.ds(me, 1)]

    copies[2].wait()
    turn_angles(angles, turned)
    angle_tables(turned, table, 0, SPLIT)

    new_args = (lambda to: new_own, news, sh, rh)
    new_own[...] = basis[2016:2048, :]
    for i in range(1, NBAND):
        band_copy(i, *new_args).start()
    news[pl.ds(band, 1)] = new_own[...].reshape(1, 32, 128)

    for i in range(3, 7):
        copies[i].wait()
    position = columns[...].astype(F32)
    pos_x = jnp.floor((position + 0.5) * (1.0 / NG))
    pos_y = position - NG * pos_x
    k_row = lax.broadcasted_iota(jnp.int32, (256, NCOL), 0).astype(F32)
    hot_x = (k_row == pos_x).astype(F32).astype(BF16)
    hot_y = (k_row == pos_y).astype(F32).astype(BF16)
    a_both = dot(tx[...], jnp.concatenate([hot_x, hot_x], 0))
    a_cos[...] = a_both[:HALF]
    a_sin[...] = a_both[HALF:]
    right2[...] = dot(ty_t[...], hot_y).astype(BF16)
    wide_y = jnp.broadcast_to(pos_y, (128, NCOL)).T
    lane_k = lax.broadcasted_iota(jnp.int32, (NCOL, 128), 1).astype(F32)
    hot_yt = jnp.concatenate(
        [(wide_y == lane_k).astype(F32), (wide_y == lane_k + 128.0).astype(F32)], 1
    ).astype(BF16)
    right1[...] = dot(hot_yt, ty[...]).astype(BF16)
    turns = (pos_x + pos_y) * (NG - 1.0)
    turns = turns - (2.0 * NG) * jnp.floor((turns + 0.5) * (0.5 / NG))
    center = jnp.broadcast_to(turns * (math.pi / NG), (8, NCOL))
    phase[0] = jnp.cos(center)
    phase[1] = jnp.sin(center)
    for j in range(4):
        phase_out[:, 4 * j : 4 * j + 4, :] = phase[:, 0:4, 128 * j : 128 * j + 128]
    freq_x = jnp.where(pos_x < NG // 2, pos_x, pos_x - NG)
    freq_y = jnp.where(pos_y < NG // 2, pos_y, pos_y - NG)
    radius[...] = jnp.broadcast_to(freq_x * freq_x + freq_y * freq_y, (128, NCOL)).T
    g_buf[...] = jnp.zeros_like(g_buf)

    for i in range(7, 10):
        copies[i].wait()
    fold_potential(potential, folded)
    fft_wait_recv(*first)

    lanes = lax.broadcasted_iota(jnp.int32, (8, 128), 1)
    wide_lanes = lax.broadcasted_iota(jnp.int32, (16, 128), 1)
    lines = [jnp.concatenate([recv1[8 * j + t] for j in range(4)], 0) for t in range(8)]
    for q in range(8):
        total = jnp.zeros((16, 128), F32)
        for t in range(8):
            piece = lines[t]
            move = (16 * t - 16 * q) % 128
            if move:
                piece = pltpu.roll(piece, move, 1)
            total = jnp.where((wide_lanes >> 4) == t, piece, total)
        coef[q] = total

    def mix(v):
        for q in (2 * v, 2 * v + 4):
            old_re, old_im = coef[q], coef[q + 1]
            coef[q] = old_re * phase_out[0] - old_im * phase_out[1]
            coef[q + 1] = old_re * phase_out[1] + old_im * phase_out[0]

    def unmix(v):
        for q in (2 * v, 2 * v + 4):
            new_re, new_im = g_buf[q], g_buf[q + 1]
            g_buf[q] = new_re * phase_out[0] + new_im * phase_out[1]
            g_buf[q + 1] = new_im * phase_out[0] - new_re * phase_out[1]

    def block(z, a, i):
        return pl.ds(HALF * (4 * z + 2 * a + i), HALF)

    def plane(z):
        return pl.ds(4 * HALF * z, 4 * HALF)

    def spread(v, z):
        for i in range(2):
            q = 4 * (z % 2) + 2 * v + i
            row = jnp.concatenate(
                [coef[q, 4 * j + z // 2 : 4 * j + z // 2 + 1, :] for j in range(4)], 1
            )
            for a, part in enumerate((a_cos, a_sin)):
                d_buf[block(z, a, i), :] = (part[...] * row).astype(BF16)

    def to_field(v, z):
        q_buf[plane(z), :] = dot(d_buf[plane(z), :], right1[...])

    def multiply(v, z):
        q = [
            [tuple(q_buf[block(z, a, i), 128 * b : 128 * b + 128] for i in range(2)) for b in range(2)]
            for a in range(2)
        ]
        back = times_potential(q, [[folded[z, u, w] for w in range(2)] for u in range(2)])
        for a in range(2):
            for b in range(2):
                for i in range(2):
                    p_buf[block(z, a, i), 128 * b : 128 * b + 128] = back[a][b][i].astype(BF16)

    def from_field(v, z):
        u_buf[plane(z), :] = dot(p_buf[plane(z), :], right2[...])

    def collect(v, z):
        for i in range(2):
            total = jnp.sum(
                a_cos[...] * u_buf[block(z, 0, i), :] + a_sin[...] * u_buf[block(z, 1, i), :],
                axis=0,
                keepdims=True,
            )
            for j in range(4):
                g_buf[4 * (z % 2) + 2 * v + i, 4 * j + z // 2 : 4 * j + z // 2 + 1, :] = total[
                    :, 128 * j : 128 * j + 128
                ]

    steps = (spread, to_field, multiply, from_field, collect)

    for v in range(2):
        mix(v)
    for t in range(2 * SLAB + len(steps) - 1):
        for s, step in enumerate(steps):
            if 0 <= t - s < 2 * SLAB:
                step((t - s) // SLAB, (t - s) % SLAB)
    for v in range(2):
        unmix(v)

    volume = 1.0 / float(NG) ** 3
    for t in range(8):
        total = jnp.zeros((16, 128), F32)
        for q in range(8):
            piece = g_buf[q]
            move = (16 * q - 16 * t) % 128
            if move:
                piece = pltpu.roll(piece, move, 1)
            total = jnp.where((wide_lanes >> 4) == q, piece, total)
        total = total * volume
        for j in range(4):
            send2[8 * j + t] = total[4 * j : 4 * j + 4]
    own = band * NFFT + me

    for steps in every:
        to = peer(steps)
        pltpu.make_async_remote_copy(
            src_ref=send2.at[to[1], pl.ds(0, 3)],
            dst_ref=recv2.at[own, pl.ds(0, 3)],
            send_sem=s2,
            recv_sem=r2,
            device_id=to,
            device_id_type=MESH,
        ).start()
    back_part = recv2.at[pl.ds(0, NBAND * NFFT - 1), pl.ds(0, 3)]
    back_all = pltpu.make_async_remote_copy(
        src_ref=back_part,
        dst_ref=back_part,
        send_sem=s2,
        recv_sem=r2,
        device_id=(band, lax.rem(me + 1, NFFT)),
        device_id_type=MESH,
    )
    recv2[pl.ds(own, 1)] = send2[pl.ds(me, 1)]
    angle_tables(turned, table, SPLIT, ROUNDS)
    rotate_factor(band, state, table, inv, factor)
    couple(me, hsub, factor, factor_wide, y_own, z_buf, sendz, sendr)
    z_args = (lambda to: sendz.at[to], recvz, sz, rz)
    row_args = (lambda to: sendr, recvr, sr, rr)
    for i in range(1, NBAND):
        band_copy(i, *z_args).start()
    for i in range(1, NBAND):
        band_copy(i, *row_args).start()
    recvz[pl.ds(band, 1)] = sendz[pl.ds(band, 1)]
    recvr[pl.ds(band, 1)] = sendr[...].reshape(1, 8, ORDER)

    vector_weights(basis, y_own, w_buf, bands_part)
    bands_args = (lambda to: bands_part.at[to], recvb, sb, rb)
    for i in range(1, NBAND):
        band_copy(i, *bands_args).start()
    recvb[pl.ds(band, 1)] = bands_part[pl.ds(band, 1)]
    for i in range(1, NBAND):
        band_arrival(i, *new_args).wait_recv()
    slot = lax.broadcasted_iota(jnp.int32, (16, 128), 1) & (NZC - 1)
    freq_z = jnp.where(slot < NZC // 2, slot, slot - NZC).astype(F32)
    own_radius = radius[pl.ds(pl.multiple_of(me * 16, 16), 16), :]
    kinetic = (own_radius + freq_z * freq_z) / (2.0 * (NG // 4) ** 2)

    back_all.wait_recv()
    slabs = []
    for b in range(NBAND):
        parts = [recv2[NFFT * b : NFFT * b + NFFT, r, :] for r in range(3)]
        parts.append(jnp.zeros((NFFT, 128), F32))
        slabs.append(jnp.concatenate(parts, 0).T.astype(BF16))
    local = dot(jnp.concatenate(slabs, 0), tb[...])
    for b in range(NBAND):
        for v in range(2):
            term = jnp.zeros((16, 128), F32)
            for n in range(2):
                row, lane = 128 * b + 64 * n + 32 * v, 256 * n
                term = term + local[row : row + 16, lane : lane + 128]
                term = term + local[row + 16 : row + 32, lane + 128 : lane + 256]
            coeffs = news[b, 16 * v : 16 * v + 16, :].astype(F32)
            hall[b, 16 * v : 16 * v + 16, :] = (kinetic * coeffs + term).astype(BF16)

    pairs = dot_nt(basis[...], hall[...].reshape(128, 128))
    pair_row = lax.broadcasted_iota(jnp.int32, (2048, 128), 0)
    pair_lane = lax.broadcasted_iota(jnp.int32, (2048, 128), 1)
    pairs = jnp.where(((pair_row ^ pair_lane) & 15) == 0, pairs, 0.0)
    by_group = jnp.sum(pairs.reshape(GROUP, 16, 128), axis=1)
    pick_row = lax.broadcasted_iota(jnp.int32, (128, 512), 0)
    pick_lane = lax.broadcasted_iota(jnp.int32, (128, 512), 1)
    slot_of = pick_lane & 127
    picked = ((slot_of >> 3) == (pick_lane >> 7)) & ((slot_of & 7) == (pick_row >> 4))
    pick = picked.astype(F32).astype(BF16)
    high, low_part = split(by_group)
    fresh = dot(high, pick) + dot(low_part, pick)
    fresh = jnp.concatenate([fresh[:, 128 * j : 128 * j + 128] for j in range(4)], 0).astype(BF16)
    send3[...] = dot(factor_wide[...], fresh).reshape(NBAND * NFFT, 1, 128)
    for steps in every:
        to = peer(steps)
        pltpu.make_async_remote_copy(
            src_ref=send3.at[to[0] * NFFT + to[1]],
            dst_ref=recv3.at[own],
            send_sem=s3,
            recv_sem=r3,
            device_id=to,
            device_id_type=MESH,
        ).start()
    sum_part = recv3.at[pl.ds(0, NBAND * NFFT - 1)]
    sum_all = pltpu.make_async_remote_copy(
        src_ref=sum_part,
        dst_ref=sum_part,
        send_sem=s3,
        recv_sem=r3,
        device_id=(band, lax.rem(me + 1, NFFT)),
        device_id_type=MESH,
    )
    recv3[pl.ds(own, 1)] = send3[pl.ds(own, 1)]
    for i in range(1, NBAND):
        band_arrival(i, *z_args).wait_recv()
    z_sum = recvz[0] + recvz[1] + recvz[2] + recvz[3]
    old = dot_nt(z_sum.astype(BF16), factor[...].astype(BF16))
    sendf[...] = old.reshape(NBAND, 8, ORDER)
    final_args = (lambda to: sendf.at[to], recvf, sf, rf)
    for i in range(1, NBAND):
        band_copy(i, *final_args).start()
    recvf[pl.ds(band, 1)] = sendf[pl.ds(band, 1)]

    hblock_out[...] = hall[pl.ds(band, 1)].reshape(32, 128)
    for i in range(1, NBAND):
        band_arrival(i, *bands_args).wait_recv()
    bands_total = recvb[0].astype(F32)
    for b in range(1, NBAND):
        bands_total = bands_total + recvb[b].astype(F32)
    bands_out[...] = bands_total.astype(BF16)
    for i in range(1, NBAND):
        band_arrival(i, *final_args).wait_recv()
    old_part = recvf[0] + recvf[1] + recvf[2] + recvf[3]
    for i in range(1, NBAND):
        band_arrival(i, *row_args).wait_recv()
    new_rows = jnp.concatenate([recvr[b, 6:8, :] for b in range(NBAND)], 0)
    wide_rows = jnp.concatenate([new_rows] * 4 + [jnp.zeros((96, ORDER), F32)], 0).astype(BF16)
    fft_wait_send(*first)
    back_all.wait_send()
    for i in range(1, NBAND):
        band_copy(i, *bands_args).wait_send()
        band_copy(i, *new_args).wait_send()
        band_copy(i, *final_args).wait_send()
        band_copy(i, *z_args).wait_send()
        band_copy(i, *row_args).wait_send()

    sum_all.wait_recv()
    total = jnp.sum(recv3[...].reshape(NBAND * NFFT, 128), axis=0, keepdims=True)
    total = total * (1.0 / math.sqrt(2 * NCOL * NZC))
    spread_rows = lax.broadcasted_iota(jnp.int32, (8, 128), 0)
    total = jnp.where((lanes >> 3) == spread_rows, total, 0.0)
    new_part = dot(total.astype(BF16), wide_rows)
    rotated_out[...] = (old_part + new_part)[0:4]
    sum_all.wait_send()


def main_part(*operands):
    vmem = pl.BlockSpec(memory_space=pltpu.VMEM)
    dma = pltpu.SemaphoreType.DMA
    return pl.pallas_call(
        main_kernel,
        out_shape=(
            jax.ShapeDtypeStruct((32, 128), BF16),
            jax.ShapeDtypeStruct((4, ORDER), F32),
            jax.ShapeDtypeStruct((32, 128), BF16),
        ),
        in_specs=[pl.BlockSpec(memory_space=pl.ANY)] * len(operands),
        out_specs=(vmem,) * 3,
        scratch_shapes=[pltpu.VMEM(x.shape, x.dtype) for x in operands]
        + [
            pltpu.VMEM((2, 16, TILE, 128), F32),
            pltpu.VMEM((2, TILE, 256), F32),
            pltpu.VMEM((2, 8 * ROUNDS, TILE, 128), F32),
            pltpu.VMEM((ORDER, 128), F32),
            pltpu.VMEM((128, ORDER), BF16),
            pltpu.VMEM((40, GROUP), F32),
            pltpu.VMEM((ORDER, 128), F32),
            pltpu.VMEM((NBAND, 32, GROUP), F32),
            pltpu.VMEM((NBAND, 32, GROUP), F32),
            pltpu.VMEM((8, ORDER), F32),
            pltpu.VMEM((NBAND, 8, ORDER), F32),
            pltpu.VMEM((128, 2048), BF16),
            pltpu.VMEM((NBAND, 32, 128), BF16),
            pltpu.VMEM((NFFT, 4, 128), F32),
            pltpu.VMEM((NFFT, 4, 128), F32),
            pltpu.VMEM((NFFT, 4, 128), F32),
            pltpu.VMEM((NBAND * NFFT, 4, 128), F32),
            pltpu.VMEM((NBAND * NFFT, 1, 128), F32),
            pltpu.VMEM((NBAND * NFFT, 1, 128), F32),
            pltpu.VMEM((32, 128), BF16),
            pltpu.VMEM((NBAND, 32, 128), BF16),
            pltpu.VMEM((NBAND, 32, 128), BF16),
            pltpu.VMEM((NBAND, 32, 128), BF16),
            pltpu.VMEM((NBAND, 8, ORDER), F32),
            pltpu.VMEM((NBAND, 8, ORDER), F32),
            pltpu.VMEM((4 * SLAB * HALF, 256), F32),
            pltpu.VMEM((4 * SLAB * HALF, NCOL), F32),
            pltpu.VMEM((HALF, NCOL), F32),
            pltpu.VMEM((HALF, NCOL), F32),
            pltpu.VMEM((2, 8, NCOL), F32),
            pltpu.VMEM((2, 16, 128), F32),
            pltpu.VMEM((SLAB, 2, 2, HALF, 128), F32),
            pltpu.VMEM((NCOL, 256), BF16),
            pltpu.VMEM((256, NCOL), BF16),
            pltpu.VMEM((NCOL, 128), F32),
            pltpu.VMEM((8, 16, 128), F32),
            pltpu.VMEM((4 * SLAB * HALF, NCOL), BF16),
            pltpu.VMEM((4 * SLAB * HALF, 256), BF16),
            pltpu.VMEM((8, 16, 128), F32),
        ]
        + [dma] * 6
        + [dma((NBAND,))] * 10
        + [dma((len(operands),))],
        compiler_params=pltpu.CompilerParams(
            collective_id=0, has_side_effects=True, vmem_limit_bytes=56 * 2**20
        ),
        name="main_part",
    )(*operands)


def result_kernel(*refs):
    sources, targets, sems = refs[:3], refs[3:6], refs[6]
    copies = [
        pltpu.make_async_copy(a, b, sems.at[i]) for i, (a, b) in enumerate(zip(sources, targets))
    ]
    for copy in copies:
        copy.start()
    for copy in copies:
        copy.wait()


def result_part(*operands):
    anywhere = pl.BlockSpec(memory_space=pl.ANY)
    return pl.pallas_call(
        result_kernel,
        out_shape=tuple(jax.ShapeDtypeStruct(x.shape, x.dtype) for x in operands),
        in_specs=[anywhere] * 3,
        out_specs=(anywhere,) * 3,
        scratch_shapes=[pltpu.SemaphoreType.DMA((3,))],
        compiler_params=pltpu.CompilerParams(vmem_limit_bytes=56 * 2**20),
        name="result_part",
    )(*operands)


def per_device(basis, potential, colmap, hsub_old, inv_factor, angles):
    table = y_table()
    results = main_part(
        basis.reshape(2048, 128),
        colmap.reshape(1, NCOL),
        angles.reshape(8 * ROUNDS, TILE),
        inv_factor,
        hsub_old.T,
        jnp.asarray(x_table()),
        jnp.asarray(table.astype(BF16)),
        jnp.asarray(table.T.astype(BF16)),
        potential,
        jnp.asarray(z_table_back().astype(BF16)),
    )
    hblock, rotated, bands = result_part(*results)
    return (hblock.reshape(2, 16, 128), rotated, bands.reshape(2, 16, 128))


def solution(mesh):
    in_specs = (P("band", "fft", None), P("fft", None, None), P(), P("band", None), P(), P())
    out_specs = (P("band", "fft", None), P(("band", "fft"), None), P("band", "fft", None))
    return jax.shard_map(
        per_device, mesh=mesh, in_specs=in_specs, out_specs=out_specs, check_vma=False
    )
```
